512 devices in a mesh: series: 8 (over x, core), tm: 64 (over z, y).
Axes of the slice: x: 4, y: 8, z: 8, core: 2. Of those that a mesh axis runs over, the one named last changes fastest.
Arguments:
- panel: float32 [1024, 32768], P('series', 'tm'), may hold values from -6 to 6
- observed: int32 [1024, 256], P('series', 'tm'), may hold values 0 or 1
- start_time: float32 [64, 32768], P(None, 'tm'), may hold values from -0.125 to 0.125
- ar_weight: float32 [64, 14], replicated, may hold values from -0.3 to 0.3
- lags: int32 [14], replicated, may hold values from 1 to 2016, as said below
Outputs:
- series_factors: float32 [1024, 64], P('series')
- time_factors: float32 [64, 32768], P(None, 'tm')
The draws below stay inside these ranges and needn't reach their ends.
Inputs may be any that keep to these rules, and one draw needn't show every extreme that they name: `lags`: entries 0 to 11 are distinct values of 1 to 24; entry 12 lies in 256 to 511; entry 13 equals 2016.
All inputs are finite; a program needn't handle non-finite values. No bound on the sum of `observed` on one device may be relied on, other than what follows from the above.
Results may differ from the reference program's by a relative error of at most 0.0003.
Values sent between devices are 32-bit elements; how exact they have to be, the bound alone decides.
No kernel may reach another device: no remote copies, remote signals or barrier semaphores. Data moves between devices by JAX's collectives and lax.ppermute only.
A program may use at most 64 MiB of HBM per device.

```python
import jax
import jax.numpy as jnp
from jax import lax

K = 64
TILE = 128
LAGS = 14
TS = 512
CELLS = 1024
STEPS = 32768
TILES = 256
LAGMAX = 2016


def draw_lags(key, part):
    key = jax.random.fold_in(key, 7)
    first, second = jax.random.split(key)
    short_lags = jax.random.permutation(first, 24)[:12] + 1
    middle = jax.random.randint(second, (1,), TS // 2, TS)
    return jnp.concatenate([short_lags.astype(jnp.int32), middle.astype(jnp.int32), jnp.array([LAGMAX], jnp.int32)])


def set_ends(entries, key, smallest, high):
    spot = [jax.random.randint(jax.random.fold_in(key, axis), (), 0, length) for axis, length in enumerate(entries.shape)]
    main_axis = entries.shape.index(max(entries.shape))
    neighbour = spot[:main_axis] + [(spot[main_axis] + 1) % entries.shape[main_axis]] + spot[main_axis + 1:]
    return entries.at[tuple(spot)].set(smallest).at[tuple(neighbour)].set(high)


def levels(rng, extent, pieces, smallest, largest):
    def one(dim, blocks):
        steps = jax.random.uniform(jax.random.fold_in(jax.random.fold_in(rng, 6), dim), (blocks,), jnp.float32, smallest / len(pieces), largest / len(pieces))
        return jnp.repeat(jnp.exp(steps), extent[dim] // blocks).reshape((-1,) + (1,) * (len(extent) - dim - 1))

    factor_of = one(*pieces[0])
    for cut in pieces[1:]:
        factor_of = factor_of * one(*cut)
    return factor_of


def scatter_about(own_key, shape, scale, reach, cuts=(), kind=jnp.bfloat16):
    factor_of = levels(own_key, shape, cuts, -0.22, 0.18) if cuts else 1.0
    entries = jax.random.normal(own_key, shape, jnp.float32) * scale * factor_of
    return jnp.minimum(jnp.maximum(entries, -reach), reach).astype(kind)


def setup_inputs(seed: int = 0) -> dict:
    arg_keys = jax.random.split(jax.random.key(seed), 6)
    return {
        "panel": scatter_about(arg_keys[0], (CELLS, STEPS), 1.0, 6.0, ((0, 8), (1, 64)), jnp.float32),
        "observed": set_ends((jax.random.randint(arg_keys[1], (CELLS, TILES), 0, 4) < 3).astype(jnp.int32), jax.random.fold_in(arg_keys[1], 1), 0, 1),
        "start_time": scatter_about(arg_keys[2], (K, STEPS), (STEPS // 16) ** -0.5, 0.125, ((1, 64),), jnp.float32),
        "ar_weight": jnp.clip(jax.random.uniform(arg_keys[3], (K, LAGS), jnp.float32, -0.3, 0.3), -0.3, 0.3),
        "lags": draw_lags(jax.random.fold_in(arg_keys[5], 71), 0),
    }


HIGH = lax.Precision.HIGHEST
ridge_factor = 1.0
ridge_time = 0.05
ar_strength = 0.25

def solve_cells(gram_flat, rhs):
    count = rhs.shape[0]
    rank = rhs.shape[1]
    mats = gram_flat.reshape(count, rank, rank) + ridge_factor * jnp.eye(rank, dtype=jnp.float32)
    chol = jnp.linalg.cholesky(mats)

    def single(lower, vector):
        return jax.scipy.linalg.cho_solve((lower, True), vector)
    return jax.vmap(single)(chol, rhs)

def reference(panel, observed, start_time, ar_weight, lags):
    flags = observed.astype(jnp.float32)
    masked = panel * jnp.repeat(flags, TILE, axis=1)
    tiles_x = start_time.reshape(K, TILES, TILE)
    grams = jnp.einsum('kbt,jbt->bkj', tiles_x, tiles_x, precision=HIGH).reshape(TILES, K * K)
    cell_gram = jnp.dot(flags, grams, precision=HIGH)
    cell_rhs = jnp.dot(masked, start_time.T, precision=HIGH)
    factors = solve_cells(cell_gram, cell_rhs)
    outer = (factors[:, :, None] * factors[:, None, :]).reshape(CELLS, K * K)
    tile_h = (jnp.dot(flags.T, outer, precision=HIGH) / CELLS).reshape(TILES, K, K)
    rhs_time = jnp.dot(factors.T, masked, precision=HIGH) / CELLS
    valid = (jnp.arange(STEPS) >= LAGMAX).astype(jnp.float32)[None, :]

    def apply(field):
        data = jnp.einsum('bkj,jbt->kbt', tile_h, field.reshape(K, TILES, TILE), precision=HIGH).reshape(K, STEPS)
        padded = jnp.pad(field, ((0, 0), (LAGMAX, 0)))
        lagged = jnp.zeros((K, STEPS), jnp.float32)
        for index in range(LAGS):
            start = (LAGMAX - lags[index]).astype(jnp.int32)
            lagged = lagged + ar_weight[:, index:index + 1] * lax.dynamic_slice_in_dim(padded, start, STEPS, 1)
        errors = valid * (field - lagged)
        ahead = jnp.pad(errors, ((0, 0), (0, LAGMAX)))
        back = errors
        for index in range(LAGS):
            start = lags[index].astype(jnp.int32)
            back = back - ar_weight[:, index:index + 1] * lax.dynamic_slice_in_dim(ahead, start, STEPS, 1)
        return data + ridge_time * field + ar_strength * back
    solution = start_time
    residual = rhs_time - apply(solution)
    direction = residual
    norm_now = jnp.sum(residual * residual)
    for step in range(3):
        image = apply(direction)
        alpha = norm_now / jnp.sum(direction * image)
        solution = solution + alpha * direction
        residual = residual - alpha * image
        norm_next = jnp.sum(residual * residual)
        direction = residual + norm_next / norm_now * direction
        norm_now = norm_next
    return (factors, solution)
```

```python
import functools

import jax
import jax.numpy as jnp
from jax import lax
from jax.experimental import pallas as pl
from jax.experimental.pallas import tpu as pltpu
from jax.sharding import Mesh, PartitionSpec as P

HIGH = lax.Precision.HIGHEST
TILE = 128
LAGS = 14
LONGEST = 2016
RIDGE_FACTOR = 1.0
RIDGE_TIME = 0.05
AR = 0.25
TM = ("tz", "ty")
F32 = jnp.float32
VMEM = pl.BlockSpec(memory_space=pltpu.VMEM)
SMEM = pl.BlockSpec(memory_space=pltpu.SMEM)


def struct(*shape):
    return jax.ShapeDtypeStruct(shape, F32)


def iota(shape, dim):
    return lax.broadcasted_iota(jnp.int32, shape, dim)


def call(kernel, outs, ins, scratch=()):
    specs = [SMEM if a.dtype == jnp.int32 and a.ndim == 1 else VMEM for a in ins]
    return pl.pallas_call(
        kernel,
        out_shape=outs,
        in_specs=specs,
        out_specs=jax.tree.map(lambda _: VMEM, outs),
        scratch_shapes=list(scratch),
        compiler_params=pltpu.CompilerParams(vmem_limit_bytes=32 * 1024 * 1024),
    )(*ins)


def dot(a, b, dims):
    return lax.dot_general(a, b, (dims, ((), ())), precision=HIGH, preferred_element_type=F32)


def front_kernel(panel_ref, obs_ref, x_ref, out_ref):
    flags = obs_ref[...].astype(F32)
    x = x_ref[...]
    row = iota((32, 128), 0)
    col = iota((32, 128), 1) % 64
    keep = (col < 32) | (col - 32 >= row)
    diag_at = iota((64, 128), 0) == iota((64, 128), 1) % 64
    left = iota((64, 128), 1) < 64
    packs, diags, lanes = [], [], []
    masked = []
    for b in range(4):
        xb = x[:, b * TILE : (b + 1) * TILE]
        gram = dot(xb, xb, ((1,), (1,)))
        twice = jnp.concatenate([gram, gram], axis=1)
        packs.append(jnp.where(keep, twice[32:64], pltpu.roll(twice[0:32], 32, axis=1)))
        diags.append(jnp.sum(jnp.where(diag_at, twice, 0.0), axis=0, keepdims=True))
        flag = flags[:, b : b + 1]
        lanes.append(jnp.where(left, flag[0:64], flag[64:128]))
        masked.append(panel_ref[:, b * TILE : (b + 1) * TILE] * flag)
    rhs = dot(jnp.concatenate(masked, axis=1), x, ((1,), (1,)))
    rhs = jnp.concatenate([rhs[0:64], rhs[64:128]], axis=1)
    diag = lanes[0] * diags[0] + lanes[1] * diags[1] + lanes[2] * diags[2] + lanes[3] * diags[3]
    sub = iota((8, 128), 0)
    for j in range(64):
        total = packs[0] * lanes[0][j : j + 1]
        for b in range(1, 4):
            total = total + packs[b] * lanes[b][j : j + 1]
        out_ref[j, 0:32, :] = total
        tail = jnp.where(sub == 0, diag[j : j + 1], jnp.where(sub == 1, rhs[j : j + 1], 0.0))
        out_ref[j, 32:40, :] = tail


def solve_kernel(parts_ref, out_ref):
    total = parts_ref[0]
    for j in range(1, 64):
        total = total + parts_ref[j]
    pack = total[0:32]
    diag = total[32:33]
    rhs = total[33:34]
    flipped = jnp.concatenate([pack, pack, pack, pack], axis=0).T
    row = iota((32, 128), 0)
    lane = iota((32, 128), 1)
    group = lane // 32
    col = lane % 32
    first = lane < 64
    upper_t = jnp.where(first, flipped[32:64], flipped[96:128])
    cross = jnp.where(first, flipped[0:32], flipped[64:96])
    odd = group % 2 == 1
    top_left = jnp.where(col < row, pltpu.roll(pack, 96, axis=1), jnp.where(col == row, diag, upper_t))
    top = jnp.where(odd, cross, top_left)
    bottom = jnp.where(odd & (col < row), upper_t, pack)
    eye = (iota((64, 128), 0) == iota((64, 128), 1) % 64).astype(F32)
    mat = jnp.concatenate([top, bottom], axis=0) + RIDGE_FACTOR * eye
    blocks = [mat[8 * i : 8 * i + 8] for i in range(8)]
    side = jnp.broadcast_to(rhs, (8, 128))
    half = iota((8, 128), 1) < 64
    within = iota((8, 128), 1) % 64

    def spread(value, k):
        return jnp.where(half, value[:, k : k + 1], value[:, 64 + k : 65 + k])

    for k in range(64):
        i, r = divmod(k, 8)
        pivot_row = jnp.broadcast_to(blocks[i][r : r + 1], (8, 128))
        inverse = 1.0 / spread(pivot_row, k)
        factor = jnp.where(within == k, 1.0 - inverse, pivot_row * inverse)
        side = side - spread(side, k) * factor
        for m in range(i if r < 7 else i + 1, 8):
            blocks[m] = blocks[m] - spread(blocks[m], k) * factor
    out_ref[...] = jnp.broadcast_to(side[0:1][None], out_ref.shape)


def normal_kernel(scale, gathered_ref, panel_ref, obs_ref, factors_ref, out_ref):
    gathered = gathered_ref[...]
    factors = jnp.concatenate([gathered[:, 0:64], gathered[:, 64:128]], axis=0)
    factors_ref[...] = factors
    flags = obs_ref[...].astype(F32)
    for b in range(4):
        flag = flags[:, b : b + 1]
        out_ref[:, b * TILE : (b + 1) * TILE] = scale * dot(
            factors, panel_ref[:, b * TILE : (b + 1) * TILE] * flag, ((0,), (0,))
        )
    for pair in range(2):
        halves = [dot(factors * flags[:, b : b + 1], factors, ((0,), (0,))) for b in (2 * pair, 2 * pair + 1)]
        out_ref[:, 512 + 128 * pair : 640 + 128 * pair] = scale * jnp.concatenate(halves, axis=1)


def lagged(read, count, lags_ref, weight_ref, ahead):
    lane = iota((8, 128), 1)
    sums = [None] * count
    for index in range(LAGS):
        lag = lags_ref[index]
        if ahead:
            start = lag // 128
            shift = lag % 128
        else:
            back = (lag + 127) // 128
            start = -back
            shift = back * 128 - lag
        cut = 128 - shift
        weight = weight_ref[index]
        own = lane < cut
        turn = jnp.where(cut == 128, 0, cut)
        low = pltpu.roll(read(start), turn, axis=1)
        for j in range(count):
            high = pltpu.roll(read(start + j + 1), turn, axis=1)
            term = weight * jnp.where(own, low, high)
            sums[j] = term if sums[j] is None else sums[j] + term
            low = high
    return sums


def residuals(read, count, first_step, steps_all, meta_ref, weight_ref):
    past = lagged(read, count, meta_ref, weight_ref, False)
    lane = iota((8, 128), 1)
    out = []
    for j in range(count):
        step = first_step + 128 * j + lane
        out.append(jnp.where((step >= LONGEST) & (step < steps_all), read(j) - past[j], 0.0))
    return out


def ar_part(read, first_step, steps_all, meta_ref, weight_ref, errors_ref):
    errors = residuals(read, 20, first_step, steps_all, meta_ref, weight_ref)
    for j in range(20):
        errors_ref[j] = errors[j]
    later = lagged(lambda j: errors_ref[j], 4, meta_ref, weight_ref, True)
    return [errors[j] - later[j] for j in range(4)]


def start_kernel(steps_all, sums_ref, x_ref, near_ref, weight_ref, meta_ref, out_ref, h_ref, context_ref, errors_ref):
    slab, y = meta_ref[LAGS], meta_ref[LAGS + 1]
    fill_context(near_ref, context_ref)
    base = 16 + 4 * y
    total = sums_ref[0]
    for j in range(1, 8):
        total = total + sums_ref[j]

    def read(j):
        return context_ref[base + j]

    back = ar_part(read, slab * 512, steps_all, meta_ref, weight_ref, errors_ref)
    for q in range(4):
        h = total[:, 512 + 64 * q : 576 + 64 * q]
        h_ref[q] = h
        image = dot(h, x_ref[:, q * 128 : (q + 1) * 128], ((1,), (0,))) + RIDGE_TIME * read(q) + AR * back[q]
        value = total[:, q * 128 : (q + 1) * 128] - image
        for j in range(8):
            out_ref[j, q] = value


def fill_context(near_refs, context_ref):
    middle, before, after = near_refs
    for j in range(16):
        context_ref[j] = before[j]
        if after is not None:
            context_ref[48 + j] = after[j]
    for j in range(32):
        context_ref[16 + j] = middle[j]


def data_part(h_ref, wide_ref, q):
    return dot(h_ref[q], wide_ref[:, q].reshape(64, 128), ((1,), (0,)))


def image_kernel(
    steps_all, middle_ref, before_ref, after_ref, wide_ref, h_ref, weight_ref, theta_ref, meta_ref,
    out_ref, context_ref, errors_ref,
):
    slab, y = meta_ref[LAGS], meta_ref[LAGS + 1]
    fill_context((middle_ref, before_ref, after_ref), context_ref)
    base = 16 + 4 * y

    def read(j):
        return context_ref[base + j]

    back = ar_part(read, slab * 512, steps_all, meta_ref, weight_ref, errors_ref)
    theta = theta_ref[...]
    for q in range(4):
        own = read(q)
        value = data_part(h_ref, wide_ref, q) + (RIDGE_TIME - theta) * own + AR * back[q]
        for j in range(8):
            out_ref[j, q] = value


def two_sum(a, b):
    s = a + b
    t = s - a
    return s, (a - (s - t)) + (b - t)


def pair_add(a, b):
    s, e = two_sum(a[0], b[0])
    e = e + (a[1] + b[1])
    high = s + e
    return high, e - (high - s)


def split(a):
    c = a * 4097.0
    high = c - (c - a)
    return high, a - high


def pair_mul(a, b):
    p = a[0] * b[0]
    ah, al = split(a[0])
    bh, bl = split(b[0])
    e = ((ah * bh - p) + ah * bl + al * bh) + al * bl
    e = e + (a[0] * b[1] + a[1] * b[0])
    high = p + e
    return high, e - (high - p)


def pair_neg(a):
    return -a[0], -a[1]


def pair_sub(a, b):
    return pair_add(a, pair_neg(b))


def pair_div(a, b):
    first = a[0] / b[0]
    zero = jnp.zeros_like(first)
    rest = pair_sub(a, pair_mul(b, (first, zero)))
    second = rest[0] / b[0]
    return two_sum(first, second)


def pair_tree(values):
    while len(values) > 1:
        values = [
            pair_add(values[i], values[i + 1]) if i + 1 < len(values) else values[i]
            for i in range(0, len(values), 2)
        ]
    return values[0]


def moment_kernel(
    steps_all, middle_ref, before_ref, wide_ref, h_ref, weight_ref, u0_ref, u1_ref, u2_ref, meta_ref,
    out_ref, context_ref,
):
    slab, y = meta_ref[LAGS], meta_ref[LAGS + 1]
    fill_context((middle_ref, before_ref, None), context_ref)
    base = 16 + 4 * y

    def read(j):
        return context_ref[base + j]

    errors = residuals(read, 4, slab * 512, steps_all, meta_ref, weight_ref)
    sums = [jnp.zeros((8, 128), F32)] * 7
    for q in range(4):
        u0, u1, u2 = u0_ref[0, q], u1_ref[0, q], u2_ref[0, q]
        image = data_part(h_ref, wide_ref, q) + RIDGE_TIME * u2
        terms = [u0 * u0, u0 * u1, u0 * u2, u1 * u1, u1 * u2, u2 * u2, u2 * image + AR * (errors[q] * errors[q])]
        sums = [a + b for a, b in zip(sums, terms)]
    zero = jnp.zeros((8, 128), F32)
    sub = iota((8, 128), 0)
    packed = (zero, zero)
    for i in range(7):
        pair = (sums[i], zero)
        for by in (4, 2, 1):
            pair = pair_add(pair, (pltpu.roll(pair[0], by, axis=0), pltpu.roll(pair[1], by, axis=0)))
        packed = (jnp.where(sub == i, pair[0], packed[0]), jnp.where(sub == i, pair[1], packed[1]))
    for by in (64, 32, 16, 8, 4, 2, 1):
        packed = pair_add(packed, (pltpu.roll(packed[0], by, axis=1), pltpu.roll(packed[1], by, axis=1)))
    value = jnp.where(iota((8, 128), 1) < 64, packed[0], packed[1])
    out_ref[...] = jnp.broadcast_to(value[None], out_ref.shape)


def sum_pairs(parts_ref, count):
    half = iota((8, 128), 1) < 64
    pairs = []
    for j in range(count):
        part = parts_ref[j]
        other = pltpu.roll(part, 64, axis=1)
        pairs.append((jnp.where(half, part, other), jnp.where(half, other, part)))
    return pair_tree(pairs)


def join_kernel(parts_ref, out_ref):
    high, low = sum_pairs(parts_ref, 8)
    value = jnp.where(iota((8, 128), 1) < 64, high, low)
    out_ref[...] = jnp.broadcast_to(value[None], out_ref.shape)


def finish_kernel(parts_ref, theta_ref, x_ref, wide0_ref, wide1_ref, wide2_ref, out_ref):
    high, low = sum_pairs(parts_ref, 64)

    def moment(i):
        return tuple(jnp.broadcast_to(a[i : i + 1], (8, 128)) for a in (high, low))

    g00, g01, g02, g11, g12, g22, m22 = [moment(i) for i in range(7)]
    theta = (theta_ref[...], jnp.zeros((8, 128), F32))
    m00 = pair_add(g01, pair_mul(theta, g00))
    m01 = pair_add(g11, pair_mul(theta, g01))
    m02 = pair_add(g12, pair_mul(theta, g02))
    m11 = pair_add(g12, pair_mul(theta, g11))
    m12 = pair_add(g22, pair_mul(theta, g12))
    l10 = pair_div(m01, m00)
    l20 = pair_div(m02, m00)
    d1 = pair_sub(m11, pair_mul(l10, m01))
    n12 = pair_sub(m12, pair_mul(l10, m02))
    y1 = pair_sub(g01, pair_mul(l10, g00))
    l21 = pair_div(n12, d1)
    d2 = pair_sub(pair_sub(m22, pair_mul(l20, m02)), pair_mul(l21, n12))
    y2 = pair_sub(pair_sub(g02, pair_mul(l20, g00)), pair_mul(l21, y1))
    tiny = 1e-12
    c2 = jnp.where(d2[0] > tiny * m22[0], y2[0] / d2[0], 0.0)
    zero = jnp.zeros_like(c2)
    c1 = pair_sub(pair_div(y1, d1), pair_mul(l21, (c2, zero)))
    c1 = jnp.where(d1[0] > tiny * m11[0], c1[0], 0.0)
    c0 = pair_div(g00, m00)
    c0 = pair_sub(c0, pair_mul(l10, (c1, zero)))
    c0 = pair_sub(c0, pair_mul(l20, (c2, zero)))[0]
    for s in range(8):
        for q in range(4):
            at = (slice(8 * s, 8 * s + 8), slice(128 * q, 128 * q + 128))
            step = c0 * wide0_ref[s, q] + c1 * wide1_ref[s, q] + c2 * wide2_ref[s, q]
            out_ref[at] = x_ref[at] + step


def ring(length, by):
    return [(i, (i + by) % length) for i in range(length)]


def planes(spread, both):
    middle = lax.all_to_all(spread, "ty", 0, 0).reshape(32, 8, 128)
    count = lax.axis_size("tz")
    before = lax.ppermute(middle[16:32], "tz", ring(count, 1))
    after = lax.ppermute(middle[0:16], "tz", ring(count, -1)) if both else None
    return middle, before, after


def per_device(panel, observed, start_time, ar_weight, lags):
    cells = panel.shape[0]
    steps_all = 64 * 512
    cells_all = cells * 8
    series = lax.axis_index("series")
    y = lax.axis_index("ty")
    slab = lax.axis_index("tz") * 8 + y
    meta = jnp.concatenate([lags, jnp.stack([slab, y]).astype(jnp.int32)])
    own_weight = lax.dynamic_slice_in_dim(ar_weight, 8 * series, 8, 0)
    weight = jnp.broadcast_to(own_weight.T[:, :, None], (LAGS, 8, 128))
    theta = RIDGE_TIME + AR * (1.0 + jnp.sum(ar_weight * ar_weight) / 64.0)
    theta = jnp.broadcast_to(theta, (8, 128))
    context = pltpu.VMEM((64, 8, 128), F32)
    errors = pltpu.VMEM((20, 8, 128), F32)

    own_x = lax.dynamic_slice_in_dim(start_time, 8 * series, 8, 0).reshape(8, 4, 128).transpose(1, 0, 2)
    near_x = planes(jnp.broadcast_to(own_x[None], (8, 4, 8, 128)), True)

    parts = call(front_kernel, struct(64, 40, 128), (panel, observed, start_time))
    parts = lax.all_to_all(parts, TM, 0, 0)
    solved = call(solve_kernel, struct(64, 1, 128), (parts,))
    gathered = lax.all_to_all(solved, TM, 0, 0).reshape(64, 128)
    factors, normal = call(
        functools.partial(normal_kernel, 1.0 / cells_all),
        (struct(cells, 64), struct(64, 768)),
        (gathered, panel, observed),
    )
    sums = lax.all_to_all(normal.reshape(8, 8, 768), "series", 0, 0)

    def begin(sums, x, middle, before, after, weight, meta, out, h, ctx, err):
        start_kernel(steps_all, sums, x, (middle, before, after), weight, meta, out, h, ctx, err)

    u0, h = call(
        begin,
        (struct(8, 4, 8, 128), struct(4, 8, 64)),
        (sums, start_time, *near_x, weight, meta),
        (context, errors),
    )
    middle, before, after = planes(u0, True)
    wide0 = lax.all_to_all(u0, "series", 0, 0)
    image = functools.partial(image_kernel, steps_all)
    u1 = call(
        image, struct(8, 4, 8, 128), (middle, before, after, wide0, h, weight, theta, meta), (context, errors)
    )
    middle, before, after = planes(u1, True)
    wide1 = lax.all_to_all(u1, "series", 0, 0)
    u2 = call(
        image, struct(8, 4, 8, 128), (middle, before, after, wide1, h, weight, theta, meta), (context, errors)
    )
    middle, before, _ = planes(u2, False)
    wide2 = lax.all_to_all(u2, "series", 0, 0)
    moments = call(
        functools.partial(moment_kernel, steps_all),
        struct(8, 8, 128),
        (middle, before, wide2, h, weight, u0, u1, u2, meta),
        (context,),
    )
    moments = lax.all_to_all(moments, "series", 0, 0)
    moments = call(join_kernel, struct(64, 8, 128), (moments,))
    moments = lax.all_to_all(moments, TM, 0, 0)
    result = call(finish_kernel, struct(64, 512), (moments, theta, start_time, wide0, wide1, wide2))
    return (factors, result)


def solution(mesh):
    grid = Mesh(mesh.devices.reshape(8, 8, 8), ("series", "tz", "ty"))
    return jax.shard_map(
        per_device,
        mesh=grid,
        in_specs=(P("series", TM), P("series", TM), P(None, TM), P(), P()),
        out_specs=(P("series", None), P(None, TM)),
        check_vma=False,
    )
```

```python
import functools

import jax
import jax.numpy as jnp
from jax import lax
from jax.experimental import pallas as pl
from jax.experimental.pallas import tpu as pltpu
from jax.sharding import Mesh, PartitionSpec as P

HIGH = lax.Precision.HIGHEST
TILE = 128
LAGS = 14
LONGEST = 2016
RIDGE_FACTOR = 1.0
RIDGE_TIME = 0.05
AR = 0.25
TM = ("tz", "ty")
F32 = jnp.float32
VMEM = pl.BlockSpec(memory_space=pltpu.VMEM)
SMEM = pl.BlockSpec(memory_space=pltpu.SMEM)


def struct(*shape):
    return jax.ShapeDtypeStruct(shape, F32)


def iota(shape, dim):
    return lax.broadcasted_iota(jnp.int32, shape, dim)


def call(kernel, outs, ins, scratch=()):
    specs = [SMEM if a.dtype == jnp.int32 and a.ndim == 1 else VMEM for a in ins]
    return pl.pallas_call(
        kernel,
        out_shape=outs,
        in_specs=specs,
        out_specs=jax.tree.map(lambda _: VMEM, outs),
        scratch_shapes=list(scratch),
        compiler_params=pltpu.CompilerParams(vmem_limit_bytes=32 * 1024 * 1024),
    )(*ins)


def dot(a, b, dims):
    return lax.dot_general(a, b, (dims, ((), ())), precision=HIGH, preferred_element_type=F32)


def front_kernel(panel_ref, obs_ref, x_ref, own_ref, out_ref):
    flags = obs_ref[...].astype(F32)
    x = x_ref[...]
    row = iota((32, 64), 0)
    col = iota((32, 64), 1)
    keep = (col < 32) | (col - 32 >= row)
    diag_at = iota((64, 128), 0) == iota((64, 128), 1) % 64
    lane = iota((8, 128), 1)
    sub = iota((8, 128), 0)
    packs, masked = [], []
    extra = jnp.zeros((8, 128), F32)
    for b in range(4):
        xb = x[:, b * TILE : (b + 1) * TILE]
        gram = dot(xb, xb, ((1,), (1,)))
        moved = jnp.concatenate([gram[0:32, 32:64], gram[0:32, 0:32]], axis=1)
        packs.append(jnp.where(keep, gram[32:64], moved))
        twice = jnp.concatenate([gram, gram], axis=1)
        diag = jnp.sum(jnp.where(diag_at, twice, 0.0), axis=0, keepdims=True)
        extra = jnp.where((sub == b) & (lane % 64 < 32), diag, extra)
        masked.append(panel_ref[:, b * TILE : (b + 1) * TILE] * flags[:, b : b + 1])
    rhs = dot(jnp.concatenate(masked, axis=1), x, ((1,), (1,)))
    pairs = [jnp.concatenate([packs[0], packs[1]], axis=1), jnp.concatenate([packs[2], packs[3]], axis=1)]
    for y in range(8):
        out_ref[y, 0:32, :] = pairs[0]
        out_ref[y, 32:64, :] = pairs[1]
        first, second = slice(16 * y, 16 * y + 8), slice(16 * y + 8, 16 * y + 16)
        out_ref[y, 64:72, :] = jnp.concatenate([rhs[first], rhs[second]], axis=1)
        tail = extra
        for b in range(4):
            tail = jnp.where(lane // 8 == 4 + b, flags[first, b : b + 1], tail)
            tail = jnp.where(lane // 8 == 12 + b, flags[second, b : b + 1], tail)
        out_ref[y, 72:80, :] = tail
        for q in range(4):
            out_ref[y, 80 + 8 * q : 88 + 8 * q, :] = own_ref[q]


def middle_kernel(parts_ref, out_ref, x_ref):
    lane = iota((8, 128), 1)
    sub = iota((8, 128), 0)
    left = lane < 64
    wide_left = iota((32, 128), 1) < 64
    totals = [None] * 8
    diag = jnp.zeros((8, 128), F32)
    rhs = jnp.zeros((8, 128), F32)
    for y in range(8):
        extra = parts_ref[y, 72:80, :]
        rhs = rhs + parts_ref[y, 64:72, :]
        for pair in range(2):
            both = parts_ref[y, 32 * pair : 32 * pair + 32, :]
            other = pltpu.roll(both, 64, axis=1)
            packs = (jnp.where(wide_left, both, other), jnp.where(wide_left, other, both))
            for half in range(2):
                b = 2 * pair + half
                flag = jnp.where(left, extra[:, 32 + 8 * b : 33 + 8 * b], extra[:, 96 + 8 * b : 97 + 8 * b])
                diag = diag + flag * extra[b : b + 1]
                for z in range(8):
                    term = packs[half] * flag[z : z + 1]
                    totals[z] = term if totals[z] is None else totals[z] + term
        for q in range(4):
            x_ref[4 * y + q] = parts_ref[y, 80 + 8 * q : 88 + 8 * q, :]
    for z in range(8):
        out_ref[z, 0:32, :] = totals[z]
        out_ref[z, 32:40, :] = jnp.where(sub == 0, diag[z : z + 1], jnp.where(sub == 1, rhs[z : z + 1], 0.0))


def solve_kernel(parts_ref, out_ref):
    total = parts_ref[0]
    for j in range(1, 8):
        total = total + parts_ref[j]
    pack = total[0:32]
    diag = total[32:33]
    rhs = total[33:34]
    flipped = jnp.concatenate([pack, pack, pack, pack], axis=0).T
    row = iota((32, 128), 0)
    lane = iota((32, 128), 1)
    group = lane // 32
    col = lane % 32
    first = lane < 64
    upper_t = jnp.where(first, flipped[32:64], flipped[96:128])
    cross = jnp.where(first, flipped[0:32], flipped[64:96])
    odd = group % 2 == 1
    top_left = jnp.where(col < row, pltpu.roll(pack, 96, axis=1), jnp.where(col == row, diag, upper_t))
    top = jnp.where(odd, cross, top_left)
    bottom = jnp.where(odd & (col < row), upper_t, pack)
    eye = (iota((64, 128), 0) == iota((64, 128), 1) % 64).astype(F32)
    mat = jnp.concatenate([top, bottom], axis=0) + RIDGE_FACTOR * eye
    blocks = [mat[8 * i : 8 * i + 8] for i in range(8)]
    side = jnp.broadcast_to(rhs, (8, 128))
    half = iota((8, 128), 1) < 64
    within = iota((8, 128), 1) % 64

    def spread(value, k):
        return jnp.where(half, value[:, k : k + 1], value[:, 64 + k : 65 + k])

    for k in range(64):
        i, r = divmod(k, 8)
        pivot_row = jnp.broadcast_to(blocks[i][r : r + 1], (8, 128))
        inverse = 1.0 / spread(pivot_row, k)
        factor = jnp.where(within == k, 1.0 - inverse, pivot_row * inverse)
        side = side - spread(side, k) * factor
        for m in range(i if r < 7 else i + 1, 8):
            blocks[m] = blocks[m] - spread(blocks[m], k) * factor
    out_ref[...] = jnp.broadcast_to(side[0:1][None], out_ref.shape)


def normal_kernel(scale, gathered_ref, panel_ref, obs_ref, factors_ref, out_ref):
    pieces = []
    for y in range(8):
        pair = gathered_ref[8 * y : 8 * y + 8, :]
        pieces += [pair[:, 0:64], pair[:, 64:128]]
    factors = jnp.concatenate(pieces, axis=0)
    factors_ref[...] = factors
    flags = obs_ref[...].astype(F32)
    for b in range(4):
        flag = flags[:, b : b + 1]
        out_ref[:, b * TILE : (b + 1) * TILE] = scale * dot(
            factors, panel_ref[:, b * TILE : (b + 1) * TILE] * flag, ((0,), (0,))
        )
    for pair in range(2):
        halves = [dot(factors * flags[:, b : b + 1], factors, ((0,), (0,))) for b in (2 * pair, 2 * pair + 1)]
        out_ref[:, 512 + 128 * pair : 640 + 128 * pair] = scale * jnp.concatenate(halves, axis=1)


def lagged(read, count, lags_ref, weight_ref, ahead):
    lane = iota((8, 128), 1)
    sums = [None] * count
    for index in range(LAGS):
        lag = lags_ref[index]
        if ahead:
            start = lag // 128
            shift = lag % 128
        else:
            back = (lag + 127) // 128
            start = -back
            shift = back * 128 - lag
        cut = 128 - shift
        weight = weight_ref[index]
        own = lane < cut
        turn = jnp.where(cut == 128, 0, cut)
        low = pltpu.roll(read(start), turn, axis=1)
        for j in range(count):
            high = pltpu.roll(read(start + j + 1), turn, axis=1)
            term = weight * jnp.where(own, low, high)
            sums[j] = term if sums[j] is None else sums[j] + term
            low = high
    return sums


def residuals(read, count, first_step, steps_all, meta_ref, weight_ref):
    past = lagged(read, count, meta_ref, weight_ref, False)
    lane = iota((8, 128), 1)
    out = []
    for j in range(count):
        step = first_step + 128 * j + lane
        out.append(jnp.where((step >= LONGEST) & (step < steps_all), read(j) - past[j], 0.0))
    return out


def ar_part(read, first_step, steps_all, meta_ref, weight_ref, errors_ref):
    errors = residuals(read, 20, first_step, steps_all, meta_ref, weight_ref)
    for j in range(20):
        errors_ref[j] = errors[j]
    later = lagged(lambda j: errors_ref[j], 4, meta_ref, weight_ref, True)
    return [errors[j] - later[j] for j in range(4)]


def start_kernel(
    steps_all, sums_ref, x_ref, plane_ref, near_ref, weight_ref, meta_ref, out_ref, h_ref, context_ref, errors_ref
):
    slab, y = meta_ref[LAGS], meta_ref[LAGS + 1]
    read = fill_context(plane_ref, near_ref, context_ref, y)
    total = sums_ref[0]
    for j in range(1, 8):
        total = total + sums_ref[j]
    back = ar_part(read, slab * 512, steps_all, meta_ref, weight_ref, errors_ref)
    for q in range(4):
        h = total[:, 512 + 64 * q : 576 + 64 * q]
        h_ref[q] = h
        image = dot(h, x_ref[:, q * 128 : (q + 1) * 128], ((1,), (0,))) + RIDGE_TIME * read(q) + AR * back[q]
        value = total[:, q * 128 : (q + 1) * 128] - image
        for j in range(8):
            out_ref[j, q] = value


def fill_context(plane_ref, near_ref, context_ref, y):
    lower = y < 4
    at = jnp.where(lower, 16, 0)
    near_at = jnp.where(lower, 0, 32)
    near_from = jnp.where(lower, 16, 0)
    for j in range(32):
        context_ref[at + j] = plane_ref[j]
    for j in range(16):
        context_ref[near_at + j] = near_ref[near_from + j]
    base = at + 4 * y
    return lambda j: context_ref[base + j]


def data_part(h_ref, wide_ref, q):
    return dot(h_ref[q], wide_ref[:, q].reshape(64, 128), ((1,), (0,)))


def image_kernel(
    steps_all, plane_ref, near_ref, wide_ref, h_ref, weight_ref, theta_ref, meta_ref,
    out_ref, context_ref, errors_ref,
):
    slab, y = meta_ref[LAGS], meta_ref[LAGS + 1]
    read = fill_context(plane_ref, near_ref, context_ref, y)
    back = ar_part(read, slab * 512, steps_all, meta_ref, weight_ref, errors_ref)
    theta = theta_ref[...]
    for q in range(4):
        own = read(q)
        value = data_part(h_ref, wide_ref, q) + (RIDGE_TIME - theta) * own + AR * back[q]
        for j in range(8):
            out_ref[j, q] = value


def two_sum(a, b):
    s = a + b
    t = s - a
    return s, (a - (s - t)) + (b - t)


def pair_add(a, b):
    s, e = two_sum(a[0], b[0])
    e = e + (a[1] + b[1])
    high = s + e
    return high, e - (high - s)


def split(a):
    c = a * 4097.0
    high = c - (c - a)
    return high, a - high


def pair_mul(a, b):
    p = a[0] * b[0]
    ah, al = split(a[0])
    bh, bl = split(b[0])
    e = ((ah * bh - p) + ah * bl + al * bh) + al * bl
    e = e + (a[0] * b[1] + a[1] * b[0])
    high = p + e
    return high, e - (high - p)


def pair_neg(a):
    return -a[0], -a[1]


def pair_sub(a, b):
    return pair_add(a, pair_neg(b))


def pair_div(a, b):
    first = a[0] / b[0]
    zero = jnp.zeros_like(first)
    rest = pair_sub(a, pair_mul(b, (first, zero)))
    second = rest[0] / b[0]
    return two_sum(first, second)


def pair_tree(values):
    while len(values) > 1:
        values = [
            pair_add(values[i], values[i + 1]) if i + 1 < len(values) else values[i]
            for i in range(0, len(values), 2)
        ]
    return values[0]


def moment_kernel(
    steps_all, plane_ref, near_ref, wide_ref, h_ref, weight_ref, u0_ref, u1_ref, u2_ref, meta_ref,
    out_ref, context_ref,
):
    slab, y = meta_ref[LAGS], meta_ref[LAGS + 1]
    read = fill_context(plane_ref, near_ref, context_ref, y)
    errors = residuals(read, 4, slab * 512, steps_all, meta_ref, weight_ref)
    sums = [jnp.zeros((8, 128), F32)] * 7
    for q in range(4):
        u0, u1, u2 = u0_ref[0, q], u1_ref[0, q], u2_ref[0, q]
        image = data_part(h_ref, wide_ref, q) + RIDGE_TIME * u2
        terms = [u0 * u0, u0 * u1, u0 * u2, u1 * u1, u1 * u2, u2 * u2, u2 * image + AR * (errors[q] * errors[q])]
        sums = [a + b for a, b in zip(sums, terms)]
    zero = jnp.zeros((8, 128), F32)
    sub = iota((8, 128), 0)
    packed = (zero, zero)
    for i in range(7):
        pair = (sums[i], zero)
        for by in (4, 2, 1):
            pair = pair_add(pair, (pltpu.roll(pair[0], by, axis=0), pltpu.roll(pair[1], by, axis=0)))
        packed = (jnp.where(sub == i, pair[0], packed[0]), jnp.where(sub == i, pair[1], packed[1]))
    for by in (64, 32, 16, 8, 4, 2, 1):
        packed = pair_add(packed, (pltpu.roll(packed[0], by, axis=1), pltpu.roll(packed[1], by, axis=1)))
    value = jnp.where(iota((8, 128), 1) < 64, packed[0], packed[1])
    out_ref[...] = jnp.broadcast_to(value[None], out_ref.shape)


def sum_pairs(parts_ref, count):
    half = iota((8, 128), 1) < 64
    pairs = []
    for j in range(count):
        part = parts_ref[j]
        other = pltpu.roll(part, 64, axis=1)
        pairs.append((jnp.where(half, part, other), jnp.where(half, other, part)))
    return pair_tree(pairs)


def join_kernel(parts_ref, out_ref):
    high, low = sum_pairs(parts_ref, 8)
    value = jnp.where(iota((8, 128), 1) < 64, high, low)
    out_ref[...] = jnp.broadcast_to(value[None], out_ref.shape)


def finish_kernel(parts_ref, theta_ref, x_ref, wide0_ref, wide1_ref, wide2_ref, out_ref):
    high, low = sum_pairs(parts_ref, 64)

    def moment(i):
        return tuple(jnp.broadcast_to(a[i : i + 1], (8, 128)) for a in (high, low))

    g00, g01, g02, g11, g12, g22, m22 = [moment(i) for i in range(7)]
    theta = (theta_ref[...], jnp.zeros((8, 128), F32))
    m00 = pair_add(g01, pair_mul(theta, g00))
    m01 = pair_add(g11, pair_mul(theta, g01))
    m02 = pair_add(g12, pair_mul(theta, g02))
    m11 = pair_add(g12, pair_mul(theta, g11))
    m12 = pair_add(g22, pair_mul(theta, g12))
    l10 = pair_div(m01, m00)
    l20 = pair_div(m02, m00)
    d1 = pair_sub(m11, pair_mul(l10, m01))
    n12 = pair_sub(m12, pair_mul(l10, m02))
    y1 = pair_sub(g01, pair_mul(l10, g00))
    l21 = pair_div(n12, d1)
    d2 = pair_sub(pair_sub(m22, pair_mul(l20, m02)), pair_mul(l21, n12))
    y2 = pair_sub(pair_sub(g02, pair_mul(l20, g00)), pair_mul(l21, y1))
    tiny = 1e-12
    c2 = jnp.where(d2[0] > tiny * m22[0], y2[0] / d2[0], 0.0)
    zero = jnp.zeros_like(c2)
    c1 = pair_sub(pair_div(y1, d1), pair_mul(l21, (c2, zero)))
    c1 = jnp.where(d1[0] > tiny * m11[0], c1[0], 0.0)
    c0 = pair_div(g00, m00)
    c0 = pair_sub(c0, pair_mul(l10, (c1, zero)))
    c0 = pair_sub(c0, pair_mul(l20, (c2, zero)))[0]
    for s in range(8):
        for q in range(4):
            at = (slice(8 * s, 8 * s + 8), slice(128 * q, 128 * q + 128))
            step = c0 * wide0_ref[s, q] + c1 * wide1_ref[s, q] + c2 * wide2_ref[s, q]
            out_ref[at] = x_ref[at] + step


def neighbour(plane):
    pairs = [(8 * z + y, 8 * ((z + (1 if y < 4 else -1)) % 8) + y) for z in range(8) for y in range(8)]
    return lax.ppermute(plane, TM, pairs)


def exchange(spread):
    plane = lax.all_to_all(spread, "ty", 0, 0).reshape(32, 8, 128)
    return plane, neighbour(plane), lax.all_to_all(spread, "series", 0, 0)


def per_device(panel, observed, start_time, ar_weight, lags):
    cells = panel.shape[0]
    steps_all = 64 * 512
    cells_all = cells * 8
    series = lax.axis_index("series")
    y = lax.axis_index("ty")
    slab = lax.axis_index("tz") * 8 + y
    meta = jnp.concatenate([lags, jnp.stack([slab, y]).astype(jnp.int32)])
    own_weight = lax.dynamic_slice_in_dim(ar_weight, 8 * series, 8, 0)
    weight = jnp.broadcast_to(own_weight.T[:, :, None], (LAGS, 8, 128))
    theta = RIDGE_TIME + AR * (1.0 + jnp.sum(ar_weight * ar_weight) / 64.0)
    theta = jnp.broadcast_to(theta, (8, 128))
    own_x = lax.dynamic_slice_in_dim(start_time, 8 * series, 8, 0).reshape(8, 4, 128).transpose(1, 0, 2)
    context = pltpu.VMEM((48, 8, 128), F32)
    errors = pltpu.VMEM((20, 8, 128), F32)

    parts = call(front_kernel, struct(8, 112, 128), (panel, observed, start_time, own_x))
    parts = lax.all_to_all(parts, "ty", 0, 0)
    parts, plane = call(middle_kernel, (struct(8, 40, 128), struct(32, 8, 128)), (parts,))
    near = neighbour(plane)
    parts = lax.all_to_all(parts, "tz", 0, 0)
    solved = call(solve_kernel, struct(64, 1, 128), (parts,))
    gathered = lax.all_to_all(solved, ("ty", "tz"), 0, 0).reshape(64, 128)
    factors, normal = call(
        functools.partial(normal_kernel, 1.0 / cells_all),
        (struct(cells, 64), struct(64, 768)),
        (gathered, panel, observed),
    )
    sums = lax.all_to_all(normal.reshape(8, 8, 768), "series", 0, 0)
    u0, h = call(
        functools.partial(start_kernel, steps_all),
        (struct(8, 4, 8, 128), struct(4, 8, 64)),
        (sums, start_time, plane, near, weight, meta),
        (context, errors),
    )

    def image(plane, near, wide):
        return call(
            functools.partial(image_kernel, steps_all),
            struct(8, 4, 8, 128),
            (plane, near, wide, h, weight, theta, meta),
            (context, errors),
        )

    plane, near, wide0 = exchange(u0)
    u1 = image(plane, near, wide0)
    plane, near, wide1 = exchange(u1)
    u2 = image(plane, near, wide1)
    plane, near, wide2 = exchange(u2)
    moments = call(
        functools.partial(moment_kernel, steps_all),
        struct(8, 8, 128),
        (plane, near, wide2, h, weight, u0, u1, u2, meta),
        (context,),
    )
    moments = lax.all_to_all(moments, "series", 0, 0)
    moments = call(join_kernel, struct(64, 8, 128), (moments,))
    moments = lax.all_to_all(moments, TM, 0, 0)
    result = call(finish_kernel, struct(64, 512), (moments, theta, start_time, wide0, wide1, wide2))
    return (factors, result)


def solution(mesh):
    grid = Mesh(mesh.devices.reshape(8, 8, 8), ("series", "tz", "ty"))
    return jax.shard_map(
        per_device,
        mesh=grid,
        in_specs=(P("series", TM), P("series", TM), P(None, TM), P(), P()),
        out_specs=(P("series", None), P(None, TM)),
        check_vma=False,
    )
```

```python
import functools

import jax
import jax.numpy as jnp
from jax import lax
from jax.experimental import pallas as pl
from jax.experimental.pallas import tpu as pltpu
from jax.sharding import Mesh, PartitionSpec as P

HIGH = lax.Precision.HIGHEST
TILE = 128
LAGS = 14
LONGEST = 2016
RIDGE_FACTOR = 1.0
RIDGE_TIME = 0.05
AR = 0.25
TM = ("tz", "ty")
F32 = jnp.float32
VMEM = pl.BlockSpec(memory_space=pltpu.VMEM)
HBM = pl.BlockSpec(memory_space=pltpu.HBM)
SMEM = pl.BlockSpec(memory_space=pltpu.SMEM)


def struct(*shape):
    return jax.ShapeDtypeStruct(shape, F32)


def iota(shape, dim):
    return lax.broadcasted_iota(jnp.int32, shape, dim)


def call(kernel, outs, ins, scratch=(), place=VMEM, room=32):
    specs = [SMEM if a.dtype == jnp.int32 and a.ndim == 1 else place for a in ins]
    return pl.pallas_call(
        kernel,
        out_shape=outs,
        in_specs=specs,
        out_specs=jax.tree.map(lambda _: VMEM, outs),
        scratch_shapes=list(scratch),
        compiler_params=pltpu.CompilerParams(vmem_limit_bytes=room * 1024 * 1024),
    )(*ins)


def dot(a, b, dims):
    return lax.dot_general(a, b, (dims, ((), ())), precision=HIGH, preferred_element_type=F32)


def columns_of(obs_ref):
    flags = obs_ref[...].astype(F32)
    return jnp.concatenate([flags] * 32, axis=0).T


def front_kernel(panel_hbm, obs_hbm, x_hbm, out_ref, panel_ref, obs_ref, x_ref, sems):
    copies = [
        pltpu.make_async_copy(source, target, sems.at[i])
        for i, (source, target) in enumerate(((x_hbm, x_ref), (obs_hbm, obs_ref), (panel_hbm, panel_ref)))
    ]
    for copy in copies:
        copy.start()
    copies[0].wait()
    x = x_ref[...]
    row = iota((32, 64), 0)
    col = iota((32, 64), 1)
    keep = (col < 32) | (col - 32 >= row)
    diag_at = iota((64, 128), 0) == iota((64, 128), 1) % 64
    lane = iota((8, 128), 1)
    sub = iota((8, 128), 0)
    packs, masked = [], []
    extra = jnp.zeros((8, 128), F32)
    for b in range(4):
        xb = x[:, b * TILE : (b + 1) * TILE]
        gram = dot(xb, xb, ((1,), (1,)))
        moved = jnp.concatenate([gram[0:32, 32:64], gram[0:32, 0:32]], axis=1)
        packs.append(jnp.where(keep, gram[32:64], moved))
        twice = jnp.concatenate([gram, gram], axis=1)
        diag = jnp.sum(jnp.where(diag_at, twice, 0.0), axis=0, keepdims=True)
        extra = jnp.where((sub == b) & (lane % 64 < 32), diag, extra)
    copies[1].wait()
    flags = columns_of(obs_ref)
    copies[2].wait()
    for b in range(4):
        masked.append(panel_ref[:, b * TILE : (b + 1) * TILE] * flags[:, b : b + 1])
    rhs = dot(jnp.concatenate(masked, axis=1), x, ((1,), (1,)))
    mine = pl.ds(pl.multiple_of(8 * lax.axis_index("series"), 8), 8)
    own = [x_ref[mine, q * TILE : (q + 1) * TILE] for q in range(4)]
    pairs = [jnp.concatenate([packs[0], packs[1]], axis=1), jnp.concatenate([packs[2], packs[3]], axis=1)]
    for y in range(8):
        out_ref[y, 0:32, :] = pairs[0]
        out_ref[y, 32:64, :] = pairs[1]
        first, second = slice(16 * y, 16 * y + 8), slice(16 * y + 8, 16 * y + 16)
        out_ref[y, 64:72, :] = jnp.concatenate([rhs[first], rhs[second]], axis=1)
        tail = extra
        for b in range(4):
            tail = jnp.where(lane // 8 == 4 + b, flags[first, b : b + 1], tail)
            tail = jnp.where(lane // 8 == 12 + b, flags[second, b : b + 1], tail)
        out_ref[y, 72:80, :] = tail
        for q in range(4):
            out_ref[y, 80 + 8 * q : 88 + 8 * q, :] = own[q]


def middle_kernel(parts_ref, out_ref, x_ref):
    lane = iota((8, 128), 1)
    sub = iota((8, 128), 0)
    left = lane < 64
    wide_left = iota((32, 128), 1) < 64
    totals = [None] * 8
    diag = jnp.zeros((8, 128), F32)
    rhs = jnp.zeros((8, 128), F32)
    for y in range(8):
        extra = parts_ref[y, 72:80, :]
        rhs = rhs + parts_ref[y, 64:72, :]
        for pair in range(2):
            both = parts_ref[y, 32 * pair : 32 * pair + 32, :]
            other = pltpu.roll(both, 64, axis=1)
            packs = (jnp.where(wide_left, both, other), jnp.where(wide_left, other, both))
            for half in range(2):
                b = 2 * pair + half
                flag = jnp.where(left, extra[:, 32 + 8 * b : 33 + 8 * b], extra[:, 96 + 8 * b : 97 + 8 * b])
                diag = diag + flag * extra[b : b + 1]
                for z in range(8):
                    term = packs[half] * flag[z : z + 1]
                    totals[z] = term if totals[z] is None else totals[z] + term
        for q in range(4):
            x_ref[4 * y + q] = parts_ref[y, 80 + 8 * q : 88 + 8 * q, :]
    for z in range(8):
        out_ref[z, 0:32, :] = totals[z]
        out_ref[z, 32:40, :] = jnp.where(sub == 0, diag[z : z + 1], jnp.where(sub == 1, rhs[z : z + 1], 0.0))


def solve_kernel(parts_ref, out_ref):
    total = parts_ref[0]
    for j in range(1, 8):
        total = total + parts_ref[j]
    pack = total[0:32]
    diag = total[32:33]
    rhs = total[33:34]
    flipped = jnp.concatenate([pack, pack, pack, pack], axis=0).T
    row = iota((32, 128), 0)
    lane = iota((32, 128), 1)
    group = lane // 32
    col = lane % 32
    first = lane < 64
    upper_t = jnp.where(first, flipped[32:64], flipped[96:128])
    cross = jnp.where(first, flipped[0:32], flipped[64:96])
    odd = group % 2 == 1
    top_left = jnp.where(col < row, pltpu.roll(pack, 96, axis=1), jnp.where(col == row, diag, upper_t))
    top = jnp.where(odd, cross, top_left)
    bottom = jnp.where(odd & (col < row), upper_t, pack)
    eye = (iota((64, 128), 0) == iota((64, 128), 1) % 64).astype(F32)
    mat = jnp.concatenate([top, bottom], axis=0) + RIDGE_FACTOR * eye
    blocks = [mat[8 * i : 8 * i + 8] for i in range(8)]
    side = jnp.broadcast_to(rhs, (8, 128))
    half = iota((8, 128), 1) < 64
    within = iota((8, 128), 1) % 64

    def spread(value, k):
        return jnp.where(half, value[:, k : k + 1], value[:, 64 + k : 65 + k])

    for i in range(8):
        columns = [[spread(blocks[m], 8 * i + j) for j in range(8)] for m in range(i, 8)]
        ends = [spread(side, 8 * i + j) for j in range(8)]
        for r in range(8):
            inverse = 1.0 / jnp.broadcast_to(columns[0][r][r : r + 1], (8, 128))
            pivot_row = jnp.broadcast_to(blocks[i][r : r + 1], (8, 128))
            factor = jnp.where(within == 8 * i + r, 1.0 - inverse, pivot_row * inverse)
            factors = [jnp.broadcast_to(columns[0][j][r : r + 1], (8, 128)) * inverse for j in range(r + 1, 8)]
            for m in range(i if r < 7 else i + 1, 8):
                own = columns[m - i]
                blocks[m] = blocks[m] - own[r] * factor
                for j in range(r + 1, 8):
                    own[j] = own[j] - own[r] * factors[j - r - 1]
            side = side - ends[r] * factor
            for j in range(r + 1, 8):
                ends[j] = ends[j] - ends[r] * factors[j - r - 1]
    out_ref[...] = jnp.broadcast_to(side[0:1][None], out_ref.shape)


def normal_kernel(scale, gathered_ref, panel_ref, obs_ref, factors_ref, out_ref):
    pieces = []
    for y in range(8):
        pair = gathered_ref[8 * y : 8 * y + 8, :]
        pieces += [pair[:, 0:64], pair[:, 64:128]]
    factors = jnp.concatenate(pieces, axis=0)
    factors_ref[...] = factors
    flags = columns_of(obs_ref)
    for b in range(4):
        flag = flags[:, b : b + 1]
        out_ref[:, b * TILE : (b + 1) * TILE] = scale * dot(
            factors, panel_ref[:, b * TILE : (b + 1) * TILE] * flag, ((0,), (0,))
        )
    for pair in range(2):
        halves = [dot(factors * flags[:, b : b + 1], factors, ((0,), (0,))) for b in (2 * pair, 2 * pair + 1)]
        out_ref[:, 512 + 128 * pair : 640 + 128 * pair] = scale * jnp.concatenate(halves, axis=1)


def lagged(read, count, lags_ref, weight_ref, ahead):
    lane = iota((8, 128), 1)
    sums = [None] * count
    for index in range(LAGS):
        lag = lags_ref[index]
        if ahead:
            start = lag // 128
            shift = lag % 128
        else:
            back = (lag + 127) // 128
            start = -back
            shift = back * 128 - lag
        cut = 128 - shift
        weight = weight_ref[index]
        own = lane < cut
        turn = jnp.where(cut == 128, 0, cut)
        low = pltpu.roll(read(start), turn, axis=1)
        for j in range(count):
            high = pltpu.roll(read(start + j + 1), turn, axis=1)
            term = weight * jnp.where(own, low, high)
            sums[j] = term if sums[j] is None else sums[j] + term
            low = high
    return sums


def residuals(read, count, first_step, steps_all, lags_ref, weight_ref):
    past = lagged(read, count, lags_ref, weight_ref, False)
    lane = iota((8, 128), 1)
    out = []
    for j in range(count):
        step = first_step + 128 * j + lane
        out.append(jnp.where((step >= LONGEST) & (step < steps_all), read(j) - past[j], 0.0))
    return out


def ar_part(read, first_step, steps_all, lags_ref, weight_ref, errors_ref):
    errors = residuals(read, 20, first_step, steps_all, lags_ref, weight_ref)
    for j in range(20):
        errors_ref[j] = errors[j]
    later = lagged(lambda j: errors_ref[j], 4, lags_ref, weight_ref, True)
    return [errors[j] - later[j] for j in range(4)]


def place():
    y = lax.axis_index("ty")
    return lax.axis_index("tz") * 8 + y, y


def start_kernel(
    steps_all, sums_ref, x_ref, plane_ref, near_ref, weight_ref, lags_ref, out_ref, h_ref, context_ref, errors_ref
):
    slab, y = place()
    read = fill_context(plane_ref, near_ref, context_ref, y)
    total = sums_ref[0]
    for j in range(1, 8):
        total = total + sums_ref[j]
    back = ar_part(read, slab * 512, steps_all, lags_ref, weight_ref, errors_ref)
    for q in range(4):
        h = total[:, 512 + 64 * q : 576 + 64 * q]
        h_ref[q] = h
        image = dot(h, x_ref[:, q * 128 : (q + 1) * 128], ((1,), (0,))) + RIDGE_TIME * read(q) + AR * back[q]
        value = total[:, q * 128 : (q + 1) * 128] - image
        for j in range(8):
            out_ref[j, q] = value


def fill_context(plane_ref, near_ref, context_ref, y):
    lower = y < 4
    at = jnp.where(lower, 16, 0)
    near_at = jnp.where(lower, 0, 32)
    near_from = jnp.where(lower, 16, 0)
    for j in range(32):
        context_ref[at + j] = plane_ref[j]
    for j in range(16):
        context_ref[near_at + j] = near_ref[near_from + j]
    base = at + 4 * y
    return lambda j: context_ref[base + j]


def data_part(h_ref, wide_ref, q):
    return dot(h_ref[q], wide_ref[:, q].reshape(64, 128), ((1,), (0,)))


def image_kernel(
    steps_all, plane_ref, near_ref, wide_ref, h_ref, weight_ref, theta_ref, lags_ref,
    out_ref, context_ref, errors_ref,
):
    slab, y = place()
    read = fill_context(plane_ref, near_ref, context_ref, y)
    back = ar_part(read, slab * 512, steps_all, lags_ref, weight_ref, errors_ref)
    theta = theta_ref[...]
    for q in range(4):
        own = read(q)
        value = data_part(h_ref, wide_ref, q) + (RIDGE_TIME - theta) * own + AR * back[q]
        for j in range(8):
            out_ref[j, q] = value


def two_sum(a, b):
    s = a + b
    t = s - a
    return s, (a - (s - t)) + (b - t)


def pair_add(a, b):
    s, e = two_sum(a[0], b[0])
    e = e + (a[1] + b[1])
    high = s + e
    return high, e - (high - s)


def split(a):
    c = a * 4097.0
    high = c - (c - a)
    return high, a - high


def pair_mul(a, b):
    p = a[0] * b[0]
    ah, al = split(a[0])
    bh, bl = split(b[0])
    e = ((ah * bh - p) + ah * bl + al * bh) + al * bl
    e = e + (a[0] * b[1] + a[1] * b[0])
    high = p + e
    return high, e - (high - p)


def pair_neg(a):
    return -a[0], -a[1]


def pair_sub(a, b):
    return pair_add(a, pair_neg(b))


def pair_div(a, b):
    first = a[0] / b[0]
    zero = jnp.zeros_like(first)
    rest = pair_sub(a, pair_mul(b, (first, zero)))
    second = rest[0] / b[0]
    return two_sum(first, second)


def pair_tree(values):
    while len(values) > 1:
        values = [
            pair_add(values[i], values[i + 1]) if i + 1 < len(values) else values[i]
            for i in range(0, len(values), 2)
        ]
    return values[0]


def moment_kernel(
    steps_all, plane_ref, near_ref, wide_ref, h_ref, weight_ref, u0_ref, u1_ref, u2_ref, lags_ref,
    out_ref, context_ref,
):
    slab, y = place()
    read = fill_context(plane_ref, near_ref, context_ref, y)
    errors = residuals(read, 4, slab * 512, steps_all, lags_ref, weight_ref)
    sums = [jnp.zeros((8, 128), F32)] * 7
    for q in range(4):
        u0, u1, u2 = u0_ref[0, q], u1_ref[0, q], u2_ref[0, q]
        image = data_part(h_ref, wide_ref, q) + RIDGE_TIME * u2
        terms = [u0 * u0, u0 * u1, u0 * u2, u1 * u1, u1 * u2, u2 * u2, u2 * image + AR * (errors[q] * errors[q])]
        sums = [a + b for a, b in zip(sums, terms)]
    zero = jnp.zeros((8, 128), F32)
    sub = iota((8, 128), 0)
    packed = (zero, zero)
    for i in range(7):
        pair = (sums[i], zero)
        for by in (4, 2, 1):
            pair = pair_add(pair, (pltpu.roll(pair[0], by, axis=0), pltpu.roll(pair[1], by, axis=0)))
        packed = (jnp.where(sub == i, pair[0], packed[0]), jnp.where(sub == i, pair[1], packed[1]))
    for by in (64, 32, 16, 8, 4, 2, 1):
        packed = pair_add(packed, (pltpu.roll(packed[0], by, axis=1), pltpu.roll(packed[1], by, axis=1)))
    value = jnp.where(iota((8, 128), 1) < 64, packed[0], packed[1])
    out_ref[...] = jnp.broadcast_to(value[None], out_ref.shape)


def sum_pairs(parts_ref, count):
    half = iota((8, 128), 1) < 64
    pairs = []
    for j in range(count):
        part = parts_ref[j]
        other = pltpu.roll(part, 64, axis=1)
        pairs.append((jnp.where(half, part, other), jnp.where(half, other, part)))
    return pair_tree(pairs)


def join_kernel(parts_ref, out_ref):
    high, low = sum_pairs(parts_ref, 8)
    value = jnp.where(iota((8, 128), 1) < 64, high, low)
    out_ref[...] = jnp.broadcast_to(value[None], out_ref.shape)


def finish_kernel(parts_ref, theta_ref, x_ref, wide0_ref, wide1_ref, wide2_ref, out_ref):
    high, low = sum_pairs(parts_ref, 64)

    def moment(i):
        return tuple(jnp.broadcast_to(a[i : i + 1], (8, 128)) for a in (high, low))

    g00, g01, g02, g11, g12, g22, m22 = [moment(i) for i in range(7)]
    theta = (theta_ref[...], jnp.zeros((8, 128), F32))
    m00 = pair_add(g01, pair_mul(theta, g00))
    m01 = pair_add(g11, pair_mul(theta, g01))
    m02 = pair_add(g12, pair_mul(theta, g02))
    m11 = pair_add(g12, pair_mul(theta, g11))
    m12 = pair_add(g22, pair_mul(theta, g12))
    l10 = pair_div(m01, m00)
    l20 = pair_div(m02, m00)
    d1 = pair_sub(m11, pair_mul(l10, m01))
    n12 = pair_sub(m12, pair_mul(l10, m02))
    y1 = pair_sub(g01, pair_mul(l10, g00))
    l21 = pair_div(n12, d1)
    d2 = pair_sub(pair_sub(m22, pair_mul(l20, m02)), pair_mul(l21, n12))
    y2 = pair_sub(pair_sub(g02, pair_mul(l20, g00)), pair_mul(l21, y1))
    tiny = 1e-12
    c2 = jnp.where(d2[0] > tiny * m22[0], y2[0] / d2[0], 0.0)
    zero = jnp.zeros_like(c2)
    c1 = pair_sub(pair_div(y1, d1), pair_mul(l21, (c2, zero)))
    c1 = jnp.where(d1[0] > tiny * m11[0], c1[0], 0.0)
    c0 = pair_div(g00, m00)
    c0 = pair_sub(c0, pair_mul(l10, (c1, zero)))
    c0 = pair_sub(c0, pair_mul(l20, (c2, zero)))[0]
    for s in range(8):
        for q in range(4):
            at = (slice(8 * s, 8 * s + 8), slice(128 * q, 128 * q + 128))
            step = c0 * wide0_ref[s, q] + c1 * wide1_ref[s, q] + c2 * wide2_ref[s, q]
            out_ref[at] = x_ref[at] + step


def neighbour(plane):
    pairs = [(8 * z + y, 8 * ((z + (1 if y < 4 else -1)) % 8) + y) for z in range(8) for y in range(8)]
    return lax.ppermute(plane, TM, pairs)


def exchange(spread):
    plane = lax.all_to_all(spread, "ty", 0, 0).reshape(32, 8, 128)
    return plane, neighbour(plane), lax.all_to_all(spread, "series", 0, 0)


def per_device(panel, observed, start_time, ar_weight, lags):
    cells = panel.shape[0]
    steps_all = 64 * 512
    cells_all = cells * 8
    series = lax.axis_index("series")
    own_weight = lax.dynamic_slice_in_dim(ar_weight, 8 * series, 8, 0)
    weight = jnp.broadcast_to(own_weight.T[:, :, None], (LAGS, 8, 128))
    theta = RIDGE_TIME + AR * (1.0 + jnp.sum(ar_weight * ar_weight) / 64.0)
    theta = jnp.broadcast_to(theta, (8, 128))
    observed = observed.T
    context = pltpu.VMEM((48, 8, 128), F32)
    errors = pltpu.VMEM((20, 8, 128), F32)

    parts = call(
        front_kernel,
        struct(8, 112, 128),
        (panel, observed, start_time),
        (
            pltpu.VMEM(panel.shape, F32),
            pltpu.VMEM(observed.shape, jnp.int32),
            pltpu.VMEM(start_time.shape, F32),
            pltpu.SemaphoreType.DMA((3,)),
        ),
        HBM,
        60,
    )
    parts = lax.all_to_all(parts, "ty", 0, 0)
    parts, plane = call(middle_kernel, (struct(8, 40, 128), struct(32, 8, 128)), (parts,))
    parts = lax.all_to_all(parts, "tz", 0, 0)
    solved = call(solve_kernel, struct(64, 1, 128), (parts,))
    solved, plane = lax.optimization_barrier((solved, plane))
    near = neighbour(plane)
    gathered = lax.all_to_all(solved, ("ty", "tz"), 0, 0).reshape(64, 128)
    gathered, near = lax.optimization_barrier((gathered, near))
    factors, normal = call(
        functools.partial(normal_kernel, 1.0 / cells_all),
        (struct(cells, 64), struct(64, 768)),
        (gathered, panel, observed),
    )
    sums = lax.all_to_all(normal.reshape(8, 8, 768), "series", 0, 0)
    u0, h = call(
        functools.partial(start_kernel, steps_all),
        (struct(8, 4, 8, 128), struct(4, 8, 64)),
        (sums, start_time, plane, near, weight, lags),
        (context, errors),
    )

    def image(plane, near, wide):
        return call(
            functools.partial(image_kernel, steps_all),
            struct(8, 4, 8, 128),
            (plane, near, wide, h, weight, theta, lags),
            (context, errors),
        )

    plane, near, wide0 = exchange(u0)
    u1 = image(plane, near, wide0)
    plane, near, wide1 = exchange(u1)
    u2 = image(plane, near, wide1)
    plane, near, wide2 = exchange(u2)
    moments = call(
        functools.partial(moment_kernel, steps_all),
        struct(8, 8, 128),
        (plane, near, wide2, h, weight, u0, u1, u2, lags),
        (context,),
    )
    moments = lax.all_to_all(moments, "series", 0, 0)
    moments = call(join_kernel, struct(64, 8, 128), (moments,))
    moments = lax.all_to_all(moments, TM, 0, 0)
    result = call(finish_kernel, struct(64, 512), (moments, theta, start_time, wide0, wide1, wide2))
    return (factors, result)


def solution(mesh):
    grid = Mesh(mesh.devices.reshape(8, 8, 8), ("series", "tz", "ty"))
    return jax.shard_map(
        per_device,
        mesh=grid,
        in_specs=(P("series", TM), P("series", TM), P(None, TM), P(), P()),
        out_specs=(P("series", None), P(None, TM)),
        check_vma=False,
    )
```

```python
import functools

import jax
import jax.numpy as jnp
from jax import lax
from jax.experimental import pallas as pl
from jax.experimental.pallas import tpu as pltpu
from jax.sharding import Mesh, PartitionSpec as P

HIGH = lax.Precision.HIGHEST
TILE = 128
LAGS = 14
LONGEST = 2016
RIDGE_FACTOR = 1.0
RIDGE_TIME = 0.05
AR = 0.25
TM = ("tz", "ty")
F32 = jnp.float32
VMEM = pl.BlockSpec(memory_space=pltpu.VMEM)
HBM = pl.BlockSpec(memory_space=pltpu.HBM)
SMEM = pl.BlockSpec(memory_space=pltpu.SMEM)


def struct(*shape):
    return jax.ShapeDtypeStruct(shape, F32)


def iota(shape, dim):
    return lax.broadcasted_iota(jnp.int32, shape, dim)


def call(kernel, outs, ins, scratch=(), place=VMEM, room=32):
    specs = [SMEM if a.dtype == jnp.int32 and a.ndim == 1 else place for a in ins]
    return pl.pallas_call(
        kernel,
        out_shape=outs,
        in_specs=specs,
        out_specs=jax.tree.map(lambda _: VMEM, outs),
        scratch_shapes=list(scratch),
        compiler_params=pltpu.CompilerParams(vmem_limit_bytes=room * 1024 * 1024),
    )(*ins)


def dot(a, b, dims):
    return lax.dot_general(a, b, (dims, ((), ())), precision=HIGH, preferred_element_type=F32)


def columns_of(obs_ref):
    flags = obs_ref[...].astype(F32)
    return jnp.concatenate([flags] * 32, axis=0).T


def front_kernel(panel_hbm, obs_hbm, x_hbm, out_ref, panel_ref, obs_ref, x_ref, sems):
    copies = [
        pltpu.make_async_copy(source, target, sems.at[i])
        for i, (source, target) in enumerate(((x_hbm, x_ref), (obs_hbm, obs_ref), (panel_hbm, panel_ref)))
    ]
    for copy in copies:
        copy.start()
    copies[0].wait()
    x = x_ref[...]
    row = iota((32, 64), 0)
    col = iota((32, 64), 1)
    keep = (col < 32) | (col - 32 >= row)
    diag_at = iota((64, 128), 0) == iota((64, 128), 1) % 64
    lane = iota((8, 128), 1)
    sub = iota((8, 128), 0)
    packs, masked = [], []
    extra = jnp.zeros((8, 128), F32)
    for b in range(4):
        xb = x[:, b * TILE : (b + 1) * TILE]
        gram = dot(xb, xb, ((1,), (1,)))
        moved = jnp.concatenate([gram[0:32, 32:64], gram[0:32, 0:32]], axis=1)
        packs.append(jnp.where(keep, gram[32:64], moved))
        twice = jnp.concatenate([gram, gram], axis=1)
        diag = jnp.sum(jnp.where(diag_at, twice, 0.0), axis=0, keepdims=True)
        extra = jnp.where((sub == b) & (lane % 64 < 32), diag, extra)
    copies[1].wait()
    flags = columns_of(obs_ref)
    copies[2].wait()
    for b in range(4):
        masked.append(panel_ref[:, b * TILE : (b + 1) * TILE] * flags[:, b : b + 1])
    rhs = dot(jnp.concatenate(masked, axis=1), x, ((1,), (1,)))
    mine = pl.ds(pl.multiple_of(8 * lax.axis_index("series"), 8), 8)
    own = [x_ref[mine, q * TILE : (q + 1) * TILE] for q in range(4)]
    pairs = [jnp.concatenate([packs[0], packs[1]], axis=1), jnp.concatenate([packs[2], packs[3]], axis=1)]
    for y in range(8):
        out_ref[y, 0:32, :] = pairs[0]
        out_ref[y, 32:64, :] = pairs[1]
        first, second = slice(16 * y, 16 * y + 8), slice(16 * y + 8, 16 * y + 16)
        out_ref[y, 64:72, :] = jnp.concatenate([rhs[first], rhs[second]], axis=1)
        tail = extra
        for b in range(4):
            tail = jnp.where(lane // 8 == 4 + b, flags[first, b : b + 1], tail)
            tail = jnp.where(lane // 8 == 12 + b, flags[second, b : b + 1], tail)
        out_ref[y, 72:80, :] = tail
        for q in range(4):
            out_ref[y, 80 + 8 * q : 88 + 8 * q, :] = own[q]


def middle_kernel(parts_ref, out_ref, x_ref):
    lane = iota((8, 128), 1)
    sub = iota((8, 128), 0)
    left = lane < 64
    wide_left = iota((32, 128), 1) < 64
    totals = [None] * 8
    diag = jnp.zeros((8, 128), F32)
    rhs = jnp.zeros((8, 128), F32)
    for y in range(8):
        extra = parts_ref[y, 72:80, :]
        rhs = rhs + parts_ref[y, 64:72, :]
        for pair in range(2):
            both = parts_ref[y, 32 * pair : 32 * pair + 32, :]
            other = pltpu.roll(both, 64, axis=1)
            packs = (jnp.where(wide_left, both, other), jnp.where(wide_left, other, both))
            for half in range(2):
                b = 2 * pair + half
                flag = jnp.where(left, extra[:, 32 + 8 * b : 33 + 8 * b], extra[:, 96 + 8 * b : 97 + 8 * b])
                diag = diag + flag * extra[b : b + 1]
                for z in range(8):
                    term = packs[half] * flag[z : z + 1]
                    totals[z] = term if totals[z] is None else totals[z] + term
        for q in range(4):
            x_ref[4 * y + q] = parts_ref[y, 80 + 8 * q : 88 + 8 * q, :]
    for z in range(8):
        out_ref[z, 0:32, :] = totals[z]
        out_ref[z, 32:40, :] = jnp.where(sub == 0, diag[z : z + 1], jnp.where(sub == 1, rhs[z : z + 1], 0.0))


def solve_kernel(parts_ref, out_ref):
    total = parts_ref[0]
    for j in range(1, 8):
        total = total + parts_ref[j]
    pack = total[0:32]
    diag = total[32:33]
    rhs = total[33:34]
    flipped = jnp.concatenate([pack, pack, pack, pack], axis=0).T
    row = iota((32, 128), 0)
    lane = iota((32, 128), 1)
    group = lane // 32
    col = lane % 32
    first = lane < 64
    upper_t = jnp.where(first, flipped[32:64], flipped[96:128])
    cross = jnp.where(first, flipped[0:32], flipped[64:96])
    odd = group % 2 == 1
    top_left = jnp.where(col < row, pltpu.roll(pack, 96, axis=1), jnp.where(col == row, diag, upper_t))
    top = jnp.where(odd, cross, top_left)
    bottom = jnp.where(odd & (col < row), upper_t, pack)
    eye = (iota((64, 128), 0) == iota((64, 128), 1) % 64).astype(F32)
    mat = jnp.concatenate([top, bottom], axis=0) + RIDGE_FACTOR * eye
    blocks = [mat[8 * i : 8 * i + 8] for i in range(8)]
    side = jnp.broadcast_to(rhs, (8, 128))
    half = iota((8, 128), 1) < 64
    within = iota((8, 128), 1) % 64

    def spread(value, k):
        return jnp.where(half, value[:, k : k + 1], value[:, 64 + k : 65 + k])

    for i in range(8):
        columns = [[spread(blocks[m], 8 * i + j) for j in range(8)] for m in range(i, 8)]
        ends = [spread(side, 8 * i + j) for j in range(8)]
        for r in range(8):
            inverse = 1.0 / jnp.broadcast_to(columns[0][r][r : r + 1], (8, 128))
            pivot_row = jnp.broadcast_to(blocks[i][r : r + 1], (8, 128))
            factor = jnp.where(within == 8 * i + r, 1.0 - inverse, pivot_row * inverse)
            factors = [jnp.broadcast_to(columns[0][j][r : r + 1], (8, 128)) * inverse for j in range(r + 1, 8)]
            for m in range(i if r < 7 else i + 1, 8):
                own = columns[m - i]
                blocks[m] = blocks[m] - own[r] * factor
                for j in range(r + 1, 8):
                    own[j] = own[j] - own[r] * factors[j - r - 1]
            side = side - ends[r] * factor
            for j in range(r + 1, 8):
                ends[j] = ends[j] - ends[r] * factors[j - r - 1]
    out_ref[...] = jnp.broadcast_to(side[0:1][None], out_ref.shape)


def normal_kernel(scale, gathered_ref, panel_ref, obs_ref, factors_ref, out_ref):
    pieces = []
    for y in range(8):
        pair = gathered_ref[8 * y : 8 * y + 8, :]
        pieces += [pair[:, 0:64], pair[:, 64:128]]
    factors = jnp.concatenate(pieces, axis=0)
    factors_ref[...] = factors
    flags = columns_of(obs_ref)
    for b in range(4):
        flag = flags[:, b : b + 1]
        out_ref[:, b * TILE : (b + 1) * TILE] = scale * dot(
            factors, panel_ref[:, b * TILE : (b + 1) * TILE] * flag, ((0,), (0,))
        )
    for pair in range(2):
        halves = [dot(factors * flags[:, b : b + 1], factors, ((0,), (0,))) for b in (2 * pair, 2 * pair + 1)]
        out_ref[:, 512 + 128 * pair : 640 + 128 * pair] = scale * jnp.concatenate(halves, axis=1)


def lagged(read, count, lags_ref, weight_ref, ahead):
    lane = iota((8, 128), 1)
    sums = [None] * count
    for index in range(LAGS):
        lag = lags_ref[index]
        if ahead:
            start = lag // 128
            shift = lag % 128
        else:
            back = (lag + 127) // 128
            start = -back
            shift = back * 128 - lag
        cut = 128 - shift
        weight = weight_ref[index]
        own = lane < cut
        turn = jnp.where(cut == 128, 0, cut)
        low = pltpu.roll(read(start), turn, axis=1)
        for j in range(count):
            high = pltpu.roll(read(start + j + 1), turn, axis=1)
            term = weight * jnp.where(own, low, high)
            sums[j] = term if sums[j] is None else sums[j] + term
            low = high
    return sums


def residuals(read, count, first_step, steps_all, lags_ref, weight_ref):
    past = lagged(read, count, lags_ref, weight_ref, False)
    lane = iota((8, 128), 1)
    out = []
    for j in range(count):
        step = first_step + 128 * j + lane
        out.append(jnp.where((step >= LONGEST) & (step < steps_all), read(j) - past[j], 0.0))
    return out


def ar_part(read, first_step, steps_all, lags_ref, weight_ref, errors_ref):
    errors = residuals(read, 20, first_step, steps_all, lags_ref, weight_ref)
    for j in range(20):
        errors_ref[j] = errors[j]
    later = lagged(lambda j: errors_ref[j], 4, lags_ref, weight_ref, True)
    return [errors[j] - later[j] for j in range(4)]


def place():
    y = lax.axis_index("ty")
    return lax.axis_index("tz") * 8 + y, y


def start_kernel(
    steps_all, sums_ref, x_ref, plane_ref, near_ref, weight_ref, lags_ref,
    out_ref, own_ref, h_ref, context_ref, errors_ref,
):
    slab, y = place()
    read = fill_context(plane_ref, near_ref, context_ref, y)
    total = sums_ref[0]
    for j in range(1, 8):
        total = total + sums_ref[j]
    back = ar_part(read, slab * 512, steps_all, lags_ref, weight_ref, errors_ref)
    for q in range(4):
        h = total[:, 512 + 64 * q : 576 + 64 * q]
        h_ref[q] = h
        image = dot(h, x_ref[:, q * 128 : (q + 1) * 128], ((1,), (0,))) + RIDGE_TIME * read(q) + AR * back[q]
        value = total[:, q * 128 : (q + 1) * 128] - image
        own_ref[q] = value
        for j in range(8):
            out_ref[j, q] = value


def fill_context(plane_ref, near_ref, context_ref, y):
    lower = y < 4
    at = jnp.where(lower, 16, 0)
    near_at = jnp.where(lower, 0, 32)
    near_from = jnp.where(lower, 16, 0)
    for j in range(32):
        context_ref[at + j] = plane_ref[j]
    for j in range(16):
        context_ref[near_at + j] = near_ref[near_from + j]
    base = at + 4 * y
    return lambda j: context_ref[base + j]


def data_part(h_ref, wide_ref, q):
    return dot(h_ref[q], wide_ref[:, q].reshape(64, 128), ((1,), (0,)))


def image_kernel(
    steps_all, plane_ref, near_ref, wide_ref, h_ref, weight_ref, theta_ref, lags_ref,
    out_ref, own_ref, context_ref, errors_ref,
):
    slab, y = place()
    read = fill_context(plane_ref, near_ref, context_ref, y)
    back = ar_part(read, slab * 512, steps_all, lags_ref, weight_ref, errors_ref)
    theta = theta_ref[...]
    for q in range(4):
        own = read(q)
        value = data_part(h_ref, wide_ref, q) + (RIDGE_TIME - theta) * own + AR * back[q]
        own_ref[q] = value
        for j in range(8):
            out_ref[j, q] = value


def two_sum(a, b):
    s = a + b
    t = s - a
    return s, (a - (s - t)) + (b - t)


def pair_add(a, b):
    s, e = two_sum(a[0], b[0])
    e = e + (a[1] + b[1])
    high = s + e
    return high, e - (high - s)


def split(a):
    c = a * 4097.0
    high = c - (c - a)
    return high, a - high


def pair_mul(a, b):
    p = a[0] * b[0]
    ah, al = split(a[0])
    bh, bl = split(b[0])
    e = ((ah * bh - p) + ah * bl + al * bh) + al * bl
    e = e + (a[0] * b[1] + a[1] * b[0])
    high = p + e
    return high, e - (high - p)


def pair_neg(a):
    return -a[0], -a[1]


def pair_sub(a, b):
    return pair_add(a, pair_neg(b))


def pair_div(a, b):
    first = a[0] / b[0]
    zero = jnp.zeros_like(first)
    rest = pair_sub(a, pair_mul(b, (first, zero)))
    second = rest[0] / b[0]
    return two_sum(first, second)


def pair_tree(values):
    while len(values) > 1:
        values = [
            pair_add(values[i], values[i + 1]) if i + 1 < len(values) else values[i]
            for i in range(0, len(values), 2)
        ]
    return values[0]


def fold_rows(value):
    pair = (value, jnp.zeros_like(value))
    for by in (4, 2, 1):
        pair = pair_add(pair, (pltpu.roll(pair[0], by, axis=0), pltpu.roll(pair[1], by, axis=0)))
    return pair


def product_kernel(wide_ref, h_ref, u0_ref, u1_ref, u2_ref, near_ref, out_ref):
    sums = [jnp.zeros((8, 128), F32)] * 7
    for q in range(4):
        u0, u1, u2 = u0_ref[q], u1_ref[q], u2_ref[q]
        image = data_part(h_ref, wide_ref, q) + RIDGE_TIME * u2
        terms = [u0 * u0, u0 * u1, u0 * u2, u1 * u1, u1 * u2, u2 * u2, u2 * image]
        sums = [a + b for a, b in zip(sums, terms)]
    sub = iota((8, 128), 0)
    high = low = jnp.zeros((8, 128), F32)
    for i in range(7):
        pair = fold_rows(sums[i])
        high = jnp.where(sub == i, pair[0], high)
        low = jnp.where(sub == i, pair[1], low)
    for y in range(8):
        for q in range(4):
            out_ref[y, q] = u2_ref[q]
            out_ref[y, 4 + q] = near_ref[q]
        out_ref[y, 8] = high
        out_ref[y, 9] = low


def moment_kernel(steps_all, parts_ref, weight_ref, lags_ref, out_ref, context_ref):
    for y in range(8):
        for q in range(4):
            context_ref[16 + 4 * y + q] = parts_ref[y, q]
            if y >= 4:
                context_ref[4 * (y - 4) + q] = parts_ref[y, 4 + q]
    first = lax.axis_index("tz") * 4096
    square = jnp.zeros((8, 128), F32)
    for part in range(2):
        errors = residuals(
            lambda j: context_ref[16 + 16 * part + j], 16, first + 2048 * part, steps_all, lags_ref, weight_ref
        )
        for error in errors:
            square = square + error * error
    pair = fold_rows(AR * square)
    last = iota((8, 128), 0) == 6
    packed = pair_tree([(parts_ref[y, 8], parts_ref[y, 9]) for y in range(8)])
    packed = pair_add(packed, (jnp.where(last, pair[0], 0.0), jnp.where(last, pair[1], 0.0)))
    for by in (64, 32, 16, 8, 4, 2, 1):
        packed = pair_add(packed, (pltpu.roll(packed[0], by, axis=1), pltpu.roll(packed[1], by, axis=1)))
    lane = iota((8, 128), 1)
    value = jnp.where(lane < 64, packed[0], packed[1])
    value = jnp.sum(jnp.where(iota((8, 128), 0) == lane % 64 // 8, value, 0.0), axis=0, keepdims=True)
    out_ref[...] = jnp.broadcast_to(value[None], out_ref.shape)


def finish_kernel(parts_ref, theta_ref, x_ref, wide0_ref, wide1_ref, wide2_ref, out_ref):
    half = iota((8, 128), 1) < 64
    pairs = []
    for j in range(8):
        part = parts_ref[8 * j : 8 * j + 8, :]
        other = pltpu.roll(part, 64, axis=1)
        pairs.append((jnp.where(half, part, other), jnp.where(half, other, part)))
    total = pair_tree(pairs)
    for by in (4, 2, 1):
        total = pair_add(total, (pltpu.roll(total[0], by, axis=0), pltpu.roll(total[1], by, axis=0)))

    def moment(i):
        return tuple(jnp.broadcast_to(a[:, 8 * i : 8 * i + 1], (8, 128)) for a in total)

    g00, g01, g02, g11, g12, g22, m22 = [moment(i) for i in range(7)]
    theta = (theta_ref[...], jnp.zeros((8, 128), F32))
    m00 = pair_add(g01, pair_mul(theta, g00))
    m01 = pair_add(g11, pair_mul(theta, g01))
    m02 = pair_add(g12, pair_mul(theta, g02))
    m11 = pair_add(g12, pair_mul(theta, g11))
    m12 = pair_add(g22, pair_mul(theta, g12))
    l10 = pair_div(m01, m00)
    l20 = pair_div(m02, m00)
    d1 = pair_sub(m11, pair_mul(l10, m01))
    n12 = pair_sub(m12, pair_mul(l10, m02))
    y1 = pair_sub(g01, pair_mul(l10, g00))
    l21 = pair_div(n12, d1)
    d2 = pair_sub(pair_sub(m22, pair_mul(l20, m02)), pair_mul(l21, n12))
    y2 = pair_sub(pair_sub(g02, pair_mul(l20, g00)), pair_mul(l21, y1))
    tiny = 1e-12
    c2 = jnp.where(d2[0] > tiny * m22[0], y2[0] / d2[0], 0.0)
    zero = jnp.zeros_like(c2)
    c1 = pair_sub(pair_div(y1, d1), pair_mul(l21, (c2, zero)))
    c1 = jnp.where(d1[0] > tiny * m11[0], c1[0], 0.0)
    c0 = pair_div(g00, m00)
    c0 = pair_sub(c0, pair_mul(l10, (c1, zero)))
    c0 = pair_sub(c0, pair_mul(l20, (c2, zero)))[0]
    for s in range(8):
        for q in range(4):
            at = (slice(8 * s, 8 * s + 8), slice(128 * q, 128 * q + 128))
            step = c0 * wide0_ref[s, q] + c1 * wide1_ref[s, q] + c2 * wide2_ref[s, q]
            out_ref[at] = x_ref[at] + step


def neighbour(plane):
    pairs = [(8 * z + y, 8 * ((z + (1 if y < 4 else -1)) % 8) + y) for z in range(8) for y in range(8)]
    return lax.ppermute(plane, TM, pairs)


def exchange(spread):
    plane = lax.all_to_all(spread, "ty", 0, 0).reshape(32, 8, 128)
    return plane, neighbour(plane), lax.all_to_all(spread, "series", 0, 0)


def per_device(panel, observed, start_time, ar_weight, lags):
    cells = panel.shape[0]
    steps_all = 64 * 512
    cells_all = cells * 8
    series = lax.axis_index("series")
    own_weight = lax.dynamic_slice_in_dim(ar_weight, 8 * series, 8, 0)
    weight = jnp.broadcast_to(own_weight.T[:, :, None], (LAGS, 8, 128))
    theta = RIDGE_TIME + AR * (1.0 + jnp.sum(ar_weight * ar_weight) / 64.0)
    theta = jnp.broadcast_to(theta, (8, 128))
    observed = observed.T
    context = pltpu.VMEM((48, 8, 128), F32)
    errors = pltpu.VMEM((20, 8, 128), F32)

    parts = call(
        front_kernel,
        struct(8, 112, 128),
        (panel, observed, start_time),
        (
            pltpu.VMEM(panel.shape, F32),
            pltpu.VMEM(observed.shape, jnp.int32),
            pltpu.VMEM(start_time.shape, F32),
            pltpu.SemaphoreType.DMA((3,)),
        ),
        HBM,
        60,
    )
    parts = lax.all_to_all(parts, "ty", 0, 0)
    parts, plane = call(middle_kernel, (struct(8, 40, 128), struct(32, 8, 128)), (parts,))
    parts = lax.all_to_all(parts, "tz", 0, 0)
    solved = call(solve_kernel, struct(64, 1, 128), (parts,))
    solved, plane = lax.optimization_barrier((solved, plane))
    near = neighbour(plane)
    gathered = lax.all_to_all(solved, ("ty", "tz"), 0, 0).reshape(64, 128)
    gathered, near = lax.optimization_barrier((gathered, near))
    factors, normal = call(
        functools.partial(normal_kernel, 1.0 / cells_all),
        (struct(cells, 64), struct(64, 768)),
        (gathered, panel, observed),
    )
    sums = lax.all_to_all(normal.reshape(8, 8, 768), "series", 0, 0)
    u0, own0, h = call(
        functools.partial(start_kernel, steps_all),
        (struct(8, 4, 8, 128), struct(4, 8, 128), struct(4, 8, 64)),
        (sums, start_time, plane, near, weight, lags),
        (context, errors),
    )

    def image(plane, near, wide):
        return call(
            functools.partial(image_kernel, steps_all),
            (struct(8, 4, 8, 128), struct(4, 8, 128)),
            (plane, near, wide, h, weight, theta, lags),
            (context, errors),
        )

    plane, near, wide0 = exchange(u0)
    u1, own1 = image(plane, near, wide0)
    plane, near, wide1 = exchange(u1)
    u2, own2 = image(plane, near, wide1)
    near = lax.ppermute(own2, "tz", [(z, (z + 1) % 8) for z in range(8)])
    wide2 = lax.all_to_all(u2, "series", 0, 0)
    parts = call(product_kernel, struct(8, 10, 8, 128), (wide2, h, own0, own1, own2, near))
    parts = lax.all_to_all(parts, "ty", 0, 0)
    moments = call(
        functools.partial(moment_kernel, steps_all), struct(64, 1, 128), (parts, weight, lags), (context,)
    )
    moments = lax.all_to_all(moments, ("series", "tz"), 0, 0).reshape(64, 128)
    result = call(finish_kernel, struct(64, 512), (moments, theta, start_time, wide0, wide1, wide2))
    return (factors, result)


def solution(mesh):
    grid = Mesh(mesh.devices.reshape(8, 8, 8), ("series", "tz", "ty"))
    return jax.shard_map(
        per_device,
        mesh=grid,
        in_specs=(P("series", TM), P("series", TM), P(None, TM), P(), P()),
        out_specs=(P("series", None), P(None, TM)),
        check_vma=False,
    )
```

```python
import functools

import jax
import jax.numpy as jnp
from jax import lax
from jax.experimental import pallas as pl
from jax.experimental.pallas import tpu as pltpu
from jax.sharding import Mesh, PartitionSpec as P

HIGH = lax.Precision.HIGHEST
TILE = 128
LAGS = 14
LONGEST = 2016
RIDGE_FACTOR = 1.0
RIDGE_TIME = 0.05
AR = 0.25
TM = ("tz", "ty")
F32 = jnp.float32
VMEM = pl.BlockSpec(memory_space=pltpu.VMEM)
HBM = pl.BlockSpec(memory_space=pltpu.HBM)
SMEM = pl.BlockSpec(memory_space=pltpu.SMEM)


def struct(*shape):
    return jax.ShapeDtypeStruct(shape, F32)


def iota(shape, dim):
    return lax.broadcasted_iota(jnp.int32, shape, dim)


def call(kernel, outs, ins, scratch=(), place=VMEM, room=32):
    specs = [SMEM if a.dtype == jnp.int32 and a.ndim == 1 else place for a in ins]
    return pl.pallas_call(
        kernel,
        out_shape=outs,
        in_specs=specs,
        out_specs=jax.tree.map(lambda _: VMEM, outs),
        scratch_shapes=list(scratch),
        compiler_params=pltpu.CompilerParams(vmem_limit_bytes=room * 1024 * 1024),
    )(*ins)


def dot(a, b, dims):
    return lax.dot_general(a, b, (dims, ((), ())), precision=HIGH, preferred_element_type=F32)


def columns_of(obs_ref):
    flags = obs_ref[...].astype(F32)
    return jnp.concatenate([flags] * 32, axis=0).T


def front_kernel(panel_hbm, obs_hbm, x_hbm, out_ref, panel_ref, obs_ref, x_ref, sems):
    copies = [
        pltpu.make_async_copy(source, target, sems.at[i])
        for i, (source, target) in enumerate(((x_hbm, x_ref), (obs_hbm, obs_ref), (panel_hbm, panel_ref)))
    ]
    for copy in copies:
        copy.start()
    copies[0].wait()
    x = x_ref[...]
    row = iota((32, 64), 0)
    col = iota((32, 64), 1)
    keep = (col < 32) | (col - 32 >= row)
    diag_at = iota((64, 128), 0) == iota((64, 128), 1) % 64
    lane = iota((8, 128), 1)
    sub = iota((8, 128), 0)
    packs, masked = [], []
    extra = jnp.zeros((8, 128), F32)
    for b in range(4):
        xb = x[:, b * TILE : (b + 1) * TILE]
        gram = dot(xb, xb, ((1,), (1,)))
        moved = jnp.concatenate([gram[0:32, 32:64], gram[0:32, 0:32]], axis=1)
        packs.append(jnp.where(keep, gram[32:64], moved))
        twice = jnp.concatenate([gram, gram], axis=1)
        diag = jnp.sum(jnp.where(diag_at, twice, 0.0), axis=0, keepdims=True)
        extra = jnp.where((sub == b) & (lane % 64 < 32), diag, extra)
    copies[1].wait()
    flags = columns_of(obs_ref)
    copies[2].wait()
    for b in range(4):
        masked.append(panel_ref[:, b * TILE : (b + 1) * TILE] * flags[:, b : b + 1])
    rhs = dot(jnp.concatenate(masked, axis=1), x, ((1,), (1,)))
    mine = pl.ds(pl.multiple_of(8 * lax.axis_index("series"), 8), 8)
    own = [x_ref[mine, q * TILE : (q + 1) * TILE] for q in range(4)]
    pairs = [jnp.concatenate([packs[0], packs[1]], axis=1), jnp.concatenate([packs[2], packs[3]], axis=1)]
    for y in range(8):
        out_ref[y, 0:32, :] = pairs[0]
        out_ref[y, 32:64, :] = pairs[1]
        first, second = slice(16 * y, 16 * y + 8), slice(16 * y + 8, 16 * y + 16)
        out_ref[y, 64:72, :] = jnp.concatenate([rhs[first], rhs[second]], axis=1)
        tail = extra
        for b in range(4):
            tail = jnp.where(lane // 8 == 4 + b, flags[first, b : b + 1], tail)
            tail = jnp.where(lane // 8 == 12 + b, flags[second, b : b + 1], tail)
        out_ref[y, 72:80, :] = tail
        for q in range(4):
            out_ref[y, 80 + 8 * q : 88 + 8 * q, :] = own[q]


def middle_kernel(parts_ref, out_ref, x_ref):
    lane = iota((8, 128), 1)
    sub = iota((8, 128), 0)
    left = lane < 64
    wide_left = iota((32, 128), 1) < 64
    totals = [None] * 8
    diag = jnp.zeros((8, 128), F32)
    rhs = jnp.zeros((8, 128), F32)
    for y in range(8):
        extra = parts_ref[y, 72:80, :]
        rhs = rhs + parts_ref[y, 64:72, :]
        for pair in range(2):
            both = parts_ref[y, 32 * pair : 32 * pair + 32, :]
            other = pltpu.roll(both, 64, axis=1)
            packs = (jnp.where(wide_left, both, other), jnp.where(wide_left, other, both))
            for half in range(2):
                b = 2 * pair + half
                flag = jnp.where(left, extra[:, 32 + 8 * b : 33 + 8 * b], extra[:, 96 + 8 * b : 97 + 8 * b])
                diag = diag + flag * extra[b : b + 1]
                for z in range(8):
                    term = packs[half] * flag[z : z + 1]
                    totals[z] = term if totals[z] is None else totals[z] + term
        for q in range(4):
            x_ref[4 * y + q] = parts_ref[y, 80 + 8 * q : 88 + 8 * q, :]
    for z in range(8):
        out_ref[z, 0:32, :] = totals[z]
        out_ref[z, 32:40, :] = jnp.where(sub == 0, diag[z : z + 1], jnp.where(sub == 1, rhs[z : z + 1], 0.0))


def solve_kernel(parts_ref, out_ref):
    total = parts_ref[0]
    for j in range(1, 8):
        total = total + parts_ref[j]
    pack = total[0:32]
    diag = total[32:33]
    rhs = total[33:34]
    flipped = jnp.concatenate([pack, pack, pack, pack], axis=0).T
    row = iota((32, 128), 0)
    lane = iota((32, 128), 1)
    group = lane // 32
    col = lane % 32
    first = lane < 64
    upper_t = jnp.where(first, flipped[32:64], flipped[96:128])
    cross = jnp.where(first, flipped[0:32], flipped[64:96])
    odd = group % 2 == 1
    top_left = jnp.where(col < row, pltpu.roll(pack, 96, axis=1), jnp.where(col == row, diag, upper_t))
    top = jnp.where(odd, cross, top_left)
    bottom = jnp.where(odd & (col < row), upper_t, pack)
    eye = (iota((64, 128), 0) == iota((64, 128), 1) % 64).astype(F32)
    mat = jnp.concatenate([top, bottom], axis=0) + RIDGE_FACTOR * eye
    blocks = [mat[8 * i : 8 * i + 8] for i in range(8)]
    side = jnp.broadcast_to(rhs, (8, 128))
    half = iota((8, 128), 1) < 64
    within = iota((8, 128), 1) % 64

    def spread(value, k):
        return jnp.where(half, value[:, k : k + 1], value[:, 64 + k : 65 + k])

    for i in range(8):
        columns = [[spread(blocks[m], 8 * i + j) for j in range(8)] for m in range(i, 8)]
        ends = [spread(side, 8 * i + j) for j in range(8)]
        for r in range(8):
            inverse = 1.0 / jnp.broadcast_to(columns[0][r][r : r + 1], (8, 128))
            pivot_row = jnp.broadcast_to(blocks[i][r : r + 1], (8, 128))
            factor = jnp.where(within == 8 * i + r, 1.0 - inverse, pivot_row * inverse)
            factors = [jnp.broadcast_to(columns[0][j][r : r + 1], (8, 128)) * inverse for j in range(r + 1, 8)]
            for m in range(i if r < 7 else i + 1, 8):
                own = columns[m - i]
                blocks[m] = blocks[m] - own[r] * factor
                for j in range(r + 1, 8):
                    own[j] = own[j] - own[r] * factors[j - r - 1]
            side = side - ends[r] * factor
            for j in range(r + 1, 8):
                ends[j] = ends[j] - ends[r] * factors[j - r - 1]
    out_ref[...] = jnp.broadcast_to(side[0:1][None], out_ref.shape)


def normal_kernel(scale, gathered_ref, panel_ref, obs_ref, factors_ref, out_ref):
    pieces = []
    for y in range(8):
        pair = gathered_ref[8 * y : 8 * y + 8, :]
        pieces += [pair[:, 0:64], pair[:, 64:128]]
    factors = jnp.concatenate(pieces, axis=0)
    factors_ref[...] = factors
    flags = columns_of(obs_ref)
    right = [panel_ref[:, b * TILE : (b + 1) * TILE] * flags[:, b : b + 1] for b in range(4)]
    for b in (0, 2):
        right.append(jnp.concatenate([factors * flags[:, b : b + 1], factors * flags[:, b + 1 : b + 2]], axis=1))
    out_ref[...] = scale * dot(factors, jnp.concatenate(right, axis=1), ((0,), (0,)))


def lagged(read, count, lags_ref, weight_ref, ahead):
    lane = iota((8, 128), 1)
    sums = [None] * count
    for index in range(LAGS):
        lag = lags_ref[index]
        if ahead:
            start = lag // 128
            shift = lag % 128
        else:
            back = (lag + 127) // 128
            start = -back
            shift = back * 128 - lag
        cut = 128 - shift
        weight = weight_ref[index]
        own = lane < cut
        turn = jnp.where(cut == 128, 0, cut)
        low = pltpu.roll(read(start), turn, axis=1)
        for j in range(count):
            high = pltpu.roll(read(start + j + 1), turn, axis=1)
            term = weight * jnp.where(own, low, high)
            sums[j] = term if sums[j] is None else sums[j] + term
            low = high
    return sums


def residuals(read, count, first_step, steps_all, lags_ref, weight_ref):
    past = lagged(read, count, lags_ref, weight_ref, False)
    lane = iota((8, 128), 1)
    out = []
    for j in range(count):
        step = first_step + 128 * j + lane
        out.append(jnp.where((step >= LONGEST) & (step < steps_all), read(j) - past[j], 0.0))
    return out


def ar_part(read, first_step, steps_all, lags_ref, weight_ref, errors_ref):
    errors = residuals(read, 20, first_step, steps_all, lags_ref, weight_ref)
    for j in range(20):
        errors_ref[j] = errors[j]
    later = lagged(lambda j: errors_ref[j], 4, lags_ref, weight_ref, True)
    return [errors[j] - later[j] for j in range(4)]


def place():
    y = lax.axis_index("ty")
    return lax.axis_index("tz") * 8 + y, y


def drift_kernel(
    steps_all, plane_ref, near_ref, weight_ref, all_ref, lags_ref, out_ref, theta_ref, context_ref, errors_ref
):
    slab, y = place()
    read = fill_context(plane_ref, near_ref, context_ref, y)
    back = ar_part(read, slab * 512, steps_all, lags_ref, weight_ref, errors_ref)
    for q in range(4):
        out_ref[q] = RIDGE_TIME * read(q) + AR * back[q]
    squares = all_ref[...] * all_ref[...]
    theta_ref[...] = jnp.full((8, 128), RIDGE_TIME + AR) + (AR / 64.0) * jnp.sum(squares)


def start_kernel(sums_ref, x_ref, drift_ref, out_ref, own_ref, h_ref):
    total = sums_ref[0]
    for j in range(1, 8):
        total = total + sums_ref[j]
    for q in range(4):
        h = total[:, 512 + 64 * q : 576 + 64 * q]
        h_ref[q] = h
        image = dot(h, x_ref[:, q * 128 : (q + 1) * 128], ((1,), (0,))) + drift_ref[q]
        value = total[:, q * 128 : (q + 1) * 128] - image
        own_ref[q] = value
        for j in range(8):
            out_ref[j, q] = value


def fill_context(plane_ref, near_ref, context_ref, y):
    lower = y < 4
    at = jnp.where(lower, 16, 0)
    near_at = jnp.where(lower, 0, 32)
    near_from = jnp.where(lower, 16, 0)
    for j in range(32):
        context_ref[at + j] = plane_ref[j]
    for j in range(16):
        context_ref[near_at + j] = near_ref[near_from + j]
    base = at + 4 * y
    return lambda j: context_ref[base + j]


def data_part(h_ref, wide_ref, q):
    return dot(h_ref[q], wide_ref[:, q].reshape(64, 128), ((1,), (0,)))


def image_kernel(
    steps_all, plane_ref, near_ref, wide_ref, h_ref, weight_ref, theta_ref, lags_ref,
    out_ref, own_ref, context_ref, errors_ref,
):
    slab, y = place()
    read = fill_context(plane_ref, near_ref, context_ref, y)
    back = ar_part(read, slab * 512, steps_all, lags_ref, weight_ref, errors_ref)
    theta = theta_ref[...]
    for q in range(4):
        own = read(q)
        value = data_part(h_ref, wide_ref, q) + (RIDGE_TIME - theta) * own + AR * back[q]
        own_ref[q] = value
        for j in range(8):
            out_ref[j, q] = value


def two_sum(a, b):
    s = a + b
    t = s - a
    return s, (a - (s - t)) + (b - t)


def pair_add(a, b):
    s, e = two_sum(a[0], b[0])
    e = e + (a[1] + b[1])
    high = s + e
    return high, e - (high - s)


def split(a):
    c = a * 4097.0
    high = c - (c - a)
    return high, a - high


def pair_mul(a, b):
    p = a[0] * b[0]
    ah, al = split(a[0])
    bh, bl = split(b[0])
    e = ((ah * bh - p) + ah * bl + al * bh) + al * bl
    e = e + (a[0] * b[1] + a[1] * b[0])
    high = p + e
    return high, e - (high - p)


def pair_neg(a):
    return -a[0], -a[1]


def pair_sub(a, b):
    return pair_add(a, pair_neg(b))


def pair_div(a, b):
    first = a[0] / b[0]
    zero = jnp.zeros_like(first)
    rest = pair_sub(a, pair_mul(b, (first, zero)))
    second = rest[0] / b[0]
    return two_sum(first, second)


def pair_tree(values):
    while len(values) > 1:
        values = [
            pair_add(values[i], values[i + 1]) if i + 1 < len(values) else values[i]
            for i in range(0, len(values), 2)
        ]
    return values[0]


def lane_sum(pair):
    high, low = pair
    large = 6144.0 * jnp.max(jnp.abs(high), axis=1, keepdims=True)
    lead = (high + large) - large
    rest = (high - lead) + low
    total = [jnp.broadcast_to(jnp.sum(a, axis=1, keepdims=True), (8, 128)) for a in (lead, rest)]
    return two_sum(*total)


def fold_rows(value):
    pair = (value, jnp.zeros_like(value))
    for by in (4, 2, 1):
        pair = pair_add(pair, (pltpu.roll(pair[0], by, axis=0), pltpu.roll(pair[1], by, axis=0)))
    return pair


def product_kernel(wide_ref, h_ref, u0_ref, u1_ref, u2_ref, near_ref, out_ref):
    sums = [jnp.zeros((8, 128), F32)] * 7
    for q in range(4):
        u0, u1, u2 = u0_ref[q], u1_ref[q], u2_ref[q]
        image = data_part(h_ref, wide_ref, q) + RIDGE_TIME * u2
        terms = [u0 * u0, u0 * u1, u0 * u2, u1 * u1, u1 * u2, u2 * u2, u2 * image]
        sums = [a + b for a, b in zip(sums, terms)]
    sub = iota((8, 128), 0)
    high = low = jnp.zeros((8, 128), F32)
    for i in range(7):
        pair = fold_rows(sums[i])
        high = jnp.where(sub == i, pair[0], high)
        low = jnp.where(sub == i, pair[1], low)
    for y in range(8):
        for q in range(4):
            out_ref[y, q] = u2_ref[q]
            out_ref[y, 4 + q] = near_ref[q]
        out_ref[y, 8] = high
        out_ref[y, 9] = low


def moment_kernel(steps_all, parts_ref, weight_ref, lags_ref, out_ref, context_ref):
    for y in range(8):
        for q in range(4):
            context_ref[16 + 4 * y + q] = parts_ref[y, q]
            if y >= 4:
                context_ref[4 * (y - 4) + q] = parts_ref[y, 4 + q]
    first = lax.axis_index("tz") * 4096
    square = jnp.zeros((8, 128), F32)
    for part in range(2):
        errors = residuals(
            lambda j: context_ref[16 + 16 * part + j], 16, first + 2048 * part, steps_all, lags_ref, weight_ref
        )
        for error in errors:
            square = square + error * error
    pair = fold_rows(AR * square)
    last = iota((8, 128), 0) == 6
    packed = pair_tree([(parts_ref[y, 8], parts_ref[y, 9]) for y in range(8)])
    packed = pair_add(packed, (jnp.where(last, pair[0], 0.0), jnp.where(last, pair[1], 0.0)))
    packed = lane_sum(packed)
    lane = iota((8, 128), 1)
    value = jnp.where(lane < 64, packed[0], packed[1])
    value = jnp.sum(jnp.where(iota((8, 128), 0) == lane % 64 // 8, value, 0.0), axis=0, keepdims=True)
    out_ref[...] = jnp.broadcast_to(value[None], out_ref.shape)


def finish_kernel(parts_ref, theta_ref, x_ref, wide0_ref, wide1_ref, wide2_ref, out_ref):
    half = iota((8, 128), 1) < 64
    pairs = []
    for j in range(8):
        part = parts_ref[8 * j : 8 * j + 8, :]
        other = pltpu.roll(part, 64, axis=1)
        pairs.append((jnp.where(half, part, other), jnp.where(half, other, part)))
    total = pair_tree(pairs)
    for by in (4, 2, 1):
        total = pair_add(total, (pltpu.roll(total[0], by, axis=0), pltpu.roll(total[1], by, axis=0)))

    def moment(i):
        return tuple(jnp.broadcast_to(a[:, 8 * i : 8 * i + 1], (8, 128)) for a in total)

    g00, g01, g02, g11, g12, g22, m22 = [moment(i) for i in range(7)]
    theta = (theta_ref[...], jnp.zeros((8, 128), F32))
    m00 = pair_add(g01, pair_mul(theta, g00))
    m01 = pair_add(g11, pair_mul(theta, g01))
    m02 = pair_add(g12, pair_mul(theta, g02))
    m11 = pair_add(g12, pair_mul(theta, g11))
    m12 = pair_add(g22, pair_mul(theta, g12))
    l10 = pair_div(m01, m00)
    l20 = pair_div(m02, m00)
    d1 = pair_sub(m11, pair_mul(l10, m01))
    n12 = pair_sub(m12, pair_mul(l10, m02))
    y1 = pair_sub(g01, pair_mul(l10, g00))
    l21 = pair_div(n12, d1)
    d2 = pair_sub(pair_sub(m22, pair_mul(l20, m02)), pair_mul(l21, n12))
    y2 = pair_sub(pair_sub(g02, pair_mul(l20, g00)), pair_mul(l21, y1))
    tiny = 1e-12
    c2 = jnp.where(d2[0] > tiny * m22[0], y2[0] / d2[0], 0.0)
    zero = jnp.zeros_like(c2)
    c1 = pair_sub(pair_div(y1, d1), pair_mul(l21, (c2, zero)))
    c1 = jnp.where(d1[0] > tiny * m11[0], c1[0], 0.0)
    c0 = pair_div(g00, m00)
    c0 = pair_sub(c0, pair_mul(l10, (c1, zero)))
    c0 = pair_sub(c0, pair_mul(l20, (c2, zero)))[0]
    for s in range(8):
        for q in range(4):
            at = (slice(8 * s, 8 * s + 8), slice(128 * q, 128 * q + 128))
            step = c0 * wide0_ref[s, q] + c1 * wide1_ref[s, q] + c2 * wide2_ref[s, q]
            out_ref[at] = x_ref[at] + step


def neighbour(plane):
    pairs = [(8 * z + y, 8 * ((z + (1 if y < 4 else -1)) % 8) + y) for z in range(8) for y in range(8)]
    return lax.ppermute(plane, TM, pairs)


def exchange(spread):
    plane = lax.all_to_all(spread, "ty", 0, 0).reshape(32, 8, 128)
    return plane, neighbour(plane), lax.all_to_all(spread, "series", 0, 0)


def per_device(panel, observed, start_time, ar_weight, lags):
    cells = panel.shape[0]
    steps_all = 64 * 512
    cells_all = cells * 8
    series = lax.axis_index("series")
    own_weight = lax.dynamic_slice_in_dim(ar_weight, 8 * series, 8, 0)
    weight = jnp.broadcast_to(own_weight.T[:, :, None], (LAGS, 8, 128))
    observed = observed.T
    context = pltpu.VMEM((48, 8, 128), F32)
    errors = pltpu.VMEM((20, 8, 128), F32)

    parts = call(
        front_kernel,
        struct(8, 112, 128),
        (panel, observed, start_time),
        (
            pltpu.VMEM(panel.shape, F32),
            pltpu.VMEM(observed.shape, jnp.int32),
            pltpu.VMEM(start_time.shape, F32),
            pltpu.SemaphoreType.DMA((3,)),
        ),
        HBM,
        60,
    )
    parts = lax.all_to_all(parts, "ty", 0, 0)
    parts, plane = call(middle_kernel, (struct(8, 40, 128), struct(32, 8, 128)), (parts,))
    parts = lax.all_to_all(parts, "tz", 0, 0)
    solved = call(solve_kernel, struct(64, 1, 128), (parts,))
    solved, plane = lax.optimization_barrier((solved, plane))
    near = neighbour(plane)
    gathered = lax.all_to_all(solved, ("ty", "tz"), 0, 0).reshape(64, 128)
    gathered, near = lax.optimization_barrier((gathered, near))
    gathered, near = lax.optimization_barrier((gathered, near))
    factors, normal = call(
        functools.partial(normal_kernel, 1.0 / cells_all),
        (struct(cells, 64), struct(64, 768)),
        (gathered, panel, observed),
    )
    sums = lax.all_to_all(normal.reshape(8, 8, 768), "series", 0, 0)
    drift, theta = call(
        functools.partial(drift_kernel, steps_all),
        (struct(4, 8, 128), struct(8, 128)),
        (plane, near, weight, ar_weight, lags),
        (context, errors),
    )
    u0, own0, h = call(
        start_kernel,
        (struct(8, 4, 8, 128), struct(4, 8, 128), struct(4, 8, 64)),
        (sums, start_time, drift),
    )

    def image(plane, near, wide):
        return call(
            functools.partial(image_kernel, steps_all),
            (struct(8, 4, 8, 128), struct(4, 8, 128)),
            (plane, near, wide, h, weight, theta, lags),
            (context, errors),
        )

    plane, near, wide0 = exchange(u0)
    u1, own1 = image(plane, near, wide0)
    plane, near, wide1 = exchange(u1)
    u2, own2 = image(plane, near, wide1)
    near = lax.ppermute(own2, "tz", [(z, (z + 1) % 8) for z in range(8)])
    wide2 = lax.all_to_all(u2, "series", 0, 0)
    parts = call(product_kernel, struct(8, 10, 8, 128), (wide2, h, own0, own1, own2, near))
    parts = lax.all_to_all(parts, "ty", 0, 0)
    moments = call(
        functools.partial(moment_kernel, steps_all), struct(64, 1, 128), (parts, weight, lags), (context,)
    )
    moments = lax.all_to_all(moments, ("series", "tz"), 0, 0).reshape(64, 128)
    result = call(finish_kernel, struct(64, 512), (moments, theta, start_time, wide0, wide1, wide2))
    return (factors, result)


def solution(mesh):
    grid = Mesh(mesh.devices.reshape(8, 8, 8), ("series", "tz", "ty"))
    return jax.shard_map(
        per_device,
        mesh=grid,
        in_specs=(P("series", TM), P("series", TM), P(None, TM), P(), P()),
        out_specs=(P("series", None), P(None, TM)),
        check_vma=False,
    )
```

```python
import functools

import jax
import jax.numpy as jnp
from jax import lax
from jax.experimental import pallas as pl
from jax.experimental.pallas import tpu as pltpu
from jax.sharding import Mesh, PartitionSpec as P

HIGH = lax.Precision.HIGHEST
TILE = 128
LAGS = 14
LONGEST = 2016
RIDGE_FACTOR = 1.0
RIDGE_TIME = 0.05
AR = 0.25
TM = ("tz", "ty")
F32 = jnp.float32
VMEM = pl.BlockSpec(memory_space=pltpu.VMEM)
HBM = pl.BlockSpec(memory_space=pltpu.HBM)
SMEM = pl.BlockSpec(memory_space=pltpu.SMEM)


def struct(*shape):
    return jax.ShapeDtypeStruct(shape, F32)


def iota(shape, dim):
    return lax.broadcasted_iota(jnp.int32, shape, dim)


def call(kernel, outs, ins, scratch=(), place=VMEM, room=32):
    specs = [SMEM if a.dtype == jnp.int32 and a.ndim == 1 else place for a in ins]
    return pl.pallas_call(
        kernel,
        out_shape=outs,
        in_specs=specs,
        out_specs=jax.tree.map(lambda _: VMEM, outs),
        scratch_shapes=list(scratch),
        compiler_params=pltpu.CompilerParams(vmem_limit_bytes=room * 1024 * 1024),
    )(*ins)


def dot(a, b, dims):
    return lax.dot_general(a, b, (dims, ((), ())), precision=HIGH, preferred_element_type=F32)


def columns_of(obs_ref):
    flags = obs_ref[...].astype(F32)
    return jnp.concatenate([flags] * 32, axis=0).T


def front_kernel(panel_hbm, obs_hbm, x_hbm, out_ref, panel_ref, obs_ref, x_ref, sems):
    copies = [
        pltpu.make_async_copy(source, target, sems.at[i])
        for i, (source, target) in enumerate(((x_hbm, x_ref), (obs_hbm, obs_ref), (panel_hbm, panel_ref)))
    ]
    for copy in copies:
        copy.start()
    copies[0].wait()
    x = x_ref[...]
    row = iota((32, 64), 0)
    col = iota((32, 64), 1)
    keep = (col < 32) | (col - 32 >= row)
    diag_at = iota((64, 128), 0) == iota((64, 128), 1) % 64
    lane = iota((8, 128), 1)
    sub = iota((8, 128), 0)
    packs, masked = [], []
    extra = jnp.zeros((8, 128), F32)
    for b in range(4):
        xb = x[:, b * TILE : (b + 1) * TILE]
        gram = dot(xb, xb, ((1,), (1,)))
        moved = jnp.concatenate([gram[0:32, 32:64], gram[0:32, 0:32]], axis=1)
        packs.append(jnp.where(keep, gram[32:64], moved))
        twice = jnp.concatenate([gram, gram], axis=1)
        diag = jnp.sum(jnp.where(diag_at, twice, 0.0), axis=0, keepdims=True)
        extra = jnp.where((sub == b) & (lane % 64 < 32), diag, extra)
    copies[1].wait()
    flags = columns_of(obs_ref)
    copies[2].wait()
    for b in range(4):
        masked.append(panel_ref[:, b * TILE : (b + 1) * TILE] * flags[:, b : b + 1])
    rhs = dot(jnp.concatenate(masked, axis=1), x, ((1,), (1,)))
    mine = pl.ds(pl.multiple_of(8 * lax.axis_index("series"), 8), 8)
    own = [x_ref[mine, q * TILE : (q + 1) * TILE] for q in range(4)]
    pairs = [jnp.concatenate([packs[0], packs[1]], axis=1), jnp.concatenate([packs[2], packs[3]], axis=1)]
    for y in range(8):
        out_ref[y, 0:32, :] = pairs[0]
        out_ref[y, 32:64, :] = pairs[1]
        first, second = slice(16 * y, 16 * y + 8), slice(16 * y + 8, 16 * y + 16)
        out_ref[y, 64:72, :] = jnp.concatenate([rhs[first], rhs[second]], axis=1)
        tail = extra
        for b in range(4):
            tail = jnp.where(lane // 8 == 4 + b, flags[first, b : b + 1], tail)
            tail = jnp.where(lane // 8 == 12 + b, flags[second, b : b + 1], tail)
        out_ref[y, 72:80, :] = tail
        for q in range(4):
            out_ref[y, 80 + 8 * q : 88 + 8 * q, :] = own[q]


def middle_kernel(parts_ref, out_ref, x_ref):
    lane = iota((8, 128), 1)
    sub = iota((8, 128), 0)
    left = lane < 64
    wide_left = iota((32, 128), 1) < 64
    totals = [None] * 8
    diag = jnp.zeros((8, 128), F32)
    rhs = jnp.zeros((8, 128), F32)
    for y in range(8):
        extra = parts_ref[y, 72:80, :]
        rhs = rhs + parts_ref[y, 64:72, :]
        for pair in range(2):
            both = parts_ref[y, 32 * pair : 32 * pair + 32, :]
            other = pltpu.roll(both, 64, axis=1)
            packs = (jnp.where(wide_left, both, other), jnp.where(wide_left, other, both))
            for half in range(2):
                b = 2 * pair + half
                flag = jnp.where(left, extra[:, 32 + 8 * b : 33 + 8 * b], extra[:, 96 + 8 * b : 97 + 8 * b])
                diag = diag + flag * extra[b : b + 1]
                for z in range(8):
                    term = packs[half] * flag[z : z + 1]
                    totals[z] = term if totals[z] is None else totals[z] + term
        for q in range(4):
            x_ref[4 * y + q] = parts_ref[y, 80 + 8 * q : 88 + 8 * q, :]
    for z in range(8):
        out_ref[z, 0:32, :] = totals[z]
        out_ref[z, 32:40, :] = jnp.where(sub == 0, diag[z : z + 1], jnp.where(sub == 1, rhs[z : z + 1], 0.0))


def solve_kernel(parts_ref, out_ref):
    total = parts_ref[0]
    for j in range(1, 8):
        total = total + parts_ref[j]
    pack = total[0:32]
    diag = total[32:33]
    rhs = total[33:34]
    flipped = jnp.concatenate([pack, pack, pack, pack], axis=0).T
    row = iota((32, 128), 0)
    lane = iota((32, 128), 1)
    group = lane // 32
    col = lane % 32
    first = lane < 64
    upper_t = jnp.where(first, flipped[32:64], flipped[96:128])
    cross = jnp.where(first, flipped[0:32], flipped[64:96])
    odd = group % 2 == 1
    top_left = jnp.where(col < row, pltpu.roll(pack, 96, axis=1), jnp.where(col == row, diag, upper_t))
    top = jnp.where(odd, cross, top_left)
    bottom = jnp.where(odd & (col < row), upper_t, pack)
    eye = (iota((64, 128), 0) == iota((64, 128), 1) % 64).astype(F32)
    mat = jnp.concatenate([top, bottom], axis=0) + RIDGE_FACTOR * eye
    blocks = [mat[8 * i : 8 * i + 8] for i in range(8)]
    side = jnp.broadcast_to(rhs, (8, 128))
    half = iota((8, 128), 1) < 64
    within = iota((8, 128), 1) % 64

    def spread(value, k):
        return jnp.where(half, value[:, k : k + 1], value[:, 64 + k : 65 + k])

    for i in range(8):
        columns = [[spread(blocks[m], 8 * i + j) for j in range(8)] for m in range(i, 8)]
        ends = [spread(side, 8 * i + j) for j in range(8)]
        for r in range(8):
            inverse = 1.0 / jnp.broadcast_to(columns[0][r][r : r + 1], (8, 128))
            pivot_row = jnp.broadcast_to(blocks[i][r : r + 1], (8, 128))
            factor = jnp.where(within == 8 * i + r, 1.0 - inverse, pivot_row * inverse)
            factors = [jnp.broadcast_to(columns[0][j][r : r + 1], (8, 128)) * inverse for j in range(r + 1, 8)]
            for m in range(i if r < 7 else i + 1, 8):
                own = columns[m - i]
                blocks[m] = blocks[m] - own[r] * factor
                for j in range(r + 1, 8):
                    own[j] = own[j] - own[r] * factors[j - r - 1]
            side = side - ends[r] * factor
            for j in range(r + 1, 8):
                ends[j] = ends[j] - ends[r] * factors[j - r - 1]
    out_ref[...] = jnp.broadcast_to(side[0:1][None], out_ref.shape)


def normal_kernel(scale, gathered_ref, panel_ref, obs_ref, factors_ref, out_ref):
    pieces = []
    for y in range(8):
        pair = gathered_ref[8 * y : 8 * y + 8, :]
        pieces += [pair[:, 0:64], pair[:, 64:128]]
    factors = jnp.concatenate(pieces, axis=0)
    factors_ref[...] = factors
    flags = columns_of(obs_ref)
    right = [panel_ref[:, b * TILE : (b + 1) * TILE] * flags[:, b : b + 1] for b in range(4)]
    for b in (0, 2):
        right.append(jnp.concatenate([factors * flags[:, b : b + 1], factors * flags[:, b + 1 : b + 2]], axis=1))
    right.append(factors)
    product = scale * dot(factors, jnp.concatenate(right, axis=1), ((0,), (0,)))
    out_ref[:, 0:768] = product[:, 0:768]
    gram = product[:, 768:832]
    norm = jnp.sum(gram * gram)
    trace = jnp.sum(jnp.where(iota((64, 64), 0) == iota((64, 64), 1), gram, 0.0))
    some = jnp.full((64, 128), trace)
    out_ref[:, 768:896] = jnp.where(some > 0.0, norm / jnp.where(some > 0.0, some, 1.0), 0.0)


def lagged(read, count, lags_ref, weight_ref, ahead):
    lane = iota((8, 128), 1)
    sums = [None] * count
    for index in range(LAGS):
        lag = lags_ref[index]
        if ahead:
            start = lag // 128
            shift = lag % 128
        else:
            back = (lag + 127) // 128
            start = -back
            shift = back * 128 - lag
        cut = 128 - shift
        weight = weight_ref[index]
        own = lane < cut
        turn = jnp.where(cut == 128, 0, cut)
        low = pltpu.roll(read(start), turn, axis=1)
        for j in range(count):
            high = pltpu.roll(read(start + j + 1), turn, axis=1)
            term = weight * jnp.where(own, low, high)
            sums[j] = term if sums[j] is None else sums[j] + term
            low = high
    return sums


def residuals(read, count, first_step, steps_all, lags_ref, weight_ref):
    past = lagged(read, count, lags_ref, weight_ref, False)
    lane = iota((8, 128), 1)
    out = []
    for j in range(count):
        step = first_step + 128 * j + lane
        out.append(jnp.where((step >= LONGEST) & (step < steps_all), read(j) - past[j], 0.0))
    return out


def ar_part(read, first_step, steps_all, lags_ref, weight_ref, errors_ref):
    errors = residuals(read, 20, first_step, steps_all, lags_ref, weight_ref)
    for j in range(20):
        errors_ref[j] = errors[j]
    later = lagged(lambda j: errors_ref[j], 4, lags_ref, weight_ref, True)
    return [errors[j] - later[j] for j in range(4)]


def place():
    y = lax.axis_index("ty")
    return lax.axis_index("tz") * 8 + y, y


def drift_kernel(
    steps_all, plane_ref, near_ref, weight_ref, all_ref, lags_ref, out_ref, theta_ref, context_ref, errors_ref
):
    slab, y = place()
    read = fill_context(plane_ref, near_ref, context_ref, y)
    back = ar_part(read, slab * 512, steps_all, lags_ref, weight_ref, errors_ref)
    for q in range(4):
        out_ref[q] = RIDGE_TIME * read(q) + AR * back[q]
    squares = all_ref[...] * all_ref[...]
    theta_ref[...] = jnp.full((8, 128), RIDGE_TIME + AR) + (AR / 64.0) * jnp.sum(squares)


def start_kernel(sums_ref, x_ref, drift_ref, theta_ref, out_ref, own_ref, h_ref, first_ref):
    total = sums_ref[0]
    for j in range(1, 8):
        total = total + sums_ref[j]
    first_ref[...] = theta_ref[...] + total[:, 768:896]
    for q in range(4):
        h = total[:, 512 + 64 * q : 576 + 64 * q]
        h_ref[q] = h
        image = dot(h, x_ref[:, q * 128 : (q + 1) * 128], ((1,), (0,))) + drift_ref[q]
        value = total[:, q * 128 : (q + 1) * 128] - image
        own_ref[q] = value
        for j in range(8):
            out_ref[j, q] = value


def fill_context(plane_ref, near_ref, context_ref, y):
    lower = y < 4
    at = jnp.where(lower, 16, 0)
    near_at = jnp.where(lower, 0, 32)
    near_from = jnp.where(lower, 16, 0)
    for j in range(32):
        context_ref[at + j] = plane_ref[j]
    for j in range(16):
        context_ref[near_at + j] = near_ref[near_from + j]
    base = at + 4 * y
    return lambda j: context_ref[base + j]


def data_part(h_ref, wide_ref, q):
    return dot(h_ref[q], wide_ref[:, q].reshape(64, 128), ((1,), (0,)))


def image_kernel(
    steps_all, plane_ref, near_ref, wide_ref, h_ref, weight_ref, theta_ref, lags_ref,
    out_ref, own_ref, context_ref, errors_ref,
):
    slab, y = place()
    read = fill_context(plane_ref, near_ref, context_ref, y)
    back = ar_part(read, slab * 512, steps_all, lags_ref, weight_ref, errors_ref)
    theta = theta_ref[...]
    for q in range(4):
        own = read(q)
        value = data_part(h_ref, wide_ref, q) + (RIDGE_TIME - theta) * own + AR * back[q]
        own_ref[q] = value
        for j in range(8):
            out_ref[j, q] = value


def two_sum(a, b):
    s = a + b
    t = s - a
    return s, (a - (s - t)) + (b - t)


def pair_add(a, b):
    s, e = two_sum(a[0], b[0])
    e = e + (a[1] + b[1])
    high = s + e
    return high, e - (high - s)


def split(a):
    c = a * 4097.0
    high = c - (c - a)
    return high, a - high


def pair_mul(a, b):
    p = a[0] * b[0]
    ah, al = split(a[0])
    bh, bl = split(b[0])
    e = ((ah * bh - p) + ah * bl + al * bh) + al * bl
    e = e + (a[0] * b[1] + a[1] * b[0])
    high = p + e
    return high, e - (high - p)


def pair_neg(a):
    return -a[0], -a[1]


def pair_sub(a, b):
    return pair_add(a, pair_neg(b))


def pair_div(a, b):
    first = a[0] / b[0]
    zero = jnp.zeros_like(first)
    rest = pair_sub(a, pair_mul(b, (first, zero)))
    second = rest[0] / b[0]
    return two_sum(first, second)


def pair_tree(values):
    while len(values) > 1:
        values = [
            pair_add(values[i], values[i + 1]) if i + 1 < len(values) else values[i]
            for i in range(0, len(values), 2)
        ]
    return values[0]


def lane_sum(pair):
    high, low = pair
    large = 6144.0 * jnp.max(jnp.abs(high), axis=1, keepdims=True)
    lead = (high + large) - large
    rest = (high - lead) + low
    total = [jnp.broadcast_to(jnp.sum(a, axis=1, keepdims=True), (8, 128)) for a in (lead, rest)]
    return two_sum(*total)


def fold_rows(value):
    pair = (value, jnp.zeros_like(value))
    for by in (4, 2, 1):
        pair = pair_add(pair, (pltpu.roll(pair[0], by, axis=0), pltpu.roll(pair[1], by, axis=0)))
    return pair


def product_kernel(wide_ref, h_ref, u0_ref, u1_ref, u2_ref, near_ref, out_ref):
    sums = [jnp.zeros((8, 128), F32)] * 7
    for q in range(4):
        u0, u1, u2 = u0_ref[q], u1_ref[q], u2_ref[q]
        image = data_part(h_ref, wide_ref, q) + RIDGE_TIME * u2
        terms = [u0 * u0, u0 * u1, u0 * u2, u1 * u1, u1 * u2, u2 * u2, u2 * image]
        sums = [a + b for a, b in zip(sums, terms)]
    sub = iota((8, 128), 0)
    high = low = jnp.zeros((8, 128), F32)
    for i in range(7):
        pair = fold_rows(sums[i])
        high = jnp.where(sub == i, pair[0], high)
        low = jnp.where(sub == i, pair[1], low)
    for y in range(8):
        for q in range(4):
            out_ref[y, q] = u2_ref[q]
            out_ref[y, 4 + q] = near_ref[q]
        out_ref[y, 8] = high
        out_ref[y, 9] = low


def moment_kernel(steps_all, parts_ref, weight_ref, lags_ref, out_ref, context_ref):
    for y in range(8):
        for q in range(4):
            context_ref[16 + 4 * y + q] = parts_ref[y, q]
            if y >= 4:
                context_ref[4 * (y - 4) + q] = parts_ref[y, 4 + q]
    first = lax.axis_index("tz") * 4096
    square = jnp.zeros((8, 128), F32)
    for part in range(2):
        errors = residuals(
            lambda j: context_ref[16 + 16 * part + j], 16, first + 2048 * part, steps_all, lags_ref, weight_ref
        )
        for error in errors:
            square = square + error * error
    pair = fold_rows(AR * square)
    last = iota((8, 128), 0) == 6
    packed = pair_tree([(parts_ref[y, 8], parts_ref[y, 9]) for y in range(8)])
    packed = pair_add(packed, (jnp.where(last, pair[0], 0.0), jnp.where(last, pair[1], 0.0)))
    packed = lane_sum(packed)
    lane = iota((8, 128), 1)
    value = jnp.where(lane < 64, packed[0], packed[1])
    value = jnp.sum(jnp.where(iota((8, 128), 0) == lane % 64 // 8, value, 0.0), axis=0, keepdims=True)
    out_ref[...] = jnp.broadcast_to(value[None], out_ref.shape)


def finish_kernel(parts_ref, first_ref, theta_ref, x_ref, wide0_ref, wide1_ref, wide2_ref, out_ref):
    half = iota((8, 128), 1) < 64
    pairs = []
    for j in range(8):
        part = parts_ref[8 * j : 8 * j + 8, :]
        other = pltpu.roll(part, 64, axis=1)
        pairs.append((jnp.where(half, part, other), jnp.where(half, other, part)))
    total = pair_tree(pairs)
    for by in (4, 2, 1):
        total = pair_add(total, (pltpu.roll(total[0], by, axis=0), pltpu.roll(total[1], by, axis=0)))

    def moment(i):
        return tuple(jnp.broadcast_to(a[:, 8 * i : 8 * i + 1], (8, 128)) for a in total)

    g00, g01, g02, g11, g12, g22, m22 = [moment(i) for i in range(7)]
    theta = (theta_ref[...], jnp.zeros((8, 128), F32))
    first = (first_ref[...], jnp.zeros((8, 128), F32))
    m00 = pair_add(g01, pair_mul(first, g00))
    m01 = pair_add(g11, pair_mul(first, g01))
    m02 = pair_add(g12, pair_mul(first, g02))
    m11 = pair_add(g12, pair_mul(theta, g11))
    m12 = pair_add(g22, pair_mul(theta, g12))
    l10 = pair_div(m01, m00)
    l20 = pair_div(m02, m00)
    d1 = pair_sub(m11, pair_mul(l10, m01))
    n12 = pair_sub(m12, pair_mul(l10, m02))
    y1 = pair_sub(g01, pair_mul(l10, g00))
    l21 = pair_div(n12, d1)
    d2 = pair_sub(pair_sub(m22, pair_mul(l20, m02)), pair_mul(l21, n12))
    y2 = pair_sub(pair_sub(g02, pair_mul(l20, g00)), pair_mul(l21, y1))
    tiny = 1e-12
    c2 = jnp.where(d2[0] > tiny * m22[0], y2[0] / d2[0], 0.0)
    zero = jnp.zeros_like(c2)
    c1 = pair_sub(pair_div(y1, d1), pair_mul(l21, (c2, zero)))
    c1 = jnp.where(d1[0] > tiny * m11[0], c1[0], 0.0)
    c0 = pair_div(g00, m00)
    c0 = pair_sub(c0, pair_mul(l10, (c1, zero)))
    c0 = pair_sub(c0, pair_mul(l20, (c2, zero)))[0]
    for s in range(8):
        for q in range(4):
            at = (slice(8 * s, 8 * s + 8), slice(128 * q, 128 * q + 128))
            step = c0 * wide0_ref[s, q] + c1 * wide1_ref[s, q] + c2 * wide2_ref[s, q]
            out_ref[at] = x_ref[at] + step


def neighbour(plane):
    pairs = [(8 * z + y, 8 * ((z + (1 if y < 4 else -1)) % 8) + y) for z in range(8) for y in range(8)]
    return lax.ppermute(plane, TM, pairs)


def exchange(spread):
    plane = lax.all_to_all(spread, "ty", 0, 0).reshape(32, 8, 128)
    return plane, neighbour(plane), lax.all_to_all(spread, "series", 0, 0)


def per_device(panel, observed, start_time, ar_weight, lags):
    cells = panel.shape[0]
    steps_all = 64 * 512
    cells_all = cells * 8
    series = lax.axis_index("series")
    own_weight = lax.dynamic_slice_in_dim(ar_weight, 8 * series, 8, 0)
    weight = jnp.broadcast_to(own_weight.T[:, :, None], (LAGS, 8, 128))
    observed = observed.T
    context = pltpu.VMEM((48, 8, 128), F32)
    errors = pltpu.VMEM((20, 8, 128), F32)

    parts = call(
        front_kernel,
        struct(8, 112, 128),
        (panel, observed, start_time),
        (
            pltpu.VMEM(panel.shape, F32),
            pltpu.VMEM(observed.shape, jnp.int32),
            pltpu.VMEM(start_time.shape, F32),
            pltpu.SemaphoreType.DMA((3,)),
        ),
        HBM,
        60,
    )
    parts = lax.all_to_all(parts, "ty", 0, 0)
    parts, plane = call(middle_kernel, (struct(8, 40, 128), struct(32, 8, 128)), (parts,))
    parts = lax.all_to_all(parts, "tz", 0, 0)
    solved = call(solve_kernel, struct(64, 1, 128), (parts,))
    solved, plane = lax.optimization_barrier((solved, plane))
    near = neighbour(plane)
    gathered = lax.all_to_all(solved, ("ty", "tz"), 0, 0).reshape(64, 128)
    gathered, near = lax.optimization_barrier((gathered, near))
    gathered, near = lax.optimization_barrier((gathered, near))
    factors, normal = call(
        functools.partial(normal_kernel, 1.0 / cells_all),
        (struct(cells, 64), struct(64, 896)),
        (gathered, panel, observed),
    )
    sums = lax.all_to_all(normal.reshape(8, 8, 896), "series", 0, 0)
    drift, theta = call(
        functools.partial(drift_kernel, steps_all),
        (struct(4, 8, 128), struct(8, 128)),
        (plane, near, weight, ar_weight, lags),
        (context, errors),
    )
    u0, own0, h, first = call(
        start_kernel,
        (struct(8, 4, 8, 128), struct(4, 8, 128), struct(4, 8, 64), struct(8, 128)),
        (sums, start_time, drift, theta),
    )

    def image(plane, near, wide, shift):
        return call(
            functools.partial(image_kernel, steps_all),
            (struct(8, 4, 8, 128), struct(4, 8, 128)),
            (plane, near, wide, h, weight, shift, lags),
            (context, errors),
        )

    plane, near, wide0 = exchange(u0)
    u1, own1 = image(plane, near, wide0, first)
    plane, near, wide1 = exchange(u1)
    u2, own2 = image(plane, near, wide1, theta)
    near = lax.ppermute(own2, "tz", [(z, (z + 1) % 8) for z in range(8)])
    wide2 = lax.all_to_all(u2, "series", 0, 0)
    parts = call(product_kernel, struct(8, 10, 8, 128), (wide2, h, own0, own1, own2, near))
    parts = lax.all_to_all(parts, "ty", 0, 0)
    moments = call(
        functools.partial(moment_kernel, steps_all), struct(64, 1, 128), (parts, weight, lags), (context,)
    )
    moments = lax.all_to_all(moments, ("series", "tz"), 0, 0).reshape(64, 128)
    result = call(finish_kernel, struct(64, 512), (moments, first, theta, start_time, wide0, wide1, wide2))
    return (factors, result)


def solution(mesh):
    grid = Mesh(mesh.devices.reshape(8, 8, 8), ("series", "tz", "ty"))
    return jax.shard_map(
        per_device,
        mesh=grid,
        in_specs=(P("series", TM), P("series", TM), P(None, TM), P(), P()),
        out_specs=(P("series", None), P(None, TM)),
        check_vma=False,
    )
```

```python
import functools

import jax
import jax.numpy as jnp
from jax import lax
from jax.experimental import pallas as pl
from jax.experimental.pallas import tpu as pltpu
from jax.sharding import Mesh, PartitionSpec as P

HIGH = lax.Precision.HIGHEST
TILE = 128
LAGS = 14
LONGEST = 2016
RIDGE_FACTOR = 1.0
RIDGE_TIME = 0.05
AR = 0.25
TM = ("tz", "ty")
F32 = jnp.float32
VMEM = pl.BlockSpec(memory_space=pltpu.VMEM)
HBM = pl.BlockSpec(memory_space=pltpu.HBM)
SMEM = pl.BlockSpec(memory_space=pltpu.SMEM)


def struct(*shape):
    return jax.ShapeDtypeStruct(shape, F32)


def iota(shape, dim):
    return lax.broadcasted_iota(jnp.int32, shape, dim)


def call(kernel, outs, ins, scratch=(), place=VMEM, room=32):
    specs = [SMEM if a.dtype == jnp.int32 and a.ndim == 1 else place for a in ins]
    return pl.pallas_call(
        kernel,
        out_shape=outs,
        in_specs=specs,
        out_specs=jax.tree.map(lambda _: VMEM, outs),
        scratch_shapes=list(scratch),
        compiler_params=pltpu.CompilerParams(vmem_limit_bytes=room * 1024 * 1024),
    )(*ins)


def dot(a, b, dims):
    return lax.dot_general(a, b, (dims, ((), ())), precision=HIGH, preferred_element_type=F32)


def columns_of(obs_ref):
    flags = obs_ref[...].astype(F32)
    return jnp.concatenate([flags] * 32, axis=0).T


def front_kernel(panel_hbm, obs_hbm, x_hbm, out_ref, panel_ref, obs_ref, x_ref, sems):
    copies = [
        pltpu.make_async_copy(source, target, sems.at[i])
        for i, (source, target) in enumerate(((x_hbm, x_ref), (obs_hbm, obs_ref), (panel_hbm, panel_ref)))
    ]
    for copy in copies:
        copy.start()
    copies[0].wait()
    x = x_ref[...]
    row = iota((32, 64), 0)
    col = iota((32, 64), 1)
    keep = (col < 32) | (col - 32 >= row)
    diag_at = iota((64, 128), 0) == iota((64, 128), 1) % 64
    lane = iota((8, 128), 1)
    sub = iota((8, 128), 0)
    packs, masked = [], []
    extra = jnp.zeros((8, 128), F32)
    for b in range(4):
        xb = x[:, b * TILE : (b + 1) * TILE]
        gram = dot(xb, xb, ((1,), (1,)))
        moved = jnp.concatenate([gram[0:32, 32:64], gram[0:32, 0:32]], axis=1)
        packs.append(jnp.where(keep, gram[32:64], moved))
        twice = jnp.concatenate([gram, gram], axis=1)
        diag = jnp.sum(jnp.where(diag_at, twice, 0.0), axis=0, keepdims=True)
        extra = jnp.where((sub == b) & (lane % 64 < 32), diag, extra)
    copies[1].wait()
    flags = columns_of(obs_ref)
    copies[2].wait()
    for b in range(4):
        masked.append(panel_ref[:, b * TILE : (b + 1) * TILE] * flags[:, b : b + 1])
    rhs = dot(jnp.concatenate(masked, axis=1), x, ((1,), (1,)))
    mine = pl.ds(pl.multiple_of(8 * lax.axis_index("series"), 8), 8)
    own = [x_ref[mine, q * TILE : (q + 1) * TILE] for q in range(4)]
    pairs = [jnp.concatenate([packs[0], packs[1]], axis=1), jnp.concatenate([packs[2], packs[3]], axis=1)]
    for y in range(8):
        out_ref[y, 0:32, :] = pairs[0]
        out_ref[y, 32:64, :] = pairs[1]
        first, second = slice(16 * y, 16 * y + 8), slice(16 * y + 8, 16 * y + 16)
        out_ref[y, 64:72, :] = jnp.concatenate([rhs[first], rhs[second]], axis=1)
        tail = extra
        for b in range(4):
            tail = jnp.where(lane // 8 == 4 + b, flags[first, b : b + 1], tail)
            tail = jnp.where(lane // 8 == 12 + b, flags[second, b : b + 1], tail)
        out_ref[y, 72:80, :] = tail
        for q in range(4):
            out_ref[y, 80 + 8 * q : 88 + 8 * q, :] = own[q]


def middle_kernel(parts_ref, out_ref, x_ref):
    lane = iota((8, 128), 1)
    sub = iota((8, 128), 0)
    left = lane < 64
    wide_left = iota((32, 128), 1) < 64
    totals = [None] * 8
    diag = jnp.zeros((8, 128), F32)
    rhs = jnp.zeros((8, 128), F32)
    for y in range(8):
        extra = parts_ref[y, 72:80, :]
        rhs = rhs + parts_ref[y, 64:72, :]
        for pair in range(2):
            both = parts_ref[y, 32 * pair : 32 * pair + 32, :]
            other = pltpu.roll(both, 64, axis=1)
            packs = (jnp.where(wide_left, both, other), jnp.where(wide_left, other, both))
            for half in range(2):
                b = 2 * pair + half
                flag = jnp.where(left, extra[:, 32 + 8 * b : 33 + 8 * b], extra[:, 96 + 8 * b : 97 + 8 * b])
                diag = diag + flag * extra[b : b + 1]
                for z in range(8):
                    term = packs[half] * flag[z : z + 1]
                    totals[z] = term if totals[z] is None else totals[z] + term
        for q in range(4):
            x_ref[4 * y + q] = parts_ref[y, 80 + 8 * q : 88 + 8 * q, :]
    for z in range(8):
        out_ref[z, 0:32, :] = totals[z]
        out_ref[z, 32:40, :] = jnp.where(sub == 0, diag[z : z + 1], jnp.where(sub == 1, rhs[z : z + 1], 0.0))


def solve_kernel(parts_ref, out_ref):
    total = parts_ref[0]
    for j in range(1, 8):
        total = total + parts_ref[j]
    pack = total[0:32]
    diag = total[32:33]
    rhs = total[33:34]
    flipped = jnp.concatenate([pack, pack, pack, pack], axis=0).T
    row = iota((32, 128), 0)
    lane = iota((32, 128), 1)
    group = lane // 32
    col = lane % 32
    first = lane < 64
    upper_t = jnp.where(first, flipped[32:64], flipped[96:128])
    cross = jnp.where(first, flipped[0:32], flipped[64:96])
    odd = group % 2 == 1
    top_left = jnp.where(col < row, pltpu.roll(pack, 96, axis=1), jnp.where(col == row, diag, upper_t))
    top = jnp.where(odd, cross, top_left)
    bottom = jnp.where(odd & (col < row), upper_t, pack)
    eye = (iota((64, 128), 0) == iota((64, 128), 1) % 64).astype(F32)
    mat = jnp.concatenate([top, bottom], axis=0) + RIDGE_FACTOR * eye
    blocks = [mat[8 * i : 8 * i + 8] for i in range(8)]
    side = jnp.broadcast_to(rhs, (8, 128))
    half = iota((8, 128), 1) < 64
    within = iota((8, 128), 1) % 64

    def spread(value, k):
        return jnp.where(half, value[:, k : k + 1], value[:, 64 + k : 65 + k])

    for i in range(8):
        columns = [[spread(blocks[m], 8 * i + j) for j in range(8)] for m in range(i, 8)]
        ends = [spread(side, 8 * i + j) for j in range(8)]
        for r in range(8):
            inverse = 1.0 / jnp.broadcast_to(columns[0][r][r : r + 1], (8, 128))
            pivot_row = jnp.broadcast_to(blocks[i][r : r + 1], (8, 128))
            factor = jnp.where(within == 8 * i + r, 1.0 - inverse, pivot_row * inverse)
            factors = [jnp.broadcast_to(columns[0][j][r : r + 1], (8, 128)) * inverse for j in range(r + 1, 8)]
            for m in range(i if r < 7 else i + 1, 8):
                own = columns[m - i]
                blocks[m] = blocks[m] - own[r] * factor
                for j in range(r + 1, 8):
                    own[j] = own[j] - own[r] * factors[j - r - 1]
            side = side - ends[r] * factor
            for j in range(r + 1, 8):
                ends[j] = ends[j] - ends[r] * factors[j - r - 1]
    out_ref[...] = jnp.broadcast_to(side[0:1][None], out_ref.shape)


def normal_kernel(scale, gathered_ref, panel_ref, obs_ref, factors_ref, out_ref):
    pieces = []
    for y in range(8):
        pair = gathered_ref[8 * y : 8 * y + 8, :]
        pieces += [pair[:, 0:64], pair[:, 64:128]]
    factors = jnp.concatenate(pieces, axis=0)
    factors_ref[...] = factors
    flags = columns_of(obs_ref)
    right = [panel_ref[:, b * TILE : (b + 1) * TILE] * flags[:, b : b + 1] for b in range(4)]
    for b in (0, 2):
        right.append(jnp.concatenate([factors * flags[:, b : b + 1], factors * flags[:, b + 1 : b + 2]], axis=1))
    right.append(factors)
    product = scale * dot(factors, jnp.concatenate(right, axis=1), ((0,), (0,)))
    out_ref[:, 0:768] = product[:, 0:768]
    gram = product[:, 768:832]
    norm = jnp.sum(gram * gram)
    trace = jnp.sum(jnp.where(iota((64, 64), 0) == iota((64, 64), 1), gram, 0.0))
    some = jnp.full((64, 128), trace)
    out_ref[:, 768:896] = jnp.where(some > 0.0, norm / jnp.where(some > 0.0, some, 1.0), 0.0)


def lagged(read, chunks, lags_ref, weight_ref, ahead):
    lane = iota((8, 128), 1)
    sums = {}
    for index in range(LAGS):
        lag = lags_ref[index]
        if ahead:
            start = lag // 128
            shift = lag % 128
        else:
            back = (lag + 127) // 128
            start = -back
            shift = back * 128 - lag
        cut = 128 - shift
        weight = weight_ref[index]
        own = lane < cut
        turn = jnp.where(cut == 128, 0, cut)
        for first, last in chunks:
            low = pltpu.roll(read(start + first), turn, axis=1)
            for j in range(first, last):
                high = pltpu.roll(read(start + j + 1), turn, axis=1)
                term = weight * jnp.where(own, low, high)
                sums[j] = sums[j] + term if j in sums else term
                low = high
    return sums


def residuals(read, chunks, first_step, steps_all, lags_ref, weight_ref):
    past = lagged(read, chunks, lags_ref, weight_ref, False)
    lane = iota((8, 128), 1)
    out = {}
    for j, value in past.items():
        step = first_step + 128 * j + lane
        out[j] = jnp.where((step >= LONGEST) & (step < steps_all), read(j) - value, 0.0)
    return out


def ar_part(read, first_step, steps_all, lags_ref, weight_ref, errors_ref):
    errors = residuals(read, ((0, 8), (15, 20)), first_step, steps_all, lags_ref, weight_ref)
    for j, value in errors.items():
        errors_ref[j] = value
    later = lagged(lambda j: errors_ref[j], ((0, 4),), lags_ref, weight_ref, True)
    return [errors[j] - later[j] for j in range(4)]


def place():
    y = lax.axis_index("ty")
    return lax.axis_index("tz") * 8 + y, y


def drift_kernel(
    steps_all, plane_ref, near_ref, weight_ref, all_ref, lags_ref, out_ref, theta_ref, context_ref, errors_ref
):
    slab, y = place()
    read = fill_context(plane_ref, near_ref, context_ref, y)
    back = ar_part(read, slab * 512, steps_all, lags_ref, weight_ref, errors_ref)
    for q in range(4):
        out_ref[q] = RIDGE_TIME * read(q) + AR * back[q]
    squares = all_ref[...] * all_ref[...]
    theta_ref[...] = jnp.full((8, 128), RIDGE_TIME + AR) + (AR / 64.0) * jnp.sum(squares)


def start_kernel(sums_ref, x_ref, drift_ref, theta_ref, out_ref, own_ref, h_ref, first_ref):
    total = sums_ref[0]
    for j in range(1, 8):
        total = total + sums_ref[j]
    first_ref[...] = theta_ref[...] + total[:, 768:896]
    for q in range(4):
        h = total[:, 512 + 64 * q : 576 + 64 * q]
        h_ref[q] = h
        image = dot(h, x_ref[:, q * 128 : (q + 1) * 128], ((1,), (0,))) + drift_ref[q]
        value = total[:, q * 128 : (q + 1) * 128] - image
        own_ref[q] = value
        for j in range(8):
            out_ref[j, q] = value


def fill_context(plane_ref, near_ref, context_ref, y):
    lower = y < 4
    at = jnp.where(lower, 16, 0)
    near_at = jnp.where(lower, 0, 32)
    near_from = jnp.where(lower, 16, 0)
    for j in range(32):
        context_ref[at + j] = plane_ref[j]
    for j in range(16):
        context_ref[near_at + j] = near_ref[near_from + j]
    base = at + 4 * y
    return lambda j: context_ref[base + j]


def data_part(h_ref, wide_ref, q):
    return dot(h_ref[q], wide_ref[:, q].reshape(64, 128), ((1,), (0,)))


def image_kernel(
    steps_all, plane_ref, near_ref, wide_ref, h_ref, weight_ref, theta_ref, lags_ref,
    out_ref, own_ref, context_ref, errors_ref,
):
    slab, y = place()
    read = fill_context(plane_ref, near_ref, context_ref, y)
    back = ar_part(read, slab * 512, steps_all, lags_ref, weight_ref, errors_ref)
    theta = theta_ref[...]
    for q in range(4):
        own = read(q)
        value = data_part(h_ref, wide_ref, q) + (RIDGE_TIME - theta) * own + AR * back[q]
        own_ref[q] = value
        for j in range(8):
            out_ref[j, q] = value


def two_sum(a, b):
    s = a + b
    t = s - a
    return s, (a - (s - t)) + (b - t)


def pair_add(a, b):
    s, e = two_sum(a[0], b[0])
    e = e + (a[1] + b[1])
    high = s + e
    return high, e - (high - s)


def split(a):
    c = a * 4097.0
    high = c - (c - a)
    return high, a - high


def pair_mul(a, b):
    p = a[0] * b[0]
    ah, al = split(a[0])
    bh, bl = split(b[0])
    e = ((ah * bh - p) + ah * bl + al * bh) + al * bl
    e = e + (a[0] * b[1] + a[1] * b[0])
    high = p + e
    return high, e - (high - p)


def pair_neg(a):
    return -a[0], -a[1]


def pair_sub(a, b):
    return pair_add(a, pair_neg(b))


def pair_div(a, b):
    first = a[0] / b[0]
    zero = jnp.zeros_like(first)
    rest = pair_sub(a, pair_mul(b, (first, zero)))
    second = rest[0] / b[0]
    return two_sum(first, second)


def pair_tree(values):
    while len(values) > 1:
        values = [
            pair_add(values[i], values[i + 1]) if i + 1 < len(values) else values[i]
            for i in range(0, len(values), 2)
        ]
    return values[0]


def lane_sum(pair):
    high, low = pair
    large = 6144.0 * jnp.max(jnp.abs(high), axis=1, keepdims=True)
    lead = (high + large) - large
    rest = (high - lead) + low
    total = [jnp.broadcast_to(jnp.sum(a, axis=1, keepdims=True), (8, 128)) for a in (lead, rest)]
    return two_sum(*total)


def fold_rows(value):
    pair = (value, jnp.zeros_like(value))
    for by in (4, 2, 1):
        pair = pair_add(pair, (pltpu.roll(pair[0], by, axis=0), pltpu.roll(pair[1], by, axis=0)))
    return pair


def product_kernel(wide_ref, h_ref, u0_ref, u1_ref, u2_ref, near_ref, out_ref):
    sums = [jnp.zeros((8, 128), F32)] * 7
    for q in range(4):
        u0, u1, u2 = u0_ref[q], u1_ref[q], u2_ref[q]
        image = data_part(h_ref, wide_ref, q) + RIDGE_TIME * u2
        terms = [u0 * u0, u0 * u1, u0 * u2, u1 * u1, u1 * u2, u2 * u2, u2 * image]
        sums = [a + b for a, b in zip(sums, terms)]
    sub = iota((8, 128), 0)
    high = low = jnp.zeros((8, 128), F32)
    for i in range(7):
        pair = fold_rows(sums[i])
        high = jnp.where(sub == i, pair[0], high)
        low = jnp.where(sub == i, pair[1], low)
    high, low = pair_add((high, low), (pltpu.roll(high, 64, axis=1), pltpu.roll(low, 64, axis=1)))
    value = jnp.where(iota((8, 128), 1) < 64, high, low)
    for y in range(8):
        for q in range(4):
            out_ref[y, q] = u2_ref[q]
            out_ref[y, 4 + q] = near_ref[q]
        out_ref[y, 8] = value


def moment_kernel(steps_all, parts_ref, weight_ref, lags_ref, out_ref, context_ref):
    for y in range(8):
        for q in range(4):
            context_ref[16 + 4 * y + q] = parts_ref[y, q]
            if y >= 4:
                context_ref[4 * (y - 4) + q] = parts_ref[y, 4 + q]
    first = lax.axis_index("tz") * 4096
    square = jnp.zeros((8, 128), F32)
    for part in range(2):
        errors = residuals(
            lambda j: context_ref[16 + 16 * part + j], ((0, 16),), first + 2048 * part, steps_all, lags_ref, weight_ref
        )
        for error in errors.values():
            square = square + error * error
    pair = fold_rows(AR * square)
    last = iota((8, 128), 0) == 6
    half = iota((8, 128), 1) < 64
    packed = pair_tree([
        (jnp.where(half, value, 0.0), jnp.where(half, pltpu.roll(value, 64, axis=1), 0.0))
        for value in (parts_ref[y, 8] for y in range(8))
    ])
    packed = pair_add(packed, (jnp.where(last, pair[0], 0.0), jnp.where(last, pair[1], 0.0)))
    packed = lane_sum(packed)
    lane = iota((8, 128), 1)
    value = jnp.where(lane < 64, packed[0], packed[1])
    value = jnp.sum(jnp.where(iota((8, 128), 0) == lane % 64 // 8, value, 0.0), axis=0, keepdims=True)
    out_ref[...] = jnp.broadcast_to(value[None], out_ref.shape)


def finish_kernel(parts_ref, first_ref, theta_ref, x_ref, wide0_ref, wide1_ref, wide2_ref, out_ref):
    half = iota((8, 128), 1) < 64
    pairs = []
    for j in range(8):
        part = parts_ref[8 * j : 8 * j + 8, :]
        other = pltpu.roll(part, 64, axis=1)
        pairs.append((jnp.where(half, part, other), jnp.where(half, other, part)))
    total = pair_tree(pairs)
    for by in (4, 2, 1):
        total = pair_add(total, (pltpu.roll(total[0], by, axis=0), pltpu.roll(total[1], by, axis=0)))

    def moment(i):
        return tuple(jnp.broadcast_to(a[:, 8 * i : 8 * i + 1], (8, 128)) for a in total)

    g00, g01, g02, g11, g12, g22, m22 = [moment(i) for i in range(7)]
    theta = (theta_ref[...], jnp.zeros((8, 128), F32))
    first = (first_ref[...], jnp.zeros((8, 128), F32))
    m00 = pair_add(g01, pair_mul(first, g00))
    m01 = pair_add(g11, pair_mul(first, g01))
    m02 = pair_add(g12, pair_mul(first, g02))
    m11 = pair_add(g12, pair_mul(theta, g11))
    m12 = pair_add(g22, pair_mul(theta, g12))
    l10 = pair_div(m01, m00)
    l20 = pair_div(m02, m00)
    d1 = pair_sub(m11, pair_mul(l10, m01))
    n12 = pair_sub(m12, pair_mul(l10, m02))
    y1 = pair_sub(g01, pair_mul(l10, g00))
    l21 = pair_div(n12, d1)
    d2 = pair_sub(pair_sub(m22, pair_mul(l20, m02)), pair_mul(l21, n12))
    y2 = pair_sub(pair_sub(g02, pair_mul(l20, g00)), pair_mul(l21, y1))
    tiny = 1e-12
    c2 = jnp.where(d2[0] > tiny * m22[0], y2[0] / d2[0], 0.0)
    zero = jnp.zeros_like(c2)
    c1 = pair_sub(pair_div(y1, d1), pair_mul(l21, (c2, zero)))
    c1 = jnp.where(d1[0] > tiny * m11[0], c1[0], 0.0)
    c0 = pair_div(g00, m00)
    c0 = pair_sub(c0, pair_mul(l10, (c1, zero)))
    c0 = pair_sub(c0, pair_mul(l20, (c2, zero)))[0]
    for s in range(8):
        for q in range(4):
            at = (slice(8 * s, 8 * s + 8), slice(128 * q, 128 * q + 128))
            step = c0 * wide0_ref[s, q] + c1 * wide1_ref[s, q] + c2 * wide2_ref[s, q]
            out_ref[at] = x_ref[at] + step


def neighbour(plane):
    pairs = [(8 * z + y, 8 * ((z + (1 if y < 4 else -1)) % 8) + y) for z in range(8) for y in range(8)]
    return lax.ppermute(plane, TM, pairs)


def exchange(spread):
    plane = lax.all_to_all(spread, "ty", 0, 0).reshape(32, 8, 128)
    return plane, neighbour(plane), lax.all_to_all(spread, "series", 0, 0)


def per_device(panel, observed, start_time, ar_weight, lags):
    cells = panel.shape[0]
    steps_all = 64 * 512
    cells_all = cells * 8
    series = lax.axis_index("series")
    own_weight = lax.dynamic_slice_in_dim(ar_weight, 8 * series, 8, 0)
    weight = jnp.broadcast_to(own_weight.T[:, :, None], (LAGS, 8, 128))
    observed = observed.T
    context = pltpu.VMEM((48, 8, 128), F32)
    errors = pltpu.VMEM((20, 8, 128), F32)

    parts = call(
        front_kernel,
        struct(8, 112, 128),
        (panel, observed, start_time),
        (
            pltpu.VMEM(panel.shape, F32),
            pltpu.VMEM(observed.shape, jnp.int32),
            pltpu.VMEM(start_time.shape, F32),
            pltpu.SemaphoreType.DMA((3,)),
        ),
        HBM,
        60,
    )
    parts = lax.all_to_all(parts, "ty", 0, 0)
    parts, plane = call(middle_kernel, (struct(8, 40, 128), struct(32, 8, 128)), (parts,))
    parts = lax.all_to_all(parts, "tz", 0, 0)
    solved = call(solve_kernel, struct(64, 1, 128), (parts,))
    solved, plane = lax.optimization_barrier((solved, plane))
    near = neighbour(plane)
    gathered = lax.all_to_all(solved, ("ty", "tz"), 0, 0).reshape(64, 128)
    gathered, near = lax.optimization_barrier((gathered, near))
    factors, normal = call(
        functools.partial(normal_kernel, 1.0 / cells_all),
        (struct(cells, 64), struct(64, 896)),
        (gathered, panel, observed),
    )
    sums = lax.all_to_all(normal.reshape(8, 8, 896), "series", 0, 0)
    drift, theta = call(
        functools.partial(drift_kernel, steps_all),
        (struct(4, 8, 128), struct(8, 128)),
        (plane, near, weight, ar_weight, lags),
        (context, errors),
    )
    u0, own0, h, first = call(
        start_kernel,
        (struct(8, 4, 8, 128), struct(4, 8, 128), struct(4, 8, 64), struct(8, 128)),
        (sums, start_time, drift, theta),
    )

    def image(plane, near, wide, shift):
        return call(
            functools.partial(image_kernel, steps_all),
            (struct(8, 4, 8, 128), struct(4, 8, 128)),
            (plane, near, wide, h, weight, shift, lags),
            (context, errors),
        )

    plane, near, wide0 = exchange(u0)
    u1, own1 = image(plane, near, wide0, first)
    plane, near, wide1 = exchange(u1)
    u2, own2 = image(plane, near, wide1, theta)
    near = lax.ppermute(own2, "tz", [(z, (z + 1) % 8) for z in range(8)])
    wide2 = lax.all_to_all(u2, "series", 0, 0)
    parts = call(product_kernel, struct(8, 9, 8, 128), (wide2, h, own0, own1, own2, near))
    parts = lax.all_to_all(parts, "ty", 0, 0)
    moments = call(
        functools.partial(moment_kernel, steps_all), struct(64, 1, 128), (parts, weight, lags), (context,)
    )
    moments = lax.all_to_all(moments, ("series", "tz"), 0, 0).reshape(64, 128)
    result = call(finish_kernel, struct(64, 512), (moments, first, theta, start_time, wide0, wide1, wide2))
    return (factors, result)


def solution(mesh):
    grid = Mesh(mesh.devices.reshape(8, 8, 8), ("series", "tz", "ty"))
    return jax.shard_map(
        per_device,
        mesh=grid,
        in_specs=(P("series", TM), P("series", TM), P(None, TM), P(), P()),
        out_specs=(P("series", None), P(None, TM)),
        check_vma=False,
    )
```

```python
import functools

import jax
import jax.numpy as jnp
from jax import lax
from jax.experimental import pallas as pl
from jax.experimental.pallas import tpu as pltpu
from jax.sharding import Mesh, PartitionSpec as P

HIGH = lax.Precision.HIGHEST
TILE = 128
LAGS = 14
LONGEST = 2016
RIDGE_FACTOR = 1.0
RIDGE_TIME = 0.05
AR = 0.25
TM = ("tz", "ty")
F32 = jnp.float32
VMEM = pl.BlockSpec(memory_space=pltpu.VMEM)
HBM = pl.BlockSpec(memory_space=pltpu.HBM)


def struct(*shape):
    return jax.ShapeDtypeStruct(shape, F32)


def iota(shape, dim):
    return lax.broadcasted_iota(jnp.int32, shape, dim)


def call(kernel, outs, ins, scratch=(), place=VMEM, room=32):
    return pl.pallas_call(
        kernel,
        out_shape=outs,
        in_specs=[place] * len(ins),
        out_specs=jax.tree.map(lambda _: VMEM, outs),
        scratch_shapes=list(scratch),
        compiler_params=pltpu.CompilerParams(vmem_limit_bytes=room * 1024 * 1024),
    )(*ins)


def dot(a, b, dims):
    return lax.dot_general(a, b, (dims, ((), ())), precision=HIGH, preferred_element_type=F32)


def columns_of(obs_ref):
    flags = obs_ref[...].astype(F32)
    return jnp.concatenate([flags] * 32, axis=0).T


def front_kernel(panel_hbm, obs_hbm, x_hbm, out_ref, panel_ref, obs_ref, x_ref, sems):
    copies = [
        pltpu.make_async_copy(source, target, sems.at[i])
        for i, (source, target) in enumerate(((x_hbm, x_ref), (obs_hbm, obs_ref), (panel_hbm, panel_ref)))
    ]
    for copy in copies:
        copy.start()
    copies[0].wait()
    x = x_ref[...]
    row = iota((32, 64), 0)
    col = iota((32, 64), 1)
    keep = (col < 32) | (col - 32 >= row)
    diag_at = iota((64, 128), 0) == iota((64, 128), 1) % 64
    lane = iota((8, 128), 1)
    sub = iota((8, 128), 0)
    packs, masked = [], []
    extra = jnp.zeros((8, 128), F32)
    for b in range(4):
        xb = x[:, b * TILE : (b + 1) * TILE]
        gram = dot(xb, xb, ((1,), (1,)))
        moved = jnp.concatenate([gram[0:32, 32:64], gram[0:32, 0:32]], axis=1)
        packs.append(jnp.where(keep, gram[32:64], moved))
        twice = jnp.concatenate([gram, gram], axis=1)
        diag = jnp.sum(jnp.where(diag_at, twice, 0.0), axis=0, keepdims=True)
        extra = jnp.where((sub == b) & (lane % 64 < 32), diag, extra)
    copies[1].wait()
    flags = columns_of(obs_ref)
    copies[2].wait()
    for b in range(4):
        masked.append(panel_ref[:, b * TILE : (b + 1) * TILE] * flags[:, b : b + 1])
    rhs = dot(jnp.concatenate(masked, axis=1), x, ((1,), (1,)))
    mine = pl.ds(pl.multiple_of(8 * lax.axis_index("series"), 8), 8)
    own = [x_ref[mine, q * TILE : (q + 1) * TILE] for q in range(4)]
    pairs = [jnp.concatenate([packs[0], packs[1]], axis=1), jnp.concatenate([packs[2], packs[3]], axis=1)]
    for y in range(8):
        out_ref[y, 0:32, :] = pairs[0]
        out_ref[y, 32:64, :] = pairs[1]
        first, second = slice(16 * y, 16 * y + 8), slice(16 * y + 8, 16 * y + 16)
        out_ref[y, 64:72, :] = jnp.concatenate([rhs[first], rhs[second]], axis=1)
        tail = extra
        for b in range(4):
            tail = jnp.where(lane // 8 == 4 + b, flags[first, b : b + 1], tail)
            tail = jnp.where(lane // 8 == 12 + b, flags[second, b : b + 1], tail)
        out_ref[y, 72:80, :] = tail
        for q in range(4):
            out_ref[y, 80 + 8 * q : 88 + 8 * q, :] = own[q]


def middle_kernel(parts_ref, out_ref, x_ref):
    lane = iota((8, 128), 1)
    sub = iota((8, 128), 0)
    left = lane < 64
    wide_left = iota((32, 128), 1) < 64
    totals = [None] * 8
    diag = jnp.zeros((8, 128), F32)
    rhs = jnp.zeros((8, 128), F32)
    for y in range(8):
        extra = parts_ref[y, 72:80, :]
        rhs = rhs + parts_ref[y, 64:72, :]
        for pair in range(2):
            both = parts_ref[y, 32 * pair : 32 * pair + 32, :]
            other = pltpu.roll(both, 64, axis=1)
            packs = (jnp.where(wide_left, both, other), jnp.where(wide_left, other, both))
            for half in range(2):
                b = 2 * pair + half
                flag = jnp.where(left, extra[:, 32 + 8 * b : 33 + 8 * b], extra[:, 96 + 8 * b : 97 + 8 * b])
                diag = diag + flag * extra[b : b + 1]
                for z in range(8):
                    term = packs[half] * flag[z : z + 1]
                    totals[z] = term if totals[z] is None else totals[z] + term
        for q in range(4):
            x_ref[4 * y + q] = parts_ref[y, 80 + 8 * q : 88 + 8 * q, :]
    for z in range(8):
        out_ref[z, 0:32, :] = totals[z]
        out_ref[z, 32:40, :] = jnp.where(sub == 0, diag[z : z + 1], jnp.where(sub == 1, rhs[z : z + 1], 0.0))


def solve_kernel(parts_ref, out_ref):
    total = parts_ref[0]
    for j in range(1, 8):
        total = total + parts_ref[j]
    pack = total[0:32]
    diag = total[32:33]
    rhs = total[33:34]
    flipped = jnp.concatenate([pack, pack, pack, pack], axis=0).T
    row = iota((32, 128), 0)
    lane = iota((32, 128), 1)
    group = lane // 32
    col = lane % 32
    first = lane < 64
    upper_t = jnp.where(first, flipped[32:64], flipped[96:128])
    cross = jnp.where(first, flipped[0:32], flipped[64:96])
    odd = group % 2 == 1
    top_left = jnp.where(col < row, pltpu.roll(pack, 96, axis=1), jnp.where(col == row, diag, upper_t))
    top = jnp.where(odd, cross, top_left)
    bottom = jnp.where(odd & (col < row), upper_t, pack)
    eye = (iota((64, 128), 0) == iota((64, 128), 1) % 64).astype(F32)
    mat = jnp.concatenate([top, bottom], axis=0) + RIDGE_FACTOR * eye
    blocks = [mat[8 * i : 8 * i + 8] for i in range(8)]
    side = jnp.broadcast_to(rhs, (8, 128))
    half = iota((8, 128), 1) < 64
    within = iota((8, 128), 1) % 64

    def spread(value, k):
        return jnp.where(half, value[:, k : k + 1], value[:, 64 + k : 65 + k])

    for i in range(8):
        columns = [[spread(blocks[m], 8 * i + j) for j in range(8)] for m in range(i, 8)]
        ends = [spread(side, 8 * i + j) for j in range(8)]
        for r in range(8):
            inverse = 1.0 / jnp.broadcast_to(columns[0][r][r : r + 1], (8, 128))
            pivot_row = jnp.broadcast_to(blocks[i][r : r + 1], (8, 128))
            factor = jnp.where(within == 8 * i + r, 1.0 - inverse, pivot_row * inverse)
            factors = [jnp.broadcast_to(columns[0][j][r : r + 1], (8, 128)) * inverse for j in range(r + 1, 8)]
            for m in range(i if r < 7 else i + 1, 8):
                own = columns[m - i]
                blocks[m] = blocks[m] - own[r] * factor
                for j in range(r + 1, 8):
                    own[j] = own[j] - own[r] * factors[j - r - 1]
            side = side - ends[r] * factor
            for j in range(r + 1, 8):
                ends[j] = ends[j] - ends[r] * factors[j - r - 1]
    out_ref[...] = jnp.broadcast_to(side[0:1][None], out_ref.shape)


def normal_kernel(scale, gathered_ref, panel_ref, obs_ref, factors_ref, out_ref):
    pieces = []
    for y in range(8):
        pair = gathered_ref[8 * y : 8 * y + 8, :]
        pieces += [pair[:, 0:64], pair[:, 64:128]]
    factors = jnp.concatenate(pieces, axis=0)
    turned = factors.T
    factors_ref[...] = turned
    flags = columns_of(obs_ref)
    right = [panel_ref[:, b * TILE : (b + 1) * TILE] * flags[:, b : b + 1] for b in range(4)]
    for b in (0, 2):
        right.append(jnp.concatenate([factors * flags[:, b : b + 1], factors * flags[:, b + 1 : b + 2]], axis=1))
    right.append(factors)
    product = scale * dot(turned, jnp.concatenate(right, axis=1), ((1,), (0,)))
    out_ref[:, 0:768] = product[:, 0:768]
    gram = product[:, 768:832]
    norm = jnp.sum(gram * gram)
    trace = jnp.sum(jnp.where(iota((64, 64), 0) == iota((64, 64), 1), gram, 0.0))
    some = jnp.full((64, 128), trace)
    out_ref[:, 768:896] = jnp.where(some > 0.0, norm / jnp.where(some > 0.0, some, 1.0), 0.0)


def scalars(lags_ref):
    return [jnp.max(lags_ref[index : index + 1, :]) for index in range(LAGS)]


def lagged(read, chunks, lags, weight_ref, ahead):
    lane = iota((8, 128), 1)
    sums = {}
    for index in range(LAGS):
        lag = lags[index]
        if ahead:
            start = lag // 128
            shift = lag % 128
        else:
            back = (lag + 127) // 128
            start = -back
            shift = back * 128 - lag
        cut = 128 - shift
        weight = weight_ref[index]
        own = lane < cut
        turn = jnp.where(cut == 128, 0, cut)
        for first, last in chunks:
            low = pltpu.roll(read(start + first), turn, axis=1)
            for j in range(first, last):
                high = pltpu.roll(read(start + j + 1), turn, axis=1)
                term = weight * jnp.where(own, low, high)
                sums[j] = sums[j] + term if j in sums else term
                low = high
    return sums


def residuals(read, chunks, first_step, steps_all, lags, weight_ref):
    past = lagged(read, chunks, lags, weight_ref, False)
    lane = iota((8, 128), 1)
    out = {}
    for j, value in past.items():
        step = first_step + 128 * j + lane
        out[j] = jnp.where((step >= LONGEST) & (step < steps_all), read(j) - value, 0.0)
    return out


def ar_part(read, first_step, steps_all, lags, weight_ref, errors_ref):
    errors = residuals(read, ((0, 8), (15, 20)), first_step, steps_all, lags, weight_ref)
    for j, value in errors.items():
        errors_ref[j] = value
    later = lagged(lambda j: errors_ref[j], ((0, 4),), lags, weight_ref, True)
    return [errors[j] - later[j] for j in range(4)]


def place():
    y = lax.axis_index("ty")
    return lax.axis_index("tz") * 8 + y, y


def drift_kernel(
    steps_all, plane_ref, near_ref, weight_ref, all_ref, lags_ref, out_ref, theta_ref, context_ref, errors_ref
):
    lags = scalars(lags_ref)
    slab, y = place()
    read = fill_context(plane_ref, near_ref, context_ref, y)
    back = ar_part(read, slab * 512, steps_all, lags, weight_ref, errors_ref)
    for q in range(4):
        out_ref[q] = RIDGE_TIME * read(q) + AR * back[q]
    squares = all_ref[...] * all_ref[...]
    theta_ref[...] = jnp.full((8, 128), RIDGE_TIME + AR) + (AR / 64.0) * jnp.sum(squares)


def start_kernel(sums_ref, x_ref, drift_ref, theta_ref, out_ref, own_ref, h_ref, first_ref):
    total = sums_ref[0]
    for j in range(1, 8):
        total = total + sums_ref[j]
    first_ref[...] = theta_ref[...] + total[:, 768:896]
    for q in range(4):
        h = total[:, 512 + 64 * q : 576 + 64 * q]
        h_ref[q] = h
        image = dot(h, x_ref[:, q * 128 : (q + 1) * 128], ((1,), (0,))) + drift_ref[q]
        value = total[:, q * 128 : (q + 1) * 128] - image
        own_ref[q] = value
        for j in range(8):
            out_ref[j, q] = value


def fill_context(plane_ref, near_ref, context_ref, y):
    lower = y < 4
    at = jnp.where(lower, 16, 0)
    near_at = jnp.where(lower, 0, 32)
    near_from = jnp.where(lower, 16, 0)
    for j in range(32):
        context_ref[at + j] = plane_ref[j]
    for j in range(16):
        context_ref[near_at + j] = near_ref[near_from + j]
    base = at + 4 * y
    return lambda j: context_ref[base + j]


def data_part(h_ref, wide_ref, q):
    return dot(h_ref[q], wide_ref[:, q].reshape(64, 128), ((1,), (0,)))


def image_kernel(
    steps_all, plane_ref, near_ref, wide_ref, h_ref, weight_ref, theta_ref, lags_ref,
    out_ref, own_ref, context_ref, errors_ref,
):
    lags = scalars(lags_ref)
    slab, y = place()
    read = fill_context(plane_ref, near_ref, context_ref, y)
    back = ar_part(read, slab * 512, steps_all, lags, weight_ref, errors_ref)
    theta = theta_ref[...]
    for q in range(4):
        own = read(q)
        value = data_part(h_ref, wide_ref, q) + (RIDGE_TIME - theta) * own + AR * back[q]
        own_ref[q] = value
        for j in range(8):
            out_ref[j, q] = value


def two_sum(a, b):
    s = a + b
    t = s - a
    return s, (a - (s - t)) + (b - t)


def pair_add(a, b):
    s, e = two_sum(a[0], b[0])
    e = e + (a[1] + b[1])
    high = s + e
    return high, e - (high - s)


def split(a):
    c = a * 4097.0
    high = c - (c - a)
    return high, a - high


def pair_mul(a, b):
    p = a[0] * b[0]
    ah, al = split(a[0])
    bh, bl = split(b[0])
    e = ((ah * bh - p) + ah * bl + al * bh) + al * bl
    e = e + (a[0] * b[1] + a[1] * b[0])
    high = p + e
    return high, e - (high - p)


def pair_neg(a):
    return -a[0], -a[1]


def pair_sub(a, b):
    return pair_add(a, pair_neg(b))


def pair_div(a, b):
    first = a[0] / b[0]
    zero = jnp.zeros_like(first)
    rest = pair_sub(a, pair_mul(b, (first, zero)))
    second = rest[0] / b[0]
    return two_sum(first, second)


def pair_tree(values):
    while len(values) > 1:
        values = [
            pair_add(values[i], values[i + 1]) if i + 1 < len(values) else values[i]
            for i in range(0, len(values), 2)
        ]
    return values[0]


def lane_sum(pair):
    high, low = pair
    large = 6144.0 * jnp.max(jnp.abs(high), axis=1, keepdims=True)
    lead = (high + large) - large
    rest = (high - lead) + low
    total = [jnp.broadcast_to(jnp.sum(a, axis=1, keepdims=True), (8, 128)) for a in (lead, rest)]
    return two_sum(*total)


def fold_rows(value):
    pair = (value, jnp.zeros_like(value))
    for by in (4, 2, 1):
        pair = pair_add(pair, (pltpu.roll(pair[0], by, axis=0), pltpu.roll(pair[1], by, axis=0)))
    return pair


def product_kernel(wide_ref, h_ref, u0_ref, u1_ref, u2_ref, near_ref, out_ref):
    sums = [jnp.zeros((8, 128), F32)] * 7
    for q in range(4):
        u0, u1, u2 = u0_ref[q], u1_ref[q], u2_ref[q]
        image = data_part(h_ref, wide_ref, q) + RIDGE_TIME * u2
        terms = [u0 * u0, u0 * u1, u0 * u2, u1 * u1, u1 * u2, u2 * u2, u2 * image]
        sums = [a + b for a, b in zip(sums, terms)]
    sub = iota((8, 128), 0)
    high = low = jnp.zeros((8, 128), F32)
    for i in range(7):
        pair = fold_rows(sums[i])
        high = jnp.where(sub == i, pair[0], high)
        low = jnp.where(sub == i, pair[1], low)
    high, low = pair_add((high, low), (pltpu.roll(high, 64, axis=1), pltpu.roll(low, 64, axis=1)))
    value = jnp.where(iota((8, 128), 1) < 64, high, low)
    for y in range(8):
        for q in range(4):
            out_ref[y, q] = u2_ref[q]
            out_ref[y, 4 + q] = near_ref[q]
        out_ref[y, 8] = value


def moment_kernel(steps_all, parts_ref, weight_ref, lags_ref, out_ref, stack_ref):
    starts = [512 - lag for lag in scalars(lags_ref)[: LAGS - 1]]
    lane = iota((128, 128), 1)
    none = jnp.zeros((64, 128), F32)

    def moved(runs, main, halo):
        return pltpu.roll(jnp.where(lane >= 128 - 8 * runs, halo, main), 8 * runs, axis=1)

    far = []
    for j in range(2):
        main = jnp.concatenate([parts_ref[s // 2, 2 * (s % 2) + j] for s in range(16)], axis=0).T
        halo = [parts_ref[4 + s // 2, 4 + 2 * (s % 2) + j] for s in range(8)]
        halo = jnp.concatenate([none] + halo, axis=0).T
        at = 128 * j
        stack_ref[512 + at : 640 + at, :] = main
        stack_ref[256 + at : 384 + at, :] = moved(1, main, halo)
        stack_ref[at : 128 + at, :] = moved(2, main, halo)
        far.append(moved(8, main, halo))
        if j == 0:
            end = moved(7, main, halo)[0:32]
    far = jnp.concatenate([far[0][32:128], far[1], end], axis=0)
    half = iota((8, 128), 1) < 64
    packed = pair_tree([
        (jnp.where(half, value, 0.0), jnp.where(half, pltpu.roll(value, 64, axis=1), 0.0))
        for value in (parts_ref[y, 8] for y in range(8))
    ])
    step = lax.axis_index("tz") * 4096 + iota((8, 128), 1) // 8 * 256 + iota((8, 128), 0)
    square = jnp.zeros((8, 128), F32)
    own = iota((8, 128), 0) == iota((8, 128), 1) % 8
    weights = [jnp.sum(jnp.where(own, weight_ref[index], 0.0), axis=0, keepdims=True) for index in range(LAGS)]
    for r in range(0, 256, 8):
        past = weights[LAGS - 1] * far[r : r + 8]
        for index in range(LAGS - 1):
            past = past + weights[index] * stack_ref[pl.ds(starts[index] + r, 8), :]
        valid = (step + r >= LONGEST) & (step + r < steps_all)
        error = jnp.where(valid, stack_ref[512 + r : 520 + r, :] - past, 0.0)
        square = square + error * error
    pair = fold_rows(AR * square)
    last = iota((8, 128), 0) == 6
    packed = pair_add(packed, (jnp.where(last, pair[0], 0.0), jnp.where(last, pair[1], 0.0)))
    packed = lane_sum(packed)
    lane = iota((8, 128), 1)
    value = jnp.where(lane < 64, packed[0], packed[1])
    value = jnp.sum(jnp.where(iota((8, 128), 0) == lane % 64 // 8, value, 0.0), axis=0, keepdims=True)
    out_ref[...] = jnp.broadcast_to(value[None], out_ref.shape)


def finish_kernel(parts_ref, first_ref, theta_ref, x_ref, wide0_ref, wide1_ref, wide2_ref, out_ref):
    half = iota((8, 128), 1) < 64
    pairs = []
    for j in range(8):
        part = parts_ref[8 * j : 8 * j + 8, :]
        other = pltpu.roll(part, 64, axis=1)
        pairs.append((jnp.where(half, part, other), jnp.where(half, other, part)))
    total = pair_tree(pairs)
    for by in (4, 2, 1):
        total = pair_add(total, (pltpu.roll(total[0], by, axis=0), pltpu.roll(total[1], by, axis=0)))

    def moment(i):
        return tuple(jnp.broadcast_to(a[:, 8 * i : 8 * i + 1], (8, 128)) for a in total)

    g00, g01, g02, g11, g12, g22, m22 = [moment(i) for i in range(7)]
    theta = (theta_ref[...], jnp.zeros((8, 128), F32))
    first = (first_ref[...], jnp.zeros((8, 128), F32))
    m00 = pair_add(g01, pair_mul(first, g00))
    m01 = pair_add(g11, pair_mul(first, g01))
    m02 = pair_add(g12, pair_mul(first, g02))
    m11 = pair_add(g12, pair_mul(theta, g11))
    m12 = pair_add(g22, pair_mul(theta, g12))
    l10 = pair_div(m01, m00)
    l20 = pair_div(m02, m00)
    d1 = pair_sub(m11, pair_mul(l10, m01))
    n12 = pair_sub(m12, pair_mul(l10, m02))
    y1 = pair_sub(g01, pair_mul(l10, g00))
    l21 = pair_div(n12, d1)
    d2 = pair_sub(pair_sub(m22, pair_mul(l20, m02)), pair_mul(l21, n12))
    y2 = pair_sub(pair_sub(g02, pair_mul(l20, g00)), pair_mul(l21, y1))
    tiny = 1e-12
    c2 = jnp.where(d2[0] > tiny * m22[0], y2[0] / d2[0], 0.0)
    zero = jnp.zeros_like(c2)
    c1 = pair_sub(pair_div(y1, d1), pair_mul(l21, (c2, zero)))
    c1 = jnp.where(d1[0] > tiny * m11[0], c1[0], 0.0)
    c0 = pair_div(g00, m00)
    c0 = pair_sub(c0, pair_mul(l10, (c1, zero)))
    c0 = pair_sub(c0, pair_mul(l20, (c2, zero)))[0]
    for s in range(8):
        for q in range(4):
            at = (slice(8 * s, 8 * s + 8), slice(128 * q, 128 * q + 128))
            step = c0 * wide0_ref[s, q] + c1 * wide1_ref[s, q] + c2 * wide2_ref[s, q]
            out_ref[at] = x_ref[at] + step


def neighbour(plane):
    pairs = [(8 * z + y, 8 * ((z + (1 if y < 4 else -1)) % 8) + y) for z in range(8) for y in range(8)]
    return lax.ppermute(plane, TM, pairs)


def exchange(spread):
    plane = lax.all_to_all(spread, "ty", 0, 0).reshape(32, 8, 128)
    return plane, neighbour(plane), lax.all_to_all(spread, "series", 0, 0)


def per_device(panel, observed, start_time, ar_weight, lags):
    cells = panel.shape[0]
    steps_all = 64 * 512
    cells_all = cells * 8
    series = lax.axis_index("series")
    own_weight = lax.dynamic_slice_in_dim(ar_weight, 8 * series, 8, 0)
    weight = jnp.broadcast_to(own_weight.T[:, :, None], (LAGS, 8, 128))
    observed = observed.T
    lags = jnp.broadcast_to(lags[:, None], (LAGS, 128))
    context = pltpu.VMEM((48, 8, 128), F32)
    stack = pltpu.VMEM((768, 128), F32)
    errors = pltpu.VMEM((20, 8, 128), F32)

    parts = call(
        front_kernel,
        struct(8, 112, 128),
        (panel, observed, start_time),
        (
            pltpu.VMEM(panel.shape, F32),
            pltpu.VMEM(observed.shape, jnp.int32),
            pltpu.VMEM(start_time.shape, F32),
            pltpu.SemaphoreType.DMA((3,)),
        ),
        HBM,
        60,
    )
    parts = lax.all_to_all(parts, "ty", 0, 0)
    parts, plane = call(middle_kernel, (struct(8, 40, 128), struct(32, 8, 128)), (parts,))
    parts = lax.all_to_all(parts, "tz", 0, 0)
    solved = call(solve_kernel, struct(64, 1, 128), (parts,))
    solved, plane = lax.optimization_barrier((solved, plane))
    near = neighbour(plane)
    gathered = lax.all_to_all(solved, ("ty", "tz"), 0, 0).reshape(64, 128)
    gathered, near = lax.optimization_barrier((gathered, near))
    factors, normal = call(
        functools.partial(normal_kernel, 1.0 / cells_all),
        (struct(64, cells), struct(64, 896)),
        (gathered, panel, observed),
    )
    sums = lax.all_to_all(normal.reshape(8, 8, 896), "series", 0, 0)
    drift, theta = call(
        functools.partial(drift_kernel, steps_all),
        (struct(4, 8, 128), struct(8, 128)),
        (plane, near, weight, ar_weight, lags),
        (context, errors),
    )
    u0, own0, h, first = call(
        start_kernel,
        (struct(8, 4, 8, 128), struct(4, 8, 128), struct(4, 8, 64), struct(8, 128)),
        (sums, start_time, drift, theta),
    )

    def image(plane, near, wide, shift):
        return call(
            functools.partial(image_kernel, steps_all),
            (struct(8, 4, 8, 128), struct(4, 8, 128)),
            (plane, near, wide, h, weight, shift, lags),
            (context, errors),
        )

    plane, near, wide0 = exchange(u0)
    u1, own1 = image(plane, near, wide0, first)
    plane, near, wide1 = exchange(u1)
    u2, own2 = image(plane, near, wide1, theta)
    near = lax.ppermute(own2, "tz", [(z, (z + 1) % 8) for z in range(8)])
    wide2 = lax.all_to_all(u2, "series", 0, 0)
    parts = call(product_kernel, struct(8, 9, 8, 128), (wide2, h, own0, own1, own2, near))
    parts = lax.all_to_all(parts, "ty", 0, 0)
    moments = call(
        functools.partial(moment_kernel, steps_all), struct(64, 1, 128), (parts, weight, lags), (stack,)
    )
    moments = lax.all_to_all(moments, ("series", "tz"), 0, 0).reshape(64, 128)
    result = call(finish_kernel, struct(64, 512), (moments, first, theta, start_time, wide0, wide1, wide2))
    return (factors.T, result)


def solution(mesh):
    grid = Mesh(mesh.devices.reshape(8, 8, 8), ("series", "tz", "ty"))
    return jax.shard_map(
        per_device,
        mesh=grid,
        in_specs=(P("series", TM), P("series", TM), P(None, TM), P(), P()),
        out_specs=(P("series", None), P(None, TM)),
        check_vma=False,
    )
```

```python
import functools

import jax
import jax.numpy as jnp
from jax import lax
from jax.experimental import pallas as pl
from jax.experimental.pallas import tpu as pltpu
from jax.sharding import Mesh, PartitionSpec as P

HIGH = lax.Precision.HIGHEST
TILE = 128
LAGS = 14
LONGEST = 2016
RIDGE_FACTOR = 1.0
RIDGE_TIME = 0.05
AR = 0.25
TM = ("tz", "ty")
F32 = jnp.float32
VMEM = pl.BlockSpec(memory_space=pltpu.VMEM)
HBM = pl.BlockSpec(memory_space=pltpu.HBM)


def struct(*shape):
    return jax.ShapeDtypeStruct(shape, F32)


def iota(shape, dim):
    return lax.broadcasted_iota(jnp.int32, shape, dim)


def call(kernel, outs, ins, scratch=(), place=VMEM, room=32):
    return pl.pallas_call(
        kernel,
        out_shape=outs,
        in_specs=[place] * len(ins),
        out_specs=jax.tree.map(lambda _: VMEM, outs),
        scratch_shapes=list(scratch),
        compiler_params=pltpu.CompilerParams(vmem_limit_bytes=room * 1024 * 1024),
    )(*ins)


def dot(a, b, dims):
    return lax.dot_general(a, b, (dims, ((), ())), precision=HIGH, preferred_element_type=F32)


def columns_of(obs_ref):
    flags = obs_ref[...].astype(F32)
    return jnp.concatenate([flags] * 32, axis=0).T


def front_kernel(panel_hbm, obs_hbm, x_hbm, out_ref, panel_ref, obs_ref, x_ref, sems):
    copies = [
        pltpu.make_async_copy(source, target, sems.at[i])
        for i, (source, target) in enumerate(((x_hbm, x_ref), (obs_hbm, obs_ref), (panel_hbm, panel_ref)))
    ]
    for copy in copies:
        copy.start()
    copies[0].wait()
    x = x_ref[...]
    row = iota((32, 64), 0)
    col = iota((32, 64), 1)
    keep = (col < 32) | (col - 32 >= row)
    diag_at = iota((64, 128), 0) == iota((64, 128), 1) % 64
    lane = iota((8, 128), 1)
    sub = iota((8, 128), 0)
    packs, masked = [], []
    extra = jnp.zeros((8, 128), F32)
    for b in range(4):
        xb = x[:, b * TILE : (b + 1) * TILE]
        gram = dot(xb, xb, ((1,), (1,)))
        moved = jnp.concatenate([gram[0:32, 32:64], gram[0:32, 0:32]], axis=1)
        packs.append(jnp.where(keep, gram[32:64], moved))
        twice = jnp.concatenate([gram, gram], axis=1)
        diag = jnp.sum(jnp.where(diag_at, twice, 0.0), axis=0, keepdims=True)
        extra = jnp.where((sub == b) & (lane % 64 < 32), diag, extra)
    copies[1].wait()
    flags = columns_of(obs_ref)
    copies[2].wait()
    for b in range(4):
        masked.append(panel_ref[:, b * TILE : (b + 1) * TILE] * flags[:, b : b + 1])
    rhs = dot(jnp.concatenate(masked, axis=1), x, ((1,), (1,)))
    mine = pl.ds(pl.multiple_of(8 * lax.axis_index("series"), 8), 8)
    own = [x_ref[mine, q * TILE : (q + 1) * TILE] for q in range(4)]
    pairs = [jnp.concatenate([packs[0], packs[1]], axis=1), jnp.concatenate([packs[2], packs[3]], axis=1)]
    for y in range(8):
        out_ref[y, 0:32, :] = pairs[0]
        out_ref[y, 32:64, :] = pairs[1]
        first, second = slice(16 * y, 16 * y + 8), slice(16 * y + 8, 16 * y + 16)
        out_ref[y, 64:72, :] = jnp.concatenate([rhs[first], rhs[second]], axis=1)
        tail = extra
        for b in range(4):
            tail = jnp.where(lane // 8 == 4 + b, flags[first, b : b + 1], tail)
            tail = jnp.where(lane // 8 == 12 + b, flags[second, b : b + 1], tail)
        out_ref[y, 72:80, :] = tail
        for q in range(4):
            out_ref[y, 80 + 8 * q : 88 + 8 * q, :] = own[q]


def middle_kernel(parts_ref, out_ref, x_ref, send_ref):
    lane = iota((8, 128), 1)
    sub = iota((8, 128), 0)
    left = lane < 64
    wide_left = iota((32, 128), 1) < 64
    totals = [None] * 8
    diag = jnp.zeros((8, 128), F32)
    rhs = jnp.zeros((8, 128), F32)
    for y in range(8):
        extra = parts_ref[y, 72:80, :]
        rhs = rhs + parts_ref[y, 64:72, :]
        for pair in range(2):
            both = parts_ref[y, 32 * pair : 32 * pair + 32, :]
            other = pltpu.roll(both, 64, axis=1)
            packs = (jnp.where(wide_left, both, other), jnp.where(wide_left, other, both))
            for half in range(2):
                b = 2 * pair + half
                flag = jnp.where(left, extra[:, 32 + 8 * b : 33 + 8 * b], extra[:, 96 + 8 * b : 97 + 8 * b])
                diag = diag + flag * extra[b : b + 1]
                for z in range(8):
                    term = packs[half] * flag[z : z + 1]
                    totals[z] = term if totals[z] is None else totals[z] + term
        for q in range(4):
            x_ref[4 * y + q] = parts_ref[y, 80 + 8 * q : 88 + 8 * q, :]
    at = jnp.where(lax.axis_index("ty") < 4, 16, 0)
    for j in range(16):
        send_ref[j] = x_ref[at + j]
    for z in range(8):
        out_ref[z, 0:32, :] = totals[z]
        out_ref[z, 32:40, :] = jnp.where(sub == 0, diag[z : z + 1], jnp.where(sub == 1, rhs[z : z + 1], 0.0))


def solve_kernel(parts_ref, out_ref):
    total = parts_ref[0]
    for j in range(1, 8):
        total = total + parts_ref[j]
    pack = total[0:32]
    diag = total[32:33]
    rhs = total[33:34]
    flipped = jnp.concatenate([pack, pack, pack, pack], axis=0).T
    row = iota((32, 128), 0)
    lane = iota((32, 128), 1)
    group = lane // 32
    col = lane % 32
    first = lane < 64
    upper_t = jnp.where(first, flipped[32:64], flipped[96:128])
    cross = jnp.where(first, flipped[0:32], flipped[64:96])
    odd = group % 2 == 1
    top_left = jnp.where(col < row, pltpu.roll(pack, 96, axis=1), jnp.where(col == row, diag, upper_t))
    top = jnp.where(odd, cross, top_left)
    bottom = jnp.where(odd & (col < row), upper_t, pack)
    eye = (iota((64, 128), 0) == iota((64, 128), 1) % 64).astype(F32)
    mat = jnp.concatenate([top, bottom], axis=0) + RIDGE_FACTOR * eye
    blocks = [mat[8 * i : 8 * i + 8] for i in range(8)]
    side = jnp.broadcast_to(rhs, (8, 128))
    half = iota((8, 128), 1) < 64
    within = iota((8, 128), 1) % 64

    def spread(value, k):
        return jnp.where(half, value[:, k : k + 1], value[:, 64 + k : 65 + k])

    for i in range(8):
        columns = [[spread(blocks[m], 8 * i + j) for j in range(8)] for m in range(i, 8)]
        ends = [spread(side, 8 * i + j) for j in range(8)]
        for r in range(8):
            inverse = 1.0 / jnp.broadcast_to(columns[0][r][r : r + 1], (8, 128))
            pivot_row = jnp.broadcast_to(blocks[i][r : r + 1], (8, 128))
            factor = jnp.where(within == 8 * i + r, 1.0 - inverse, pivot_row * inverse)
            factors = [jnp.broadcast_to(columns[0][j][r : r + 1], (8, 128)) * inverse for j in range(r + 1, 8)]
            for m in range(i if r < 7 else i + 1, 8):
                own = columns[m - i]
                blocks[m] = blocks[m] - own[r] * factor
                for j in range(r + 1, 8):
                    own[j] = own[j] - own[r] * factors[j - r - 1]
            side = side - ends[r] * factor
            for j in range(r + 1, 8):
                ends[j] = ends[j] - ends[r] * factors[j - r - 1]
    out_ref[...] = jnp.broadcast_to(side[0:1][None], out_ref.shape)


def normal_kernel(scale, gathered_ref, panel_ref, obs_ref, factors_ref, out_ref):
    pieces = []
    for y in range(8):
        pair = gathered_ref[8 * y : 8 * y + 8, 0, :]
        pieces += [pair[:, 0:64], pair[:, 64:128]]
    factors = jnp.concatenate(pieces, axis=0)
    turned = factors.T
    factors_ref[...] = turned
    flags = columns_of(obs_ref)
    right = [panel_ref[:, b * TILE : (b + 1) * TILE] * flags[:, b : b + 1] for b in range(4)]
    for b in (0, 2):
        right.append(jnp.concatenate([factors * flags[:, b : b + 1], factors * flags[:, b + 1 : b + 2]], axis=1))
    right.append(factors)
    product = scale * dot(turned, jnp.concatenate(right, axis=1), ((1,), (0,)))
    out_ref[:, 0:768] = product[:, 0:768]
    gram = product[:, 768:832]
    norm = jnp.sum(gram * gram)
    trace = jnp.sum(jnp.where(iota((64, 64), 0) == iota((64, 64), 1), gram, 0.0))
    some = jnp.full((64, 128), trace)
    out_ref[:, 768:896] = jnp.where(some > 0.0, norm / jnp.where(some > 0.0, some, 1.0), 0.0)


def scalars(lags_ref):
    return [jnp.max(lags_ref[index : index + 1, :]) for index in range(LAGS)]


def lagged(read, chunks, lags, weight_ref, ahead):
    lane = iota((8, 128), 1)
    sums = {}
    for index in range(LAGS):
        lag = lags[index]
        if ahead:
            start = lag // 128
            shift = lag % 128
        else:
            back = (lag + 127) // 128
            start = -back
            shift = back * 128 - lag
        cut = 128 - shift
        weight = weight_ref[index]
        own = lane < cut
        turn = jnp.where(cut == 128, 0, cut)
        for first, last in chunks:
            low = pltpu.roll(read(start + first), turn, axis=1)
            for j in range(first, last):
                high = pltpu.roll(read(start + j + 1), turn, axis=1)
                term = weight * jnp.where(own, low, high)
                sums[j] = sums[j] + term if j in sums else term
                low = high
    return sums


def residuals(read, chunks, first_step, steps_all, lags, weight_ref):
    past = lagged(read, chunks, lags, weight_ref, False)
    lane = iota((8, 128), 1)
    out = {}
    for j, value in past.items():
        step = first_step + 128 * j + lane
        out[j] = jnp.where((step >= LONGEST) & (step < steps_all), read(j) - value, 0.0)
    return out


def ar_part(read, first_step, steps_all, lags, weight_ref, errors_ref):
    errors = residuals(read, ((0, 8), (15, 20)), first_step, steps_all, lags, weight_ref)
    for j, value in errors.items():
        errors_ref[j] = value
    later = lagged(lambda j: errors_ref[j], ((0, 4),), lags, weight_ref, True)
    return [errors[j] - later[j] for j in range(4)]


def place():
    y = lax.axis_index("ty")
    return lax.axis_index("tz") * 8 + y, y


def drift_kernel(
    steps_all, plane_ref, near_ref, weight_ref, all_ref, lags_ref, out_ref, theta_ref, context_ref, errors_ref
):
    lags = scalars(lags_ref)
    slab, y = place()
    read = fill_context(plane_ref, near_ref, context_ref, y, True)
    back = ar_part(read, slab * 512, steps_all, lags, weight_ref, errors_ref)
    for q in range(4):
        out_ref[q] = RIDGE_TIME * read(q) + AR * back[q]
    squares = all_ref[...] * all_ref[...]
    theta_ref[...] = jnp.full((8, 128), RIDGE_TIME + AR) + (AR / 64.0) * jnp.sum(squares)


def start_kernel(sums_ref, x_ref, drift_ref, theta_ref, out_ref, own_ref, h_ref, first_ref):
    total = sums_ref[0]
    for j in range(1, 8):
        total = total + sums_ref[j]
    first_ref[...] = theta_ref[...] + total[:, 768:896]
    for q in range(4):
        h = total[:, 512 + 64 * q : 576 + 64 * q]
        h_ref[q] = h
        image = dot(h, x_ref[:, q * 128 : (q + 1) * 128], ((1,), (0,))) + drift_ref[q]
        value = total[:, q * 128 : (q + 1) * 128] - image
        own_ref[q] = value
        for j in range(8):
            out_ref[j, q] = value


def fill_context(plane_ref, near_ref, context_ref, y, half=False):
    lower = y < 4
    at = jnp.where(lower, 16, 0)
    near_at = jnp.where(lower, 0, 32)
    near_from = 0 if half else jnp.where(lower, 16, 0)
    for j in range(32):
        context_ref[at + j] = plane_ref[j]
    for j in range(16):
        context_ref[near_at + j] = near_ref[near_from + j]
    base = at + 4 * y
    return lambda j: context_ref[base + j]


def data_part(h_ref, wide_ref, q):
    return dot(h_ref[q], wide_ref[:, q].reshape(64, 128), ((1,), (0,)))


def image_kernel(
    steps_all, plane_ref, near_ref, wide_ref, h_ref, weight_ref, theta_ref, lags_ref,
    out_ref, own_ref, context_ref, errors_ref,
):
    lags = scalars(lags_ref)
    slab, y = place()
    read = fill_context(plane_ref, near_ref, context_ref, y)
    back = ar_part(read, slab * 512, steps_all, lags, weight_ref, errors_ref)
    theta = theta_ref[...]
    for q in range(4):
        own = read(q)
        value = data_part(h_ref, wide_ref, q) + (RIDGE_TIME - theta) * own + AR * back[q]
        own_ref[q] = value
        for j in range(8):
            out_ref[j, q] = value


def two_sum(a, b):
    s = a + b
    t = s - a
    return s, (a - (s - t)) + (b - t)


def pair_add(a, b):
    s, e = two_sum(a[0], b[0])
    e = e + (a[1] + b[1])
    high = s + e
    return high, e - (high - s)


def split(a):
    c = a * 4097.0
    high = c - (c - a)
    return high, a - high


def pair_mul(a, b):
    p = a[0] * b[0]
    ah, al = split(a[0])
    bh, bl = split(b[0])
    e = ((ah * bh - p) + ah * bl + al * bh) + al * bl
    e = e + (a[0] * b[1] + a[1] * b[0])
    high = p + e
    return high, e - (high - p)


def pair_neg(a):
    return -a[0], -a[1]


def pair_sub(a, b):
    return pair_add(a, pair_neg(b))


def pair_div(a, b):
    first = a[0] / b[0]
    zero = jnp.zeros_like(first)
    rest = pair_sub(a, pair_mul(b, (first, zero)))
    second = rest[0] / b[0]
    return two_sum(first, second)


def pair_tree(values):
    while len(values) > 1:
        values = [
            pair_add(values[i], values[i + 1]) if i + 1 < len(values) else values[i]
            for i in range(0, len(values), 2)
        ]
    return values[0]


def lane_sum(pair):
    high, low = pair
    large = 6144.0 * jnp.max(jnp.abs(high), axis=1, keepdims=True)
    lead = (high + large) - large
    rest = (high - lead) + low
    total = [jnp.broadcast_to(jnp.sum(a, axis=1, keepdims=True), (8, 128)) for a in (lead, rest)]
    return two_sum(*total)


def fold_rows(value):
    pair = (value, jnp.zeros_like(value))
    for by in (4, 2, 1):
        pair = pair_add(pair, (pltpu.roll(pair[0], by, axis=0), pltpu.roll(pair[1], by, axis=0)))
    return pair


def product_kernel(wide_ref, h_ref, u0_ref, u1_ref, u2_ref, near_ref, out_ref):
    sums = [jnp.zeros((8, 128), F32)] * 7
    for q in range(4):
        u0, u1, u2 = u0_ref[q], u1_ref[q], u2_ref[q]
        image = data_part(h_ref, wide_ref, q) + RIDGE_TIME * u2
        terms = [u0 * u0, u0 * u1, u0 * u2, u1 * u1, u1 * u2, u2 * u2, u2 * image]
        sums = [a + b for a, b in zip(sums, terms)]
    sub = iota((8, 128), 0)
    high = low = jnp.zeros((8, 128), F32)
    for i in range(7):
        pair = fold_rows(sums[i])
        high = jnp.where(sub == i, pair[0], high)
        low = jnp.where(sub == i, pair[1], low)
    high, low = pair_add((high, low), (pltpu.roll(high, 64, axis=1), pltpu.roll(low, 64, axis=1)))
    value = jnp.where(iota((8, 128), 1) < 64, high, low)
    for y in range(8):
        for q in range(4):
            out_ref[y, q] = u2_ref[q]
            out_ref[y, 4 + q] = near_ref[q]
        out_ref[y, 8] = value


def moment_kernel(steps_all, parts_ref, weight_ref, lags_ref, out_ref, stack_ref):
    starts = [512 - lag for lag in scalars(lags_ref)[: LAGS - 1]]
    lane = iota((128, 128), 1)
    none = jnp.zeros((64, 128), F32)

    def moved(runs, main, halo):
        return pltpu.roll(jnp.where(lane >= 128 - 8 * runs, halo, main), 8 * runs, axis=1)

    far = []
    for j in range(2):
        main = jnp.concatenate([parts_ref[s // 2, 2 * (s % 2) + j] for s in range(16)], axis=0).T
        halo = [parts_ref[4 + s // 2, 4 + 2 * (s % 2) + j] for s in range(8)]
        halo = jnp.concatenate([none] + halo, axis=0).T
        at = 128 * j
        stack_ref[512 + at : 640 + at, :] = main
        stack_ref[256 + at : 384 + at, :] = moved(1, main, halo)
        stack_ref[at : 128 + at, :] = moved(2, main, halo)
        far.append(moved(8, main, halo))
        if j == 0:
            end = moved(7, main, halo)[0:32]
    far = jnp.concatenate([far[0][32:128], far[1], end], axis=0)
    half = iota((8, 128), 1) < 64
    packed = pair_tree([
        (jnp.where(half, value, 0.0), jnp.where(half, pltpu.roll(value, 64, axis=1), 0.0))
        for value in (parts_ref[y, 8] for y in range(8))
    ])
    step = lax.axis_index("tz") * 4096 + iota((8, 128), 1) // 8 * 256 + iota((8, 128), 0)
    square = jnp.zeros((8, 128), F32)
    own = iota((8, 128), 0) == iota((8, 128), 1) % 8
    weights = [jnp.sum(jnp.where(own, weight_ref[index], 0.0), axis=0, keepdims=True) for index in range(LAGS)]
    for r in range(0, 256, 8):
        past = weights[LAGS - 1] * far[r : r + 8]
        for index in range(LAGS - 1):
            past = past + weights[index] * stack_ref[pl.ds(starts[index] + r, 8), :]
        valid = (step + r >= LONGEST) & (step + r < steps_all)
        error = jnp.where(valid, stack_ref[512 + r : 520 + r, :] - past, 0.0)
        square = square + error * error
    pair = fold_rows(AR * square)
    last = iota((8, 128), 0) == 6
    packed = pair_add(packed, (jnp.where(last, pair[0], 0.0), jnp.where(last, pair[1], 0.0)))
    packed = lane_sum(packed)
    lane = iota((8, 128), 1)
    value = jnp.where(lane < 64, packed[0], packed[1])
    value = jnp.sum(jnp.where(iota((8, 128), 0) == lane % 64 // 8, value, 0.0), axis=0, keepdims=True)
    out_ref[...] = jnp.broadcast_to(value[None], out_ref.shape)


def finish_kernel(parts_ref, first_ref, theta_ref, x_ref, wide0_ref, wide1_ref, wide2_ref, out_ref):
    half = iota((8, 128), 1) < 64
    pairs = []
    for j in range(8):
        part = parts_ref[8 * j : 8 * j + 8, :]
        other = pltpu.roll(part, 64, axis=1)
        pairs.append((jnp.where(half, part, other), jnp.where(half, other, part)))
    total = pair_tree(pairs)
    for by in (4, 2, 1):
        total = pair_add(total, (pltpu.roll(total[0], by, axis=0), pltpu.roll(total[1], by, axis=0)))

    def moment(i):
        return tuple(jnp.broadcast_to(a[:, 8 * i : 8 * i + 1], (8, 128)) for a in total)

    g00, g01, g02, g11, g12, g22, m22 = [moment(i) for i in range(7)]
    theta = (theta_ref[...], jnp.zeros((8, 128), F32))
    first = (first_ref[...], jnp.zeros((8, 128), F32))
    m00 = pair_add(g01, pair_mul(first, g00))
    m01 = pair_add(g11, pair_mul(first, g01))
    m02 = pair_add(g12, pair_mul(first, g02))
    m11 = pair_add(g12, pair_mul(theta, g11))
    m12 = pair_add(g22, pair_mul(theta, g12))
    l10 = pair_div(m01, m00)
    l20 = pair_div(m02, m00)
    d1 = pair_sub(m11, pair_mul(l10, m01))
    n12 = pair_sub(m12, pair_mul(l10, m02))
    y1 = pair_sub(g01, pair_mul(l10, g00))
    l21 = pair_div(n12, d1)
    d2 = pair_sub(pair_sub(m22, pair_mul(l20, m02)), pair_mul(l21, n12))
    y2 = pair_sub(pair_sub(g02, pair_mul(l20, g00)), pair_mul(l21, y1))
    tiny = 1e-12
    c2 = jnp.where(d2[0] > tiny * m22[0], y2[0] / d2[0], 0.0)
    zero = jnp.zeros_like(c2)
    c1 = pair_sub(pair_div(y1, d1), pair_mul(l21, (c2, zero)))
    c1 = jnp.where(d1[0] > tiny * m11[0], c1[0], 0.0)
    c0 = pair_div(g00, m00)
    c0 = pair_sub(c0, pair_mul(l10, (c1, zero)))
    c0 = pair_sub(c0, pair_mul(l20, (c2, zero)))[0]
    for s in range(8):
        for q in range(4):
            at = (slice(8 * s, 8 * s + 8), slice(128 * q, 128 * q + 128))
            step = c0 * wide0_ref[s, q] + c1 * wide1_ref[s, q] + c2 * wide2_ref[s, q]
            out_ref[at] = x_ref[at] + step


def neighbour(plane):
    pairs = [(8 * z + y, 8 * ((z + (1 if y < 4 else -1)) % 8) + y) for z in range(8) for y in range(8)]
    return lax.ppermute(plane, TM, pairs)


def exchange(spread):
    plane = lax.all_to_all(spread, "ty", 0, 0).reshape(32, 8, 128)
    return plane, neighbour(plane), lax.all_to_all(spread, "series", 0, 0)


def per_device(panel, observed, start_time, ar_weight, lags):
    cells = panel.shape[0]
    steps_all = 64 * 512
    cells_all = cells * 8
    series = lax.axis_index("series")
    own_weight = lax.dynamic_slice_in_dim(ar_weight, 8 * series, 8, 0)
    weight = jnp.broadcast_to(own_weight.T[:, :, None], (LAGS, 8, 128))
    observed = observed.T
    lags = jnp.broadcast_to(lags[:, None], (LAGS, 128))
    context = pltpu.VMEM((48, 8, 128), F32)
    stack = pltpu.VMEM((768, 128), F32)
    errors = pltpu.VMEM((20, 8, 128), F32)

    parts = call(
        front_kernel,
        struct(8, 112, 128),
        (panel, observed, start_time),
        (
            pltpu.VMEM(panel.shape, F32),
            pltpu.VMEM(observed.shape, jnp.int32),
            pltpu.VMEM(start_time.shape, F32),
            pltpu.SemaphoreType.DMA((3,)),
        ),
        HBM,
        60,
    )
    parts = lax.all_to_all(parts, "ty", 0, 0)
    parts, plane, send = call(
        middle_kernel, (struct(8, 40, 128), struct(32, 8, 128), struct(16, 8, 128)), (parts,)
    )
    parts = lax.all_to_all(parts, "tz", 0, 0)
    solved = call(solve_kernel, struct(64, 4, 128), (parts,))
    solved, send = lax.optimization_barrier((solved, send))
    near = neighbour(send)
    gathered = lax.all_to_all(solved, ("ty", "tz"), 0, 0)
    gathered, near = lax.optimization_barrier((gathered, near))
    factors, normal = call(
        functools.partial(normal_kernel, 1.0 / cells_all),
        (struct(64, cells), struct(64, 896)),
        (gathered, panel, observed),
    )
    sums = lax.all_to_all(normal.reshape(8, 8, 896), "series", 0, 0)
    drift, theta = call(
        functools.partial(drift_kernel, steps_all),
        (struct(4, 8, 128), struct(8, 128)),
        (plane, near, weight, ar_weight, lags),
        (context, errors),
    )
    u0, own0, h, first = call(
        start_kernel,
        (struct(8, 4, 8, 128), struct(4, 8, 128), struct(4, 8, 64), struct(8, 128)),
        (sums, start_time, drift, theta),
    )

    def image(plane, near, wide, shift):
        return call(
            functools.partial(image_kernel, steps_all),
            (struct(8, 4, 8, 128), struct(4, 8, 128)),
            (plane, near, wide, h, weight, shift, lags),
            (context, errors),
        )

    plane, near, wide0 = exchange(u0)
    u1, own1 = image(plane, near, wide0, first)
    plane, near, wide1 = exchange(u1)
    u2, own2 = image(plane, near, wide1, theta)
    near = lax.ppermute(own2, "tz", [(z, (z + 1) % 8) for z in range(8)])
    wide2 = lax.all_to_all(u2, "series", 0, 0)
    parts = call(product_kernel, struct(8, 9, 8, 128), (wide2, h, own0, own1, own2, near))
    parts = lax.all_to_all(parts, "ty", 0, 0)
    moments = call(
        functools.partial(moment_kernel, steps_all), struct(64, 1, 128), (parts, weight, lags), (stack,)
    )
    moments = lax.all_to_all(moments, ("series", "tz"), 0, 0).reshape(64, 128)
    result = call(finish_kernel, struct(64, 512), (moments, first, theta, start_time, wide0, wide1, wide2))
    return (factors.T, result)


def solution(mesh):
    grid = Mesh(mesh.devices.reshape(8, 8, 8), ("series", "tz", "ty"))
    return jax.shard_map(
        per_device,
        mesh=grid,
        in_specs=(P("series", TM), P("series", TM), P(None, TM), P(), P()),
        out_specs=(P("series", None), P(None, TM)),
        check_vma=False,
    )
```

```python
import functools

import jax
import jax.numpy as jnp
from jax import lax
from jax.experimental import pallas as pl
from jax.experimental.pallas import tpu as pltpu
from jax.sharding import Mesh, PartitionSpec as P

HIGH = lax.Precision.HIGHEST
TILE = 128
LAGS = 14
LONGEST = 2016
RIDGE_FACTOR = 1.0
RIDGE_TIME = 0.05
AR = 0.25
TM = ("tz", "ty")
F32 = jnp.float32
VMEM = pl.BlockSpec(memory_space=pltpu.VMEM)
HBM = pl.BlockSpec(memory_space=pltpu.HBM)


def struct(*shape):
    return jax.ShapeDtypeStruct(shape, F32)


def iota(shape, dim):
    return lax.broadcasted_iota(jnp.int32, shape, dim)


def call(kernel, outs, ins, scratch=(), place=VMEM, room=32):
    return pl.pallas_call(
        kernel,
        out_shape=outs,
        in_specs=[place] * len(ins),
        out_specs=jax.tree.map(lambda _: VMEM, outs),
        scratch_shapes=list(scratch),
        compiler_params=pltpu.CompilerParams(vmem_limit_bytes=room * 1024 * 1024),
    )(*ins)


def dot(a, b, dims):
    return lax.dot_general(a, b, (dims, ((), ())), precision=HIGH, preferred_element_type=F32)


def columns_of(obs_ref):
    flags = obs_ref[...].astype(F32)
    return jnp.concatenate([flags] * 32, axis=0).T


def front_kernel(panel_hbm, obs_hbm, x_hbm, out_ref, panel_ref, obs_ref, x_ref, sems):
    copies = [
        pltpu.make_async_copy(source, target, sems.at[i])
        for i, (source, target) in enumerate(((x_hbm, x_ref), (obs_hbm, obs_ref), (panel_hbm, panel_ref)))
    ]
    for copy in copies:
        copy.start()
    copies[0].wait()
    x = x_ref[...]
    row = iota((32, 64), 0)
    col = iota((32, 64), 1)
    keep = (col < 32) | (col - 32 >= row)
    diag_at = iota((64, 128), 0) == iota((64, 128), 1) % 64
    lane = iota((8, 128), 1)
    sub = iota((8, 128), 0)
    packs, masked = [], []
    extra = jnp.zeros((8, 128), F32)
    for b in range(4):
        xb = x[:, b * TILE : (b + 1) * TILE]
        gram = dot(xb, xb, ((1,), (1,)))
        moved = jnp.concatenate([gram[0:32, 32:64], gram[0:32, 0:32]], axis=1)
        packs.append(jnp.where(keep, gram[32:64], moved))
        twice = jnp.concatenate([gram, gram], axis=1)
        diag = jnp.sum(jnp.where(diag_at, twice, 0.0), axis=0, keepdims=True)
        extra = jnp.where((sub == b) & (lane % 64 < 32), diag, extra)
    copies[1].wait()
    flags = columns_of(obs_ref)
    copies[2].wait()
    for b in range(4):
        masked.append(panel_ref[:, b * TILE : (b + 1) * TILE] * flags[:, b : b + 1])
    rhs = dot(jnp.concatenate(masked, axis=1), x, ((1,), (1,)))
    mine = pl.ds(pl.multiple_of(8 * lax.axis_index("series"), 8), 8)
    own = [x_ref[mine, q * TILE : (q + 1) * TILE] for q in range(4)]
    pairs = [jnp.concatenate([packs[0], packs[1]], axis=1), jnp.concatenate([packs[2], packs[3]], axis=1)]
    for y in range(8):
        out_ref[y, 0:32, :] = pairs[0]
        out_ref[y, 32:64, :] = pairs[1]
        first, second = slice(16 * y, 16 * y + 8), slice(16 * y + 8, 16 * y + 16)
        out_ref[y, 64:72, :] = jnp.concatenate([rhs[first], rhs[second]], axis=1)
        tail = extra
        for b in range(4):
            tail = jnp.where(lane // 8 == 4 + b, flags[first, b : b + 1], tail)
            tail = jnp.where(lane // 8 == 12 + b, flags[second, b : b + 1], tail)
        out_ref[y, 72:80, :] = tail
        for q in range(4):
            out_ref[y, 80 + 8 * q : 88 + 8 * q, :] = own[q]


def middle_kernel(parts_ref, out_ref, x_ref):
    lane = iota((8, 128), 1)
    sub = iota((8, 128), 0)
    left = lane < 64
    wide_left = iota((32, 128), 1) < 64
    totals = [None] * 8
    diag = jnp.zeros((8, 128), F32)
    rhs = jnp.zeros((8, 128), F32)
    for y in range(8):
        extra = parts_ref[y, 72:80, :]
        rhs = rhs + parts_ref[y, 64:72, :]
        for pair in range(2):
            both = parts_ref[y, 32 * pair : 32 * pair + 32, :]
            other = pltpu.roll(both, 64, axis=1)
            packs = (jnp.where(wide_left, both, other), jnp.where(wide_left, other, both))
            for half in range(2):
                b = 2 * pair + half
                flag = jnp.where(left, extra[:, 32 + 8 * b : 33 + 8 * b], extra[:, 96 + 8 * b : 97 + 8 * b])
                diag = diag + flag * extra[b : b + 1]
                for z in range(8):
                    term = packs[half] * flag[z : z + 1]
                    totals[z] = term if totals[z] is None else totals[z] + term
        for q in range(4):
            x_ref[4 * y + q] = parts_ref[y, 80 + 8 * q : 88 + 8 * q, :]
    for z in range(8):
        out_ref[z, 0:32, :] = totals[z]
        out_ref[z, 32:40, :] = jnp.where(sub == 0, diag[z : z + 1], jnp.where(sub == 1, rhs[z : z + 1], 0.0))


def solve_kernel(parts_ref, out_ref):
    total = parts_ref[0]
    for j in range(1, 8):
        total = total + parts_ref[j]
    pack = total[0:32]
    diag = total[32:33]
    rhs = total[33:34]
    flipped = jnp.concatenate([pack, pack, pack, pack], axis=0).T
    row = iota((32, 128), 0)
    lane = iota((32, 128), 1)
    group = lane // 32
    col = lane % 32
    first = lane < 64
    upper_t = jnp.where(first, flipped[32:64], flipped[96:128])
    cross = jnp.where(first, flipped[0:32], flipped[64:96])
    odd = group % 2 == 1
    top_left = jnp.where(col < row, pltpu.roll(pack, 96, axis=1), jnp.where(col == row, diag, upper_t))
    top = jnp.where(odd, cross, top_left)
    bottom = jnp.where(odd & (col < row), upper_t, pack)
    eye = (iota((64, 128), 0) == iota((64, 128), 1) % 64).astype(F32)
    mat = jnp.concatenate([top, bottom], axis=0) + RIDGE_FACTOR * eye
    blocks = [mat[8 * i : 8 * i + 8] for i in range(8)]
    side = jnp.broadcast_to(rhs, (8, 128))
    half = iota((8, 128), 1) < 64
    within = iota((8, 128), 1) % 64

    def spread(value, k):
        return jnp.where(half, value[:, k : k + 1], value[:, 64 + k : 65 + k])

    for i in range(8):
        columns = [[spread(blocks[m], 8 * i + j) for j in range(8)] for m in range(i, 8)]
        ends = [spread(side, 8 * i + j) for j in range(8)]
        for r in range(8):
            inverse = 1.0 / jnp.broadcast_to(columns[0][r][r : r + 1], (8, 128))
            pivot_row = jnp.broadcast_to(blocks[i][r : r + 1], (8, 128))
            factor = jnp.where(within == 8 * i + r, 1.0 - inverse, pivot_row * inverse)
            factors = [jnp.broadcast_to(columns[0][j][r : r + 1], (8, 128)) * inverse for j in range(r + 1, 8)]
            for m in range(i if r < 7 else i + 1, 8):
                own = columns[m - i]
                blocks[m] = blocks[m] - own[r] * factor
                for j in range(r + 1, 8):
                    own[j] = own[j] - own[r] * factors[j - r - 1]
            side = side - ends[r] * factor
            for j in range(r + 1, 8):
                ends[j] = ends[j] - ends[r] * factors[j - r - 1]
    out_ref[...] = jnp.broadcast_to(side[0:1][None], out_ref.shape)


def normal_kernel(scale, gathered_ref, panel_ref, obs_ref, factors_ref, out_ref):
    pieces = []
    for y in range(8):
        pair = gathered_ref[8 * y : 8 * y + 8, :]
        pieces += [pair[:, 0:64], pair[:, 64:128]]
    factors = jnp.concatenate(pieces, axis=0)
    turned = factors.T
    factors_ref[...] = turned
    flags = columns_of(obs_ref)
    right = [panel_ref[:, b * TILE : (b + 1) * TILE] * flags[:, b : b + 1] for b in range(4)]
    for b in (0, 2):
        right.append(jnp.concatenate([factors * flags[:, b : b + 1], factors * flags[:, b + 1 : b + 2]], axis=1))
    right.append(factors)
    product = scale * dot(turned, jnp.concatenate(right, axis=1), ((1,), (0,)))
    out_ref[:, 0:768] = product[:, 0:768]
    gram = product[:, 768:832]
    norm = jnp.sum(gram * gram)
    trace = jnp.sum(jnp.where(iota((64, 64), 0) == iota((64, 64), 1), gram, 0.0))
    some = jnp.full((64, 128), trace)
    out_ref[:, 768:896] = jnp.where(some > 0.0, norm / jnp.where(some > 0.0, some, 1.0), 0.0)


def scalars(lags_ref):
    return [jnp.max(lags_ref[index : index + 1, :]) for index in range(LAGS)]


def lagged(read, chunks, lags, weight_ref, ahead):
    lane = iota((8, 128), 1)
    sums = {}
    for index in range(LAGS):
        lag = lags[index]
        if ahead:
            start = lag // 128
            shift = lag % 128
        else:
            back = (lag + 127) // 128
            start = -back
            shift = back * 128 - lag
        cut = 128 - shift
        weight = weight_ref[index]
        own = lane < cut
        turn = jnp.where(cut == 128, 0, cut)
        for first, last in chunks:
            low = pltpu.roll(read(start + first), turn, axis=1)
            for j in range(first, last):
                high = pltpu.roll(read(start + j + 1), turn, axis=1)
                term = weight * jnp.where(own, low, high)
                sums[j] = sums[j] + term if j in sums else term
                low = high
    return sums


def residuals(read, chunks, first_step, steps_all, lags, weight_ref):
    past = lagged(read, chunks, lags, weight_ref, False)
    lane = iota((8, 128), 1)
    out = {}
    for j, value in past.items():
        step = first_step + 128 * j + lane
        out[j] = jnp.where((step >= LONGEST) & (step < steps_all), read(j) - value, 0.0)
    return out


def ar_part(read, first_step, steps_all, lags, weight_ref, errors_ref):
    errors = residuals(read, ((0, 8), (15, 20)), first_step, steps_all, lags, weight_ref)
    for j, value in errors.items():
        errors_ref[j] = value
    later = lagged(lambda j: errors_ref[j], ((0, 4),), lags, weight_ref, True)
    return [errors[j] - later[j] for j in range(4)]


def place():
    y = lax.axis_index("ty")
    return lax.axis_index("tz") * 8 + y, y


def drift_kernel(
    steps_all, plane_ref, near_ref, weight_ref, all_ref, lags_ref, out_ref, theta_ref, context_ref, errors_ref
):
    lags = scalars(lags_ref)
    slab, y = place()
    read = fill_context(plane_ref, near_ref, context_ref, y)
    back = ar_part(read, slab * 512, steps_all, lags, weight_ref, errors_ref)
    for q in range(4):
        out_ref[q] = RIDGE_TIME * read(q) + AR * back[q]
    squares = all_ref[...] * all_ref[...]
    theta_ref[...] = jnp.full((8, 128), RIDGE_TIME + AR) + (AR / 64.0) * jnp.sum(squares)


def start_kernel(sums_ref, x_ref, drift_ref, theta_ref, out_ref, own_ref, h_ref, first_ref):
    total = sums_ref[0]
    for j in range(1, 8):
        total = total + sums_ref[j]
    first_ref[...] = theta_ref[...] + total[:, 768:896]
    for q in range(4):
        h = total[:, 512 + 64 * q : 576 + 64 * q]
        h_ref[q] = h
        image = dot(h, x_ref[:, q * 128 : (q + 1) * 128], ((1,), (0,))) + drift_ref[q]
        value = total[:, q * 128 : (q + 1) * 128] - image
        own_ref[q] = value
        for j in range(8):
            out_ref[j, q] = value


def fill_context(plane_ref, near_ref, context_ref, y):
    lower = y < 4
    at = jnp.where(lower, 16, 0)
    near_at = jnp.where(lower, 0, 32)
    near_from = jnp.where(lower, 16, 0)
    for j in range(32):
        context_ref[at + j] = plane_ref[j]
    for j in range(16):
        context_ref[near_at + j] = near_ref[near_from + j]
    base = at + 4 * y
    return lambda j: context_ref[base + j]


def data_part(h_ref, wide_ref, q):
    return dot(h_ref[q], wide_ref[:, q].reshape(64, 128), ((1,), (0,)))


def image_kernel(
    steps_all, plane_ref, near_ref, wide_ref, h_ref, weight_ref, theta_ref, lags_ref,
    out_ref, own_ref, context_ref, errors_ref,
):
    lags = scalars(lags_ref)
    slab, y = place()
    read = fill_context(plane_ref, near_ref, context_ref, y)
    back = ar_part(read, slab * 512, steps_all, lags, weight_ref, errors_ref)
    theta = theta_ref[...]
    for q in range(4):
        own = read(q)
        value = data_part(h_ref, wide_ref, q) + (RIDGE_TIME - theta) * own + AR * back[q]
        own_ref[q] = value
        for j in range(8):
            out_ref[j, q] = value


def two_sum(a, b):
    s = a + b
    t = s - a
    return s, (a - (s - t)) + (b - t)


def pair_add(a, b):
    s, e = two_sum(a[0], b[0])
    e = e + (a[1] + b[1])
    high = s + e
    return high, e - (high - s)


def split(a):
    c = a * 4097.0
    high = c - (c - a)
    return high, a - high


def pair_mul(a, b):
    p = a[0] * b[0]
    ah, al = split(a[0])
    bh, bl = split(b[0])
    e = ((ah * bh - p) + ah * bl + al * bh) + al * bl
    e = e + (a[0] * b[1] + a[1] * b[0])
    high = p + e
    return high, e - (high - p)


def pair_neg(a):
    return -a[0], -a[1]


def pair_sub(a, b):
    return pair_add(a, pair_neg(b))


def pair_div(a, b):
    first = a[0] / b[0]
    zero = jnp.zeros_like(first)
    rest = pair_sub(a, pair_mul(b, (first, zero)))
    second = rest[0] / b[0]
    return two_sum(first, second)


def pair_tree(values):
    while len(values) > 1:
        values = [
            pair_add(values[i], values[i + 1]) if i + 1 < len(values) else values[i]
            for i in range(0, len(values), 2)
        ]
    return values[0]


def lane_sum(pair):
    high, low = pair
    large = 6144.0 * jnp.max(jnp.abs(high), axis=1, keepdims=True)
    lead = (high + large) - large
    rest = (high - lead) + low
    total = [jnp.broadcast_to(jnp.sum(a, axis=1, keepdims=True), (8, 128)) for a in (lead, rest)]
    return two_sum(*total)


def fold_rows(value):
    pair = (value, jnp.zeros_like(value))
    for by in (4, 2, 1):
        pair = pair_add(pair, (pltpu.roll(pair[0], by, axis=0), pltpu.roll(pair[1], by, axis=0)))
    return pair


def product_kernel(wide_ref, h_ref, u0_ref, u1_ref, u2_ref, near_ref, out_ref):
    sums = [jnp.zeros((8, 128), F32)] * 7
    for q in range(4):
        u0, u1, u2 = u0_ref[q], u1_ref[q], u2_ref[q]
        image = data_part(h_ref, wide_ref, q) + RIDGE_TIME * u2
        terms = [u0 * u0, u0 * u1, u0 * u2, u1 * u1, u1 * u2, u2 * u2, u2 * image]
        sums = [a + b for a, b in zip(sums, terms)]
    sub = iota((8, 128), 0)
    high = low = jnp.zeros((8, 128), F32)
    for i in range(7):
        pair = fold_rows(sums[i])
        high = jnp.where(sub == i, pair[0], high)
        low = jnp.where(sub == i, pair[1], low)
    high, low = pair_add((high, low), (pltpu.roll(high, 64, axis=1), pltpu.roll(low, 64, axis=1)))
    value = jnp.where(iota((8, 128), 1) < 64, high, low)
    for y in range(8):
        for q in range(4):
            out_ref[y, q] = u2_ref[q]
            out_ref[y, 4 + q] = near_ref[q]
        out_ref[y, 8] = value


def moment_kernel(steps_all, parts_ref, weight_ref, lags_ref, out_ref, stack_ref):
    starts = [512 - lag for lag in scalars(lags_ref)[: LAGS - 1]]
    lane = iota((128, 128), 1)
    none = jnp.zeros((64, 128), F32)

    def moved(runs, main, halo):
        return pltpu.roll(jnp.where(lane >= 128 - 8 * runs, halo, main), 8 * runs, axis=1)

    far = []
    for j in range(2):
        main = jnp.concatenate([parts_ref[s // 2, 2 * (s % 2) + j] for s in range(16)], axis=0).T
        halo = [parts_ref[4 + s // 2, 4 + 2 * (s % 2) + j] for s in range(8)]
        halo = jnp.concatenate([none] + halo, axis=0).T
        at = 128 * j
        stack_ref[512 + at : 640 + at, :] = main
        stack_ref[256 + at : 384 + at, :] = moved(1, main, halo)
        stack_ref[at : 128 + at, :] = moved(2, main, halo)
        far.append(moved(8, main, halo))
        if j == 0:
            end = moved(7, main, halo)[0:32]
    far = jnp.concatenate([far[0][32:128], far[1], end], axis=0)
    half = iota((8, 128), 1) < 64
    packed = pair_tree([
        (jnp.where(half, value, 0.0), jnp.where(half, pltpu.roll(value, 64, axis=1), 0.0))
        for value in (parts_ref[y, 8] for y in range(8))
    ])
    step = lax.axis_index("tz") * 4096 + iota((8, 128), 1) // 8 * 256 + iota((8, 128), 0)
    square = jnp.zeros((8, 128), F32)
    own = iota((8, 128), 0) == iota((8, 128), 1) % 8
    weights = [jnp.sum(jnp.where(own, weight_ref[index], 0.0), axis=0, keepdims=True) for index in range(LAGS)]
    for r in range(0, 256, 8):
        past = weights[LAGS - 1] * far[r : r + 8]
        for index in range(LAGS - 1):
            past = past + weights[index] * stack_ref[pl.ds(starts[index] + r, 8), :]
        valid = (step + r >= LONGEST) & (step + r < steps_all)
        error = jnp.where(valid, stack_ref[512 + r : 520 + r, :] - past, 0.0)
        square = square + error * error
    pair = fold_rows(AR * square)
    last = iota((8, 128), 0) == 6
    packed = pair_add(packed, (jnp.where(last, pair[0], 0.0), jnp.where(last, pair[1], 0.0)))
    packed = lane_sum(packed)
    lane = iota((8, 128), 1)
    value = jnp.where(lane < 64, packed[0], packed[1])
    value = jnp.sum(jnp.where(iota((8, 128), 0) == lane % 64 // 8, value, 0.0), axis=0, keepdims=True)
    out_ref[...] = jnp.broadcast_to(value[None], out_ref.shape)


def finish_kernel(parts_ref, first_ref, theta_ref, x_ref, wide0_ref, wide1_ref, wide2_ref, out_ref):
    parts = parts_ref[...]
    other = pltpu.roll(parts, 64, axis=1)
    half = iota((64, 128), 1) < 64
    high, low = jnp.where(half, parts, other), jnp.where(half, other, parts)
    large = 6144.0 * jnp.max(jnp.abs(high), axis=0, keepdims=True)
    lead = (high + large) - large
    rest = (high - lead) + low
    total = two_sum(*[jnp.broadcast_to(jnp.sum(a, axis=0, keepdims=True), (8, 128)) for a in (lead, rest)])

    def moment(i):
        return tuple(jnp.broadcast_to(a[:, 8 * i : 8 * i + 1], (8, 128)) for a in total)

    g00, g01, g02, g11, g12, g22, m22 = [moment(i) for i in range(7)]
    theta = (theta_ref[...], jnp.zeros((8, 128), F32))
    first = (first_ref[...], jnp.zeros((8, 128), F32))
    m00 = pair_add(g01, pair_mul(first, g00))
    m01 = pair_add(g11, pair_mul(first, g01))
    m02 = pair_add(g12, pair_mul(first, g02))
    m11 = pair_add(g12, pair_mul(theta, g11))
    m12 = pair_add(g22, pair_mul(theta, g12))
    l10 = pair_div(m01, m00)
    l20 = pair_div(m02, m00)
    d1 = pair_sub(m11, pair_mul(l10, m01))
    n12 = pair_sub(m12, pair_mul(l10, m02))
    y1 = pair_sub(g01, pair_mul(l10, g00))
    l21 = pair_div(n12, d1)
    d2 = pair_sub(pair_sub(m22, pair_mul(l20, m02)), pair_mul(l21, n12))
    y2 = pair_sub(pair_sub(g02, pair_mul(l20, g00)), pair_mul(l21, y1))
    tiny = 1e-12
    c2 = jnp.where(d2[0] > tiny * m22[0], y2[0] / d2[0], 0.0)
    zero = jnp.zeros_like(c2)
    c1 = pair_sub(pair_div(y1, d1), pair_mul(l21, (c2, zero)))
    c1 = jnp.where(d1[0] > tiny * m11[0], c1[0], 0.0)
    c0 = pair_div(g00, m00)
    c0 = pair_sub(c0, pair_mul(l10, (c1, zero)))
    c0 = pair_sub(c0, pair_mul(l20, (c2, zero)))[0]
    for s in range(8):
        for q in range(4):
            at = (slice(8 * s, 8 * s + 8), slice(128 * q, 128 * q + 128))
            step = c0 * wide0_ref[s, q] + c1 * wide1_ref[s, q] + c2 * wide2_ref[s, q]
            out_ref[at] = x_ref[at] + step


def neighbour(plane):
    pairs = [(8 * z + y, 8 * ((z + (1 if y < 4 else -1)) % 8) + y) for z in range(8) for y in range(8)]
    return lax.ppermute(plane, TM, pairs)


def exchange(spread):
    plane = lax.all_to_all(spread, "ty", 0, 0).reshape(32, 8, 128)
    return plane, neighbour(plane), lax.all_to_all(spread, "series", 0, 0)


def per_device(panel, observed, start_time, ar_weight, lags):
    cells = panel.shape[0]
    steps_all = 64 * 512
    cells_all = cells * 8
    series = lax.axis_index("series")
    own_weight = lax.dynamic_slice_in_dim(ar_weight, 8 * series, 8, 0)
    weight = jnp.broadcast_to(own_weight.T[:, :, None], (LAGS, 8, 128))
    observed = observed.T
    lags = jnp.broadcast_to(lags[:, None], (LAGS, 128))
    context = pltpu.VMEM((48, 8, 128), F32)
    stack = pltpu.VMEM((768, 128), F32)
    errors = pltpu.VMEM((20, 8, 128), F32)

    parts = call(
        front_kernel,
        struct(8, 112, 128),
        (panel, observed, start_time),
        (
            pltpu.VMEM(panel.shape, F32),
            pltpu.VMEM(observed.shape, jnp.int32),
            pltpu.VMEM(start_time.shape, F32),
            pltpu.SemaphoreType.DMA((3,)),
        ),
        HBM,
        60,
    )
    parts = lax.all_to_all(parts, "ty", 0, 0)
    parts, plane = call(middle_kernel, (struct(8, 40, 128), struct(32, 8, 128)), (parts,))
    parts = lax.all_to_all(parts, "tz", 0, 0)
    solved = call(solve_kernel, struct(64, 1, 128), (parts,))
    solved, plane = lax.optimization_barrier((solved, plane))
    near = neighbour(plane)
    gathered = lax.all_to_all(solved, ("ty", "tz"), 0, 0).reshape(64, 128)
    gathered, near = lax.optimization_barrier((gathered, near))
    factors, normal = call(
        functools.partial(normal_kernel, 1.0 / cells_all),
        (struct(64, cells), struct(64, 896)),
        (gathered, panel, observed),
    )
    sums = lax.all_to_all(normal.reshape(8, 8, 896), "series", 0, 0)
    drift, theta = call(
        functools.partial(drift_kernel, steps_all),
        (struct(4, 8, 128), struct(8, 128)),
        (plane, near, weight, ar_weight, lags),
        (context, errors),
    )
    u0, own0, h, first = call(
        start_kernel,
        (struct(8, 4, 8, 128), struct(4, 8, 128), struct(4, 8, 64), struct(8, 128)),
        (sums, start_time, drift, theta),
    )

    def image(plane, near, wide, shift):
        return call(
            functools.partial(image_kernel, steps_all),
            (struct(8, 4, 8, 128), struct(4, 8, 128)),
            (plane, near, wide, h, weight, shift, lags),
            (context, errors),
        )

    plane, near, wide0 = exchange(u0)
    u1, own1 = image(plane, near, wide0, first)
    plane, near, wide1 = exchange(u1)
    u2, own2 = image(plane, near, wide1, theta)
    near = lax.ppermute(own2, "tz", [(z, (z + 1) % 8) for z in range(8)])
    wide2 = lax.all_to_all(u2, "series", 0, 0)
    parts = call(product_kernel, struct(8, 9, 8, 128), (wide2, h, own0, own1, own2, near))
    parts = lax.all_to_all(parts, "ty", 0, 0)
    moments = call(
        functools.partial(moment_kernel, steps_all), struct(64, 1, 128), (parts, weight, lags), (stack,)
    )
    moments = lax.all_to_all(moments, ("series", "tz"), 0, 0).reshape(64, 128)
    result = call(finish_kernel, struct(64, 512), (moments, first, theta, start_time, wide0, wide1, wide2))
    return (factors.T, result)


def solution(mesh):
    grid = Mesh(mesh.devices.reshape(8, 8, 8), ("series", "tz", "ty"))
    return jax.shard_map(
        per_device,
        mesh=grid,
        in_specs=(P("series", TM), P("series", TM), P(None, TM), P(), P()),
        out_specs=(P("series", None), P(None, TM)),
        check_vma=False,
    )
```

```python
import functools

import jax
import jax.numpy as jnp
from jax import lax
from jax.experimental import pallas as pl
from jax.experimental.pallas import tpu as pltpu
from jax.sharding import Mesh, PartitionSpec as P

HIGH = lax.Precision.HIGHEST
TILE = 128
LAGS = 14
LONGEST = 2016
RIDGE_FACTOR = 1.0
RIDGE_TIME = 0.05
AR = 0.25
TM = ("tz", "ty")
F32 = jnp.float32
VMEM = pl.BlockSpec(memory_space=pltpu.VMEM)
HBM = pl.BlockSpec(memory_space=pltpu.HBM)


def struct(*shape):
    return jax.ShapeDtypeStruct(shape, F32)


def iota(shape, dim):
    return lax.broadcasted_iota(jnp.int32, shape, dim)


def call(kernel, outs, ins, scratch=(), place=VMEM, room=32):
    return pl.pallas_call(
        kernel,
        out_shape=outs,
        in_specs=[place] * len(ins),
        out_specs=jax.tree.map(lambda _: VMEM, outs),
        scratch_shapes=list(scratch),
        compiler_params=pltpu.CompilerParams(vmem_limit_bytes=room * 1024 * 1024),
    )(*ins)


def dot(a, b, dims):
    return lax.dot_general(a, b, (dims, ((), ())), precision=HIGH, preferred_element_type=F32)


def columns_of(obs_ref):
    flags = obs_ref[...].astype(F32)
    return jnp.concatenate([flags] * 32, axis=0).T


def front_kernel(panel_hbm, obs_hbm, x_hbm, out_ref, panel_ref, obs_ref, x_ref, sems):
    copies = [
        pltpu.make_async_copy(source, target, sems.at[i])
        for i, (source, target) in enumerate(((x_hbm, x_ref), (obs_hbm, obs_ref), (panel_hbm, panel_ref)))
    ]
    for copy in copies:
        copy.start()
    copies[0].wait()
    x = x_ref[...]
    row = iota((32, 64), 0)
    col = iota((32, 64), 1)
    keep = (col < 32) | (col - 32 >= row)
    diag_at = iota((64, 128), 0) == iota((64, 128), 1) % 64
    lane = iota((8, 128), 1)
    sub = iota((8, 128), 0)
    packs, masked = [], []
    extra = jnp.zeros((8, 128), F32)
    for b in range(4):
        xb = x[:, b * TILE : (b + 1) * TILE]
        gram = dot(xb, xb, ((1,), (1,)))
        moved = jnp.concatenate([gram[0:32, 32:64], gram[0:32, 0:32]], axis=1)
        packs.append(jnp.where(keep, gram[32:64], moved))
        twice = jnp.concatenate([gram, gram], axis=1)
        diag = jnp.sum(jnp.where(diag_at, twice, 0.0), axis=0, keepdims=True)
        extra = jnp.where((sub == b) & (lane % 64 < 32), diag, extra)
    copies[1].wait()
    flags = columns_of(obs_ref)
    copies[2].wait()
    for b in range(4):
        masked.append(panel_ref[:, b * TILE : (b + 1) * TILE] * flags[:, b : b + 1])
    rhs = dot(jnp.concatenate(masked, axis=1), x, ((1,), (1,)))
    mine = pl.ds(pl.multiple_of(8 * lax.axis_index("series"), 8), 8)
    own = [x_ref[mine, q * TILE : (q + 1) * TILE] for q in range(4)]
    pairs = [jnp.concatenate([packs[0], packs[1]], axis=1), jnp.concatenate([packs[2], packs[3]], axis=1)]
    for y in range(8):
        out_ref[y, 0:32, :] = pairs[0]
        out_ref[y, 32:64, :] = pairs[1]
        first, second = slice(16 * y, 16 * y + 8), slice(16 * y + 8, 16 * y + 16)
        out_ref[y, 64:72, :] = jnp.concatenate([rhs[first], rhs[second]], axis=1)
        tail = extra
        for b in range(4):
            tail = jnp.where(lane // 8 == 4 + b, flags[first, b : b + 1], tail)
            tail = jnp.where(lane // 8 == 12 + b, flags[second, b : b + 1], tail)
        out_ref[y, 72:80, :] = tail
        for q in range(4):
            out_ref[y, 80 + 8 * q : 88 + 8 * q, :] = own[q]


def middle_kernel(parts_ref, out_ref, x_ref):
    lane = iota((8, 128), 1)
    sub = iota((8, 128), 0)
    left = lane < 64
    wide_left = iota((32, 128), 1) < 64
    totals = [None] * 8
    diag = jnp.zeros((8, 128), F32)
    rhs = jnp.zeros((8, 128), F32)
    for y in range(8):
        extra = parts_ref[y, 72:80, :]
        rhs = rhs + parts_ref[y, 64:72, :]
        for pair in range(2):
            both = parts_ref[y, 32 * pair : 32 * pair + 32, :]
            other = pltpu.roll(both, 64, axis=1)
            packs = (jnp.where(wide_left, both, other), jnp.where(wide_left, other, both))
            for half in range(2):
                b = 2 * pair + half
                flag = jnp.where(left, extra[:, 32 + 8 * b : 33 + 8 * b], extra[:, 96 + 8 * b : 97 + 8 * b])
                diag = diag + flag * extra[b : b + 1]
                for z in range(8):
                    term = packs[half] * flag[z : z + 1]
                    totals[z] = term if totals[z] is None else totals[z] + term
        for q in range(4):
            x_ref[4 * y + q] = parts_ref[y, 80 + 8 * q : 88 + 8 * q, :]
    for z in range(8):
        out_ref[z, 0:32, :] = totals[z]
        out_ref[z, 32:40, :] = jnp.where(sub == 0, diag[z : z + 1], jnp.where(sub == 1, rhs[z : z + 1], 0.0))


def solve_kernel(parts_ref, out_ref):
    total = parts_ref[0]
    for j in range(1, 8):
        total = total + parts_ref[j]
    pack = total[0:32]
    diag = total[32:33]
    rhs = total[33:34]
    flipped = jnp.concatenate([pack, pack, pack, pack], axis=0).T
    row = iota((32, 128), 0)
    lane = iota((32, 128), 1)
    group = lane // 32
    col = lane % 32
    first = lane < 64
    upper_t = jnp.where(first, flipped[32:64], flipped[96:128])
    cross = jnp.where(first, flipped[0:32], flipped[64:96])
    odd = group % 2 == 1
    top_left = jnp.where(col < row, pltpu.roll(pack, 96, axis=1), jnp.where(col == row, diag, upper_t))
    top = jnp.where(odd, cross, top_left)
    bottom = jnp.where(odd & (col < row), upper_t, pack)
    eye = (iota((64, 128), 0) == iota((64, 128), 1) % 64).astype(F32)
    mat = jnp.concatenate([top, bottom], axis=0) + RIDGE_FACTOR * eye
    blocks = [mat[8 * i : 8 * i + 8] for i in range(8)]
    side = jnp.broadcast_to(rhs, (8, 128))
    half = iota((8, 128), 1) < 64
    within = iota((8, 128), 1) % 64

    def spread(value, k):
        return jnp.where(half, value[:, k : k + 1], value[:, 64 + k : 65 + k])

    for i in range(8):
        columns = [[spread(blocks[m], 8 * i + j) for j in range(8)] for m in range(i, 8)]
        ends = [spread(side, 8 * i + j) for j in range(8)]
        for r in range(8):
            inverse = 1.0 / jnp.broadcast_to(columns[0][r][r : r + 1], (8, 128))
            pivot_row = jnp.broadcast_to(blocks[i][r : r + 1], (8, 128))
            factor = jnp.where(within == 8 * i + r, 1.0 - inverse, pivot_row * inverse)
            factors = [jnp.broadcast_to(columns[0][j][r : r + 1], (8, 128)) * inverse for j in range(r + 1, 8)]
            for m in range(i if r < 7 else i + 1, 8):
                own = columns[m - i]
                blocks[m] = blocks[m] - own[r] * factor
                for j in range(r + 1, 8):
                    own[j] = own[j] - own[r] * factors[j - r - 1]
            side = side - ends[r] * factor
            for j in range(r + 1, 8):
                ends[j] = ends[j] - ends[r] * factors[j - r - 1]
    out_ref[...] = jnp.broadcast_to(side[0:1][None], out_ref.shape)


def normal_kernel(scale, gathered_ref, panel_ref, obs_ref, factors_ref, out_ref):
    pieces = []
    for y in range(8):
        pair = gathered_ref[8 * y : 8 * y + 8, :]
        pieces += [pair[:, 0:64], pair[:, 64:128]]
    factors = jnp.concatenate(pieces, axis=0)
    turned = factors.T
    factors_ref[...] = turned
    flags = columns_of(obs_ref)
    right = [panel_ref[:, b * TILE : (b + 1) * TILE] * flags[:, b : b + 1] for b in range(4)]
    for b in (0, 2):
        right.append(jnp.concatenate([factors * flags[:, b : b + 1], factors * flags[:, b + 1 : b + 2]], axis=1))
    right.append(factors)
    product = scale * dot(turned, jnp.concatenate(right, axis=1), ((1,), (0,)))
    out_ref[:, 0:768] = product[:, 0:768]
    gram = product[:, 768:832]
    norm = jnp.sum(gram * gram)
    trace = jnp.sum(jnp.where(iota((64, 64), 0) == iota((64, 64), 1), gram, 0.0))
    some = jnp.full((64, 128), trace)
    out_ref[:, 768:896] = jnp.where(some > 0.0, norm / jnp.where(some > 0.0, some, 1.0), 0.0)


def scalars(lags_ref):
    return [jnp.max(lags_ref[index : index + 1, :]) for index in range(LAGS)]


def lagged(read, chunks, lags, weight_ref, ahead):
    lane = iota((8, 128), 1)
    sums = {}
    for index in range(LAGS):
        lag = lags[index]
        if ahead:
            start = lag // 128
            shift = lag % 128
        else:
            back = (lag + 127) // 128
            start = -back
            shift = back * 128 - lag
        cut = 128 - shift
        weight = weight_ref[index]
        own = lane < cut
        turn = jnp.where(cut == 128, 0, cut)
        for first, last in chunks:
            low = pltpu.roll(read(start + first), turn, axis=1)
            for j in range(first, last):
                high = pltpu.roll(read(start + j + 1), turn, axis=1)
                term = weight * jnp.where(own, low, high)
                sums[j] = sums[j] + term if j in sums else term
                low = high
    return sums


def residuals(read, chunks, first_step, steps_all, lags, weight_ref):
    past = lagged(read, chunks, lags, weight_ref, False)
    lane = iota((8, 128), 1)
    out = {}
    for j, value in past.items():
        step = first_step + 128 * j + lane
        out[j] = jnp.where((step >= LONGEST) & (step < steps_all), read(j) - value, 0.0)
    return out


def ar_part(read, first_step, steps_all, lags, weight_ref, errors_ref):
    errors = residuals(read, ((0, 8), (15, 20)), first_step, steps_all, lags, weight_ref)
    for j, value in errors.items():
        errors_ref[j] = value
    later = lagged(lambda j: errors_ref[j], ((0, 4),), lags, weight_ref, True)
    return [errors[j] - later[j] for j in range(4)]


def place():
    y = lax.axis_index("ty")
    return lax.axis_index("tz") * 8 + y, y


def drift_kernel(
    steps_all, plane_ref, near_ref, weight_ref, all_ref, lags_ref, out_ref, theta_ref, context_ref, errors_ref
):
    lags = scalars(lags_ref)
    slab, y = place()
    read = fill_context(plane_ref, near_ref, context_ref, y)
    back = ar_part(read, slab * 512, steps_all, lags, weight_ref, errors_ref)
    for q in range(4):
        out_ref[q] = RIDGE_TIME * read(q) + AR * back[q]
    squares = all_ref[...] * all_ref[...]
    theta_ref[...] = jnp.full((8, 128), RIDGE_TIME + AR) + (AR / 64.0) * jnp.sum(squares)


def start_kernel(sums_ref, x_ref, drift_ref, theta_ref, out_ref, own_ref, h_ref, first_ref):
    total = sums_ref[0]
    for j in range(1, 8):
        total = total + sums_ref[j]
    first_ref[...] = theta_ref[...] + total[:, 768:896]
    for q in range(4):
        h = total[:, 512 + 64 * q : 576 + 64 * q]
        h_ref[q] = h
        image = dot(h, x_ref[:, q * 128 : (q + 1) * 128], ((1,), (0,))) + drift_ref[q]
        value = total[:, q * 128 : (q + 1) * 128] - image
        own_ref[q] = value
        for j in range(8):
            out_ref[j, q] = value


def fill_context(plane_ref, near_ref, context_ref, y):
    lower = y < 4
    at = jnp.where(lower, 16, 0)
    near_at = jnp.where(lower, 0, 32)
    near_from = jnp.where(lower, 16, 0)
    for j in range(32):
        context_ref[at + j] = plane_ref[j]
    for j in range(16):
        context_ref[near_at + j] = near_ref[near_from + j]
    base = at + 4 * y
    return lambda j: context_ref[base + j]


def data_part(h_ref, wide_ref, q):
    return dot(h_ref[q], wide_ref[:, q].reshape(64, 128), ((1,), (0,)))


def image_kernel(
    steps_all, plane_ref, near_ref, wide_ref, h_ref, weight_ref, theta_ref, lags_ref,
    out_ref, own_ref, context_ref, errors_ref,
):
    lags = scalars(lags_ref)
    slab, y = place()
    read = fill_context(plane_ref, near_ref, context_ref, y)
    back = ar_part(read, slab * 512, steps_all, lags, weight_ref, errors_ref)
    theta = theta_ref[...]
    for q in range(4):
        own = read(q)
        value = data_part(h_ref, wide_ref, q) + (RIDGE_TIME - theta) * own + AR * back[q]
        own_ref[q] = value
        for j in range(8):
            out_ref[j, q] = value


def two_sum(a, b):
    s = a + b
    t = s - a
    return s, (a - (s - t)) + (b - t)


def pair_add(a, b):
    s, e = two_sum(a[0], b[0])
    e = e + (a[1] + b[1])
    high = s + e
    return high, e - (high - s)


def split(a):
    c = a * 4097.0
    high = c - (c - a)
    return high, a - high


def pair_mul(a, b):
    p = a[0] * b[0]
    ah, al = split(a[0])
    bh, bl = split(b[0])
    e = ((ah * bh - p) + ah * bl + al * bh) + al * bl
    e = e + (a[0] * b[1] + a[1] * b[0])
    high = p + e
    return high, e - (high - p)


def pair_neg(a):
    return -a[0], -a[1]


def pair_sub(a, b):
    return pair_add(a, pair_neg(b))


def pair_div(a, b):
    first = a[0] / b[0]
    zero = jnp.zeros_like(first)
    rest = pair_sub(a, pair_mul(b, (first, zero)))
    second = rest[0] / b[0]
    return two_sum(first, second)


def pair_tree(values):
    while len(values) > 1:
        values = [
            pair_add(values[i], values[i + 1]) if i + 1 < len(values) else values[i]
            for i in range(0, len(values), 2)
        ]
    return values[0]


def lane_sum(pair):
    high, low = pair
    large = 6144.0 * jnp.max(jnp.abs(high), axis=1, keepdims=True)
    lead = (high + large) - large
    rest = (high - lead) + low
    total = [jnp.broadcast_to(jnp.sum(a, axis=1, keepdims=True), (8, 128)) for a in (lead, rest)]
    return two_sum(*total)


def fold_rows(value):
    large = 6144.0 * jnp.max(jnp.abs(value), axis=0, keepdims=True)
    lead = (value + large) - large
    return two_sum(*[
        jnp.broadcast_to(jnp.sum(a, axis=0, keepdims=True), (8, 128)) for a in (lead, value - lead)
    ])


def product_kernel(wide_ref, h_ref, u0_ref, u1_ref, u2_ref, near_ref, out_ref):
    sums = [jnp.zeros((8, 128), F32)] * 7
    for q in range(4):
        u0, u1, u2 = u0_ref[q], u1_ref[q], u2_ref[q]
        image = data_part(h_ref, wide_ref, q) + RIDGE_TIME * u2
        terms = [u0 * u0, u0 * u1, u0 * u2, u1 * u1, u1 * u2, u2 * u2, u2 * image]
        sums = [a + b for a, b in zip(sums, terms)]
    sub = iota((8, 128), 0)
    high = low = jnp.zeros((8, 128), F32)
    for i in range(7):
        pair = fold_rows(sums[i])
        high = jnp.where(sub == i, pair[0], high)
        low = jnp.where(sub == i, pair[1], low)
    high, low = pair_add((high, low), (pltpu.roll(high, 64, axis=1), pltpu.roll(low, 64, axis=1)))
    value = jnp.where(iota((8, 128), 1) < 64, high, low)
    for y in range(8):
        for q in range(4):
            out_ref[y, q] = u2_ref[q]
            out_ref[y, 4 + q] = near_ref[q]
        out_ref[y, 8] = value


def moment_kernel(steps_all, parts_ref, weight_ref, lags_ref, out_ref, stack_ref):
    starts = [512 - lag for lag in scalars(lags_ref)[: LAGS - 1]]
    lane = iota((128, 128), 1)
    none = jnp.zeros((64, 128), F32)

    def moved(runs, main, halo):
        return pltpu.roll(jnp.where(lane >= 128 - 8 * runs, halo, main), 8 * runs, axis=1)

    far = []
    for j in range(2):
        main = jnp.concatenate([parts_ref[s // 2, 2 * (s % 2) + j] for s in range(16)], axis=0).T
        halo = [parts_ref[4 + s // 2, 4 + 2 * (s % 2) + j] for s in range(8)]
        halo = jnp.concatenate([none] + halo, axis=0).T
        at = 128 * j
        stack_ref[512 + at : 640 + at, :] = main
        stack_ref[256 + at : 384 + at, :] = moved(1, main, halo)
        stack_ref[at : 128 + at, :] = moved(2, main, halo)
        far.append(moved(8, main, halo))
        if j == 0:
            end = moved(7, main, halo)[0:32]
    far = jnp.concatenate([far[0][32:128], far[1], end], axis=0)
    half = iota((8, 128), 1) < 64
    packed = pair_tree([
        (jnp.where(half, value, 0.0), jnp.where(half, pltpu.roll(value, 64, axis=1), 0.0))
        for value in (parts_ref[y, 8] for y in range(8))
    ])
    step = lax.axis_index("tz") * 4096 + iota((8, 128), 1) // 8 * 256 + iota((8, 128), 0)
    square = jnp.zeros((8, 128), F32)
    own = iota((8, 128), 0) == iota((8, 128), 1) % 8
    weights = [jnp.sum(jnp.where(own, weight_ref[index], 0.0), axis=0, keepdims=True) for index in range(LAGS)]
    for r in range(0, 256, 8):
        past = weights[LAGS - 1] * far[r : r + 8]
        for index in range(LAGS - 1):
            past = past + weights[index] * stack_ref[pl.ds(starts[index] + r, 8), :]
        valid = (step + r >= LONGEST) & (step + r < steps_all)
        error = jnp.where(valid, stack_ref[512 + r : 520 + r, :] - past, 0.0)
        square = square + error * error
    pair = fold_rows(AR * square)
    last = iota((8, 128), 0) == 6
    packed = pair_add(packed, (jnp.where(last, pair[0], 0.0), jnp.where(last, pair[1], 0.0)))
    packed = lane_sum(packed)
    lane = iota((8, 128), 1)
    value = jnp.where(lane < 64, packed[0], packed[1])
    value = jnp.sum(jnp.where(iota((8, 128), 0) == lane % 64 // 8, value, 0.0), axis=0, keepdims=True)
    out_ref[...] = jnp.broadcast_to(value[None], out_ref.shape)


def finish_kernel(parts_ref, first_ref, theta_ref, x_ref, wide0_ref, wide1_ref, wide2_ref, out_ref):
    parts = parts_ref[...]
    other = pltpu.roll(parts, 64, axis=1)
    half = iota((64, 128), 1) < 64
    high, low = jnp.where(half, parts, other), jnp.where(half, other, parts)
    large = 6144.0 * jnp.max(jnp.abs(high), axis=0, keepdims=True)
    lead = (high + large) - large
    rest = (high - lead) + low
    total = two_sum(*[jnp.broadcast_to(jnp.sum(a, axis=0, keepdims=True), (8, 128)) for a in (lead, rest)])

    def moment(i):
        return tuple(jnp.broadcast_to(a[:, 8 * i : 8 * i + 1], (8, 128)) for a in total)

    g00, g01, g02, g11, g12, g22, m22 = [moment(i) for i in range(7)]
    theta = (theta_ref[...], jnp.zeros((8, 128), F32))
    first = (first_ref[...], jnp.zeros((8, 128), F32))
    m00 = pair_add(g01, pair_mul(first, g00))
    m01 = pair_add(g11, pair_mul(first, g01))
    m02 = pair_add(g12, pair_mul(first, g02))
    m11 = pair_add(g12, pair_mul(theta, g11))
    m12 = pair_add(g22, pair_mul(theta, g12))
    l10 = pair_div(m01, m00)
    l20 = pair_div(m02, m00)
    d1 = pair_sub(m11, pair_mul(l10, m01))
    n12 = pair_sub(m12, pair_mul(l10, m02))
    y1 = pair_sub(g01, pair_mul(l10, g00))
    l21 = pair_div(n12, d1)
    d2 = pair_sub(pair_sub(m22, pair_mul(l20, m02)), pair_mul(l21, n12))
    y2 = pair_sub(pair_sub(g02, pair_mul(l20, g00)), pair_mul(l21, y1))
    tiny = 1e-12
    c2 = jnp.where(d2[0] > tiny * m22[0], y2[0] / d2[0], 0.0)
    zero = jnp.zeros_like(c2)
    c1 = pair_sub(pair_div(y1, d1), pair_mul(l21, (c2, zero)))
    c1 = jnp.where(d1[0] > tiny * m11[0], c1[0], 0.0)
    c0 = pair_div(g00, m00)
    c0 = pair_sub(c0, pair_mul(l10, (c1, zero)))
    c0 = pair_sub(c0, pair_mul(l20, (c2, zero)))[0]
    for s in range(8):
        for q in range(4):
            at = (slice(8 * s, 8 * s + 8), slice(128 * q, 128 * q + 128))
            step = c0 * wide0_ref[s, q] + c1 * wide1_ref[s, q] + c2 * wide2_ref[s, q]
            out_ref[at] = x_ref[at] + step


def neighbour(plane):
    pairs = [(8 * z + y, 8 * ((z + (1 if y < 4 else -1)) % 8) + y) for z in range(8) for y in range(8)]
    return lax.ppermute(plane, TM, pairs)


def exchange(spread):
    plane = lax.all_to_all(spread, "ty", 0, 0).reshape(32, 8, 128)
    return plane, neighbour(plane), lax.all_to_all(spread, "series", 0, 0)


def per_device(panel, observed, start_time, ar_weight, lags):
    cells = panel.shape[0]
    steps_all = 64 * 512
    cells_all = cells * 8
    series = lax.axis_index("series")
    own_weight = lax.dynamic_slice_in_dim(ar_weight, 8 * series, 8, 0)
    weight = jnp.broadcast_to(own_weight.T[:, :, None], (LAGS, 8, 128))
    observed = observed.T
    lags = jnp.broadcast_to(lags[:, None], (LAGS, 128))
    context = pltpu.VMEM((48, 8, 128), F32)
    stack = pltpu.VMEM((768, 128), F32)
    errors = pltpu.VMEM((20, 8, 128), F32)

    parts = call(
        front_kernel,
        struct(8, 112, 128),
        (panel, observed, start_time),
        (
            pltpu.VMEM(panel.shape, F32),
            pltpu.VMEM(observed.shape, jnp.int32),
            pltpu.VMEM(start_time.shape, F32),
            pltpu.SemaphoreType.DMA((3,)),
        ),
        HBM,
        60,
    )
    parts = lax.all_to_all(parts, "ty", 0, 0)
    parts, plane = call(middle_kernel, (struct(8, 40, 128), struct(32, 8, 128)), (parts,))
    parts = lax.all_to_all(parts, "tz", 0, 0)
    solved = call(solve_kernel, struct(64, 1, 128), (parts,))
    solved, plane = lax.optimization_barrier((solved, plane))
    near = neighbour(plane)
    gathered = lax.all_to_all(solved, ("ty", "tz"), 0, 0).reshape(64, 128)
    gathered, near = lax.optimization_barrier((gathered, near))
    factors, normal = call(
        functools.partial(normal_kernel, 1.0 / cells_all),
        (struct(64, cells), struct(64, 896)),
        (gathered, panel, observed),
    )
    sums = lax.all_to_all(normal.reshape(8, 8, 896), "series", 0, 0)
    drift, theta = call(
        functools.partial(drift_kernel, steps_all),
        (struct(4, 8, 128), struct(8, 128)),
        (plane, near, weight, ar_weight, lags),
        (context, errors),
    )
    u0, own0, h, first = call(
        start_kernel,
        (struct(8, 4, 8, 128), struct(4, 8, 128), struct(4, 8, 64), struct(8, 128)),
        (sums, start_time, drift, theta),
    )

    def image(plane, near, wide, shift):
        return call(
            functools.partial(image_kernel, steps_all),
            (struct(8, 4, 8, 128), struct(4, 8, 128)),
            (plane, near, wide, h, weight, shift, lags),
            (context, errors),
        )

    plane, near, wide0 = exchange(u0)
    u1, own1 = image(plane, near, wide0, first)
    plane, near, wide1 = exchange(u1)
    u2, own2 = image(plane, near, wide1, theta)
    near = lax.ppermute(own2, "tz", [(z, (z + 1) % 8) for z in range(8)])
    wide2 = lax.all_to_all(u2, "series", 0, 0)
    parts = call(product_kernel, struct(8, 9, 8, 128), (wide2, h, own0, own1, own2, near))
    parts = lax.all_to_all(parts, "ty", 0, 0)
    moments = call(
        functools.partial(moment_kernel, steps_all), struct(64, 1, 128), (parts, weight, lags), (stack,)
    )
    moments = lax.all_to_all(moments, ("series", "tz"), 0, 0).reshape(64, 128)
    result = call(finish_kernel, struct(64, 512), (moments, first, theta, start_time, wide0, wide1, wide2))
    return (factors.T, result)


def solution(mesh):
    grid = Mesh(mesh.devices.reshape(8, 8, 8), ("series", "tz", "ty"))
    return jax.shard_map(
        per_device,
        mesh=grid,
        in_specs=(P("series", TM), P("series", TM), P(None, TM), P(), P()),
        out_specs=(P("series", None), P(None, TM)),
        check_vma=False,
    )
```
